32 devices in a mesh: rep: 4 (over x, core), fsdp: 2 (over y), tensor: 4 (over z).
Axes of the slice: x: 2, y: 2, z: 4, core: 2. Of those that a mesh axis runs over, the one named last changes fastest.
Arguments:
- block_input: bfloat16 [5120, 2048], P(('rep', 'fsdp', 'tensor')), may hold values from -6 to 6
- cotangent: bfloat16 [5120, 2048], P(('rep', 'fsdp', 'tensor')), may hold values from -6 to 6
- piece_starts: int32 [8, 2], P(('rep', 'fsdp')), may hold values from 0 to 384, as said below
- expert_ids: int32 [5120, 4], P(('rep', 'fsdp')), may hold values from 0 to 7, all different within a row; in each aligned block of 640 rows (0 to 639, 640 to 1279, ...) at most 400 rows name the same one
- norm_gains: bfloat16 [2, 2048], P(None, 'fsdp'), may hold values from 0.5 to 1.5
- qkv_weight: bfloat16 [3, 2048, 2048], P(None, 'fsdp', 'tensor'), may hold values from -0.125 to 0.125
- qkv_bias: bfloat16 [3, 16, 128], P(None, 'tensor', 'fsdp'), may hold values from -3 to 3
- out_weight: bfloat16 [2048, 2048], P('tensor', 'fsdp'), may hold values from -0.5 to 0.5
- router_weight: bfloat16 [2048, 8], P('fsdp'), may hold values from -0.0625 to 0.0625
- shared_gate: bfloat16 [2048], P('fsdp'), may hold values from -0.125 to 0.125
- expert_gate_up: bfloat16 [8, 2048, 2, 1408], P(None, 'fsdp', None, 'tensor'), may hold values from -0.125 to 0.125
- expert_down: bfloat16 [8, 1408, 2048], P(None, 'tensor', 'fsdp'), may hold values from -0.625 to 0.625
- shared_gate_up: bfloat16 [2048, 2, 5632], P('fsdp', None, 'tensor'), may hold values from -0.125 to 0.125
- shared_down: bfloat16 [5632, 2048], P('tensor', 'fsdp'), may hold values from -0.15625 to 0.15625
Outputs:
- output: bfloat16 [5120, 2048], P(('rep', 'fsdp', 'tensor'))
- input_grad: float32 [5120, 2048], P(('rep', 'fsdp', 'tensor'))
- norm_gains_grad: float32 [2, 2048], P(None, 'fsdp')
- qkv_weight_grad: float32 [3, 2048, 2048], P(None, 'fsdp', 'tensor')
- qkv_bias_grad: float32 [3, 16, 128], P(None, 'tensor', 'fsdp')
- out_weight_grad: float32 [2048, 2048], P('tensor', 'fsdp')
- router_weight_grad: float32 [2048, 8], P('fsdp')
- shared_gate_grad: float32 [2048], P('fsdp')
- expert_gate_up_grad: float32 [8, 2048, 2, 1408], P(None, 'fsdp', None, 'tensor')
- expert_down_grad: float32 [8, 1408, 2048], P(None, 'tensor', 'fsdp')
- shared_gate_up_grad: float32 [2048, 2, 5632], P('fsdp', None, 'tensor')
- shared_down_grad: float32 [5632, 2048], P('tensor', 'fsdp')
The draws below stay inside these ranges and needn't reach their ends.
Inputs may be any that keep to these rules, and one draw needn't show every extreme that they name: `expert_ids`: in each sequence's rows (aligned blocks of 640 rows) no expert is named by more than 400 rows, a bound that some block reaches. `piece_starts`: each row holds 2 rising starts, each at least 256 after the one before.
All inputs are finite; a program needn't handle non-finite values.
Results may differ from the reference program's by a relative error of at most 0.025.
Values may be sent and summed in bfloat16 or wider, within the bound.
A program may use at most 384 MiB of HBM per device.

```python
import math
import jax
import jax.numpy as jnp
import numpy as np
from jax import lax

D = 2048
HEADS = 16
HEAD_DIM = 128
FFE = 1408
FS = 5632
TOP = 4
EXPERTS = 8
LENGTH = 640
PIECE = 256
CAP = 400
SEQS = 8
TOKENS = 5120


def draw_piece_starts(key, part):
    key = jax.random.fold_in(key, 7)
    key_first, key_extra, key_pick = jax.random.split(key, 3)
    first_start = jax.random.randint(key_first, (SEQS,), 0, LENGTH - 2 * PIECE + 1)
    spare_room = LENGTH - 2 * PIECE - first_start
    extra_gap = jax.random.randint(key_extra, (SEQS,), 0, spare_room + 1)
    second_start = first_start + PIECE + extra_gap
    chosen = jax.random.randint(key_pick, (), 0, SEQS)
    spanning = jnp.arange(SEQS, dtype=jnp.int32) == chosen
    first_start = jnp.where(spanning, 0, first_start)
    second_start = jnp.where(spanning, LENGTH - PIECE, second_start)
    return jnp.stack([first_start, second_start], axis=1).astype(jnp.int32)


def block_levels(stream_key, dims, pieces, smallest, high):
    def one(axis_at, parts):
        steps = jax.random.uniform(jax.random.fold_in(jax.random.fold_in(stream_key, 6), axis_at), (parts,), jnp.float32, smallest / len(pieces), high / len(pieces))
        return jnp.repeat(jnp.exp(steps), dims[axis_at] // parts).reshape((-1,) + (1,) * (len(dims) - axis_at - 1))

    factor_of = one(*pieces[0])
    for cut in pieces[1:]:
        factor_of = factor_of * one(*cut)
    return factor_of


def routed_block(key, own, number, rows, count, top, limit, lean):
    ranking = jax.random.permutation(key, count)
    heavy_load, usual = portions_of(count, rows * top, limit, lean, True), portions_of(count, rows * top, limit, lean, False)
    places = jnp.arange(count)

    def named(lengths, rotation):
        used = int((lengths > 0).sum())
        fixed = max(1, used // 4)
        passed = fixed + (places - fixed + rotation * (used - fixed)) % max(1, count - fixed)
        return jnp.zeros((count,), jnp.int32).at[ranking[jnp.where(places < fixed, places, passed)]].set(jnp.asarray(lengths, jnp.int32))

    lengths = jnp.where(number % 4 == 0, named(heavy_load, number // 4), named(usual, number - number // 4 - 1))
    mixed = jax.random.permutation(jax.random.fold_in(own, 3), count)
    giver, sink = mixed[0:count // 2 * 2:2], mixed[1:count // 2 * 2:2]
    room = jnp.minimum(lengths[giver] - 1, limit - lengths[sink]) // 2
    room = jnp.where((giver == ranking[0]) | (sink == ranking[0]) | (lengths[sink] == 0), 0, jnp.maximum(room, 0))
    passed = jax.random.randint(jax.random.fold_in(own, 4), (count // 2,), 0, 1 << 20) % (room + 1)
    lengths = lengths.at[giver].add(-passed).at[sink].add(passed)
    members = jnp.searchsorted(jnp.cumsum(lengths), jnp.arange(rows * top), side="right").astype(jnp.int32)
    listing = members.reshape(top, rows).T
    listing = listing[jax.random.permutation(jax.random.fold_in(own, 1), rows)]
    rotation = jax.random.randint(jax.random.fold_in(own, 2), (rows, 1), 0, top)
    return jnp.take_along_axis(listing, (jnp.arange(top)[None, :] + rotation) % top, axis=1)


def portions_of(count, total, limit, skew, full):
    portions = [(1 << 20) // math.isqrt(standing ** skew) + 1 for standing in range(1, count + 1)]
    largest = limit if full else min(limit, max(-(-total // count), total * portions[0] // sum(portions)))
    least = 1 if total - largest >= count - 1 else 0
    holding, surplus = [largest] + [least] * (count - 1), total - largest - least * (count - 1)
    while surplus > 0:
        free = [i for i in range(1, count) if holding[i] < largest] or [i for i in range(1, count) if holding[i] < limit]
        pool, remaining = sum([portions[i] for i in free]), surplus
        for i in free:
            extra = min(limit - holding[i], max(1, remaining * portions[i] // pool), surplus)
            holding[i] = holding[i] + extra
            surplus = surplus - extra
    return np.array(holding)


def centred(own_key, shape, width, bound, cuts=(), held_as=jnp.bfloat16):
    array = jax.random.normal(own_key, shape, jnp.float32) * width
    if len(cuts) > 0:
        array = block_levels(own_key, shape, cuts, -0.22, 0.18) * array
    return jnp.clip(array, min=-bound, max=bound).astype(held_as)


def setup_inputs(seed: int = 0) -> dict:
    key_of = jax.random.split(jax.random.key(seed), 15)
    block_input = centred(key_of[0], (TOKENS, D), 1.0, 6.0, ((0, 32),))
    cotangent = centred(key_of[1], (TOKENS, D), 1.0, 6.0, ((0, 32),))
    piece_starts = draw_piece_starts(jax.random.fold_in(key_of[14], 71), 0)
    expert_ids_keys = jax.random.split(jax.random.fold_in(key_of[3], 1), TOKENS // LENGTH)
    expert_ids_turns = jax.random.permutation(jax.random.fold_in(key_of[3], 3), TOKENS // LENGTH)
    expert_ids = jax.vmap(lambda own, number: routed_block(jax.random.fold_in(key_of[3], 2), own, number, LENGTH, EXPERTS, TOP, CAP, 1))(expert_ids_keys, expert_ids_turns).reshape((TOKENS, TOP))
    norm_gains = jnp.clip(1.0 + 0.1 * jax.random.normal(key_of[4], (2, D), jnp.float32), 0.5, 1.5).astype(jnp.bfloat16)
    qkv_weight = centred(key_of[5], (3, D, D), D ** -0.5, 0.125, ((1, 2), (2, 4)))
    qkv_bias = centred(key_of[6], (3, HEADS, HEAD_DIM), 0.5, 3.0, ((1, 4), (2, 2)))
    out_weight = centred(key_of[7], (D, D), (D // 16) ** -0.5, 0.5, ((0, 4), (1, 2)))
    router_weight = centred(key_of[8], (D, EXPERTS), (4 * D) ** -0.5, 0.0625, ((0, 2),))
    shared_gate = centred(key_of[9], (D,), D ** -0.5, 0.125, ((0, 2),))
    expert_gate_up = centred(key_of[10], (EXPERTS, D, 2, FFE), D ** -0.5, 0.125, ((1, 2), (3, 4)))
    expert_down = centred(key_of[11], (EXPERTS, FFE, D), (FFE // 16) ** -0.5, 0.625, ((1, 4), (2, 2)))
    shared_gate_up = centred(key_of[12], (D, 2, FS), D ** -0.5, 0.125, ((0, 2), (2, 4)))
    shared_down = centred(key_of[13], (FS, D), (FS // 4) ** -0.5, 0.15625, ((0, 4), (1, 2)))
    return {"block_input": block_input, "cotangent": cotangent, "piece_starts": piece_starts, "expert_ids": expert_ids, "norm_gains": norm_gains, "qkv_weight": qkv_weight, "qkv_bias": qkv_bias, "out_weight": out_weight, "router_weight": router_weight, "shared_gate": shared_gate, "expert_gate_up": expert_gate_up, "expert_down": expert_down, "shared_gate_up": shared_gate_up, "shared_down": shared_down}


@jax.custom_vjp
def low(v):
    return lax.optimization_barrier(v.astype(jnp.bfloat16)).astype(jnp.float32)

@jax.custom_vjp
def low_back(v):
    return v

def low_keep(v):
    return (low(v), None)

def low_pass(kept, grad):
    return (grad,)

def back_keep(v):
    return (v, None)

def back_low(kept, grad):
    return (low(grad),)
low.defvjp(low_keep, low_pass)
low_back.defvjp(back_keep, back_low)
HIGHEST = lax.Precision.HIGHEST

def rms_scale(values, gain_row):
    return values * lax.rsqrt(lax.optimization_barrier(jnp.mean(values * values, axis=-1, keepdims=True)) + 1e-06) * gain_row

def rope_angles(length, head_dim):
    half_dim = head_dim // 2
    frequency = 1000000.0 ** (-jnp.arange(half_dim, dtype=jnp.float32) * (2.0 / head_dim))
    angles = jnp.arange(length, dtype=jnp.float32)[:, None] * frequency[None, :]
    return (jnp.cos(angles), jnp.sin(angles))

def rotate(head_rows, cos_table, sin_table):
    half_dim = head_rows.shape[-1] // 2
    leading = head_rows[..., :half_dim]
    trailing = head_rows[..., half_dim:]
    cos_rows = cos_table[:, None, :]
    sin_rows = sin_table[:, None, :]
    return jnp.concatenate([leading * cos_rows - trailing * sin_rows, trailing * cos_rows + leading * sin_rows], axis=-1)

def visible_mask(starts_row, length, piece_len):
    position = jnp.arange(length, dtype=jnp.int32)
    inside = (position[None, :] >= starts_row[:, None]) & (position[None, :] < starts_row[:, None] + piece_len)
    label_ids = jnp.arange(1, starts_row.shape[0] + 1, dtype=jnp.int32)[:, None]
    labels = lax.optimization_barrier(jnp.sum(jnp.where(inside, label_ids, 0), axis=0))
    causal = position[None, :] <= position[:, None]
    same_piece = (labels[:, None] == labels[None, :]) & (labels[:, None] > 0)
    return causal | same_piece

def slot_entries(routes, experts, capacity):
    flat_ids = routes.reshape(-1)
    onehot = (flat_ids[:, None] == jnp.arange(experts, dtype=jnp.int32)[None, :]).astype(jnp.int32)
    before = jnp.cumsum(onehot, axis=0) - onehot
    place_in = lax.optimization_barrier(jnp.sum(before * onehot, axis=1))
    target = flat_ids * capacity + place_in
    entries = jnp.full((experts * capacity,), -1, jnp.int32)
    entries = entries.at[target].set(jnp.arange(flat_ids.shape[0], dtype=jnp.int32))
    return (target.reshape(routes.shape), entries)

def layer(params, block_rows, starts_row, routes):
    norm_gains, qkv_weight, qkv_bias, out_weight, router_weight, shared_gate, expert_gate_up, expert_down, shared_gate_up, shared_down = params
    length = block_rows.shape[0]
    cos_table, sin_table = rope_angles(length, HEAD_DIM)
    normed = low(rms_scale(block_rows, norm_gains[0]))
    project = jnp.einsum('ld,cde->cle', normed, qkv_weight, precision=HIGHEST) + qkv_bias.reshape(3, 1, D)
    project = low_back(project)
    queries = low(rotate(project[0].reshape(length, HEADS, HEAD_DIM), cos_table, sin_table))
    key_rows = low(rotate(project[1].reshape(length, HEADS, HEAD_DIM), cos_table, sin_table))
    value_rows = low(project[2].reshape(length, HEADS, HEAD_DIM))
    scores = low_back(jnp.einsum('qhd,khd->hqk', queries, key_rows, precision=HIGHEST) * HEAD_DIM ** (-0.5))
    visible = visible_mask(starts_row, length, PIECE)
    scores = jnp.where(visible[None], scores, -1e+30)
    probs = jax.nn.softmax(scores, axis=-1)
    attended = jnp.einsum('hqk,khd->qhd', low(probs), value_rows, precision=HIGHEST).reshape(length, D)
    attended = low(low_back(attended))
    branch = low_back(jnp.dot(attended, out_weight, precision=HIGHEST))
    hidden = block_rows + branch
    normed_two = low(rms_scale(hidden, norm_gains[1]))
    logits = jnp.dot(normed_two, router_weight, precision=HIGHEST)
    router_probs = jax.nn.softmax(logits, axis=-1)
    gate_sel = jnp.take_along_axis(router_probs, routes, axis=1)
    target, entries = slot_entries(routes, EXPERTS, CAP)
    live = entries >= 0
    token_of = jnp.maximum(entries, 0) // TOP
    slot_rows = jnp.where(live[:, None], normed_two[token_of], 0.0).reshape(EXPERTS, CAP, D)
    expert_pre = jnp.einsum('ecd,edf->ecf', slot_rows, expert_gate_up.reshape(EXPERTS, D, 2 * FFE), precision=HIGHEST)
    expert_pre = low_back(expert_pre)
    expert_act = low(jax.nn.silu(expert_pre[..., :FFE]) * expert_pre[..., FFE:])
    expert_out = low_back(jnp.einsum('ecf,efd->ecd', expert_act, expert_down, precision=HIGHEST))
    expert_out = expert_out.reshape(EXPERTS * CAP, D)
    routed = lax.optimization_barrier(jnp.sum(gate_sel[:, :, None] * expert_out[target], axis=1))
    shared_pre = low_back(jnp.dot(normed_two, shared_gate_up.reshape(D, 2 * FS), precision=HIGHEST))
    shared_act = low(jax.nn.silu(shared_pre[:, :FS]) * shared_pre[:, FS:])
    shared_out = low_back(jnp.dot(shared_act, shared_down, precision=HIGHEST))
    shared_scale = jax.nn.sigmoid(jnp.dot(normed_two, shared_gate, precision=HIGHEST))
    return hidden + routed + shared_scale[:, None] * shared_out

def reference(block_input, cotangent, piece_starts, expert_ids, norm_gains, qkv_weight, qkv_bias, out_weight, router_weight, shared_gate, expert_gate_up, expert_down, shared_gate_up, shared_down):
    params = tuple((weight_arg.astype(jnp.float32) for weight_arg in (norm_gains, qkv_weight, qkv_bias, out_weight, router_weight, shared_gate, expert_gate_up, expert_down, shared_gate_up, shared_down)))
    seq_count = piece_starts.shape[0]
    rows_in = block_input.astype(jnp.float32).reshape(seq_count, LENGTH, D)
    routes = expert_ids.reshape(seq_count, LENGTH, TOP)

    def forward(weights, inputs):

        def one_sequence(seq_item):
            return layer(weights, seq_item[0], seq_item[1], seq_item[2])
        return lax.map(jax.checkpoint(one_sequence), (inputs, piece_starts, routes))
    result, pullback = jax.vjp(forward, params, rows_in)
    weight_grads, input_grad = pullback(cotangent.astype(jnp.float32).reshape(seq_count, LENGTH, D))
    return (result.reshape(-1, D).astype(jnp.bfloat16), input_grad.reshape(-1, D), weight_grads[0], weight_grads[1], weight_grads[2], weight_grads[3], weight_grads[4], weight_grads[5], weight_grads[6], weight_grads[7], weight_grads[8], weight_grads[9])
```

```python
import functools

import jax
import jax.numpy as jnp
from jax import lax
from jax.experimental import pallas as pl
from jax.experimental.pallas import tpu as pltpu
from jax.sharding import PartitionSpec as P

HEAD_DIM = 128
EXPERTS = 8
LENGTH = 640
PIECE = 256
EPSILON = 1e-06
BF16 = jnp.bfloat16
F32 = jnp.float32
COLS = 256


def rope_tables(length, head_dim):
    half_dim = head_dim // 2
    frequency = 1000000.0 ** (-jnp.arange(half_dim, dtype=F32) * (2.0 / head_dim))
    angles = jnp.arange(length, dtype=F32)[:, None] * frequency[None, :]
    return (jnp.cos(angles), jnp.sin(angles))


def rotate(head_rows, cos_table, sin_table):
    half_dim = head_rows.shape[-1] // 2
    leading = head_rows[..., :half_dim]
    trailing = head_rows[..., half_dim:]
    cos_rows = cos_table[:, None, :]
    sin_rows = sin_table[:, None, :]
    return jnp.concatenate(
        [leading * cos_rows - trailing * sin_rows, trailing * cos_rows + leading * sin_rows],
        axis=-1,
    )


def visible_mask(starts_row, length, piece_len):
    position = jnp.arange(length, dtype=jnp.int32)
    inside = (position[None, :] >= starts_row[:, None]) & (
        position[None, :] < starts_row[:, None] + piece_len
    )
    label_ids = jnp.arange(1, starts_row.shape[0] + 1, dtype=jnp.int32)[:, None]
    labels = jnp.sum(jnp.where(inside, label_ids, 0), axis=0)
    causal = position[None, :] <= position[:, None]
    same_piece = (labels[:, None] == labels[None, :]) & (labels[:, None] > 0)
    return causal | same_piece


def after(value, *others):
    return lax.optimization_barrier((value,) + others)[0]


def swap_y(a):
    return lax.ppermute(a, "fsdp", [(0, 1), (1, 0)])


def swap_x(a):
    n = lax.axis_size("rep")
    return lax.ppermute(a, "rep", [(i, i ^ 2) for i in range(n)])


def swap_core(a):
    n = lax.axis_size("rep")
    return lax.ppermute(a, "rep", [(i, i ^ 1) for i in range(n)])


def gather_rows(block):
    n = lax.axis_size("tensor")
    z = lax.axis_index("tensor")
    rows = block.shape[0]
    right, left = [block], [block]
    for _ in range(n - 1):
        right.append(lax.ppermute(right[-1], "tensor", [(i, i + 1) for i in range(n - 1)]))
        left.append(lax.ppermute(left[-1], "tensor", [(i, i - 1) for i in range(1, n)]))
    out = jnp.zeros((n * rows,) + block.shape[1:], block.dtype)
    out = lax.dynamic_update_slice_in_dim(out, block, z * rows, 0)
    for k in range(1, n):
        piece = jnp.where(z >= k, right[k], left[n - k])
        out = lax.dynamic_update_slice_in_dim(out, piece, lax.rem(z - k + n, n) * rows, 0)
    return out


def scatter_rows(total):
    n = lax.axis_size("tensor")
    z = lax.axis_index("tensor")
    rows = total.shape[0] // n

    def block(b):
        return lax.dynamic_slice_in_dim(total, jnp.clip(b, 0, n - 1) * rows, rows, 0).astype(F32)

    right = left = None
    for s in range(n - 1):
        to_right, to_left = block(n - 1 - s + z), block(s - (n - 1) + z)
        if s > 0:
            to_right = to_right + right.astype(F32)
            to_left = to_left + left.astype(F32)
        right = lax.ppermute(
            to_right.astype(BF16), "tensor", [(i, i + 1) for i in range(n - 1) if i <= s]
        )
        left = lax.ppermute(
            to_left.astype(BF16), "tensor", [(i, i - 1) for i in range(1, n) if n - 1 - i <= s]
        )
    return block(z) + right.astype(F32) + left.astype(F32)


def others_of(own, f, axis):
    if lax.axis_size("fsdp") == 2:
        return swap_y(own)
    whole = lax.all_gather(own, "fsdp", axis=axis, tiled=True)
    size = own.shape[axis]
    turned = jnp.roll(whole, -f * size, axis=axis)
    return lax.slice_in_dim(turned, size, whole.shape[axis], axis=axis)


def reduce_fsdp(own, other, f, axis):
    if lax.axis_size("fsdp") == 2:
        return own.astype(F32) + swap_y(other).astype(F32)
    whole = jnp.roll(jnp.concatenate([own, other], axis=axis), f * own.shape[axis], axis=axis)
    return lax.psum_scatter(whole, "fsdp", scatter_dimension=axis, tiled=True).astype(F32)


def sum_small(own, other, f):
    if lax.axis_size("fsdp") == 2:
        total = own + swap_y(other)
    else:
        whole = jnp.roll(jnp.concatenate([own, other], axis=1), f * own.shape[1], axis=1)
        total = lax.psum_scatter(whole, "fsdp", scatter_dimension=1, tiled=True)
    return sum_tensor(sum_rep(total))


def sum_rep(total):
    total = total + swap_core(total)
    return total + swap_x(total)


def sum_tensor(total):
    n = lax.axis_size("tensor")
    step = 1
    while step < n:
        total = total + lax.ppermute(total, "tensor", [(i, i ^ step) for i in range(n)])
        step *= 2
    return total


def dot_nt(a, b):
    return lax.dot_general(a, b, (((1,), (1,)), ((), ())), preferred_element_type=F32)


def dot_nn(a, b):
    return lax.dot_general(a, b, (((1,), (0,)), ((), ())), preferred_element_type=F32)


def experts_kernel(
    rows, width, own_width, hidden,
    x0, x1, c0, c1, gate, w_own, w_oth,
    dw_own, dw_oth, mix0, mix1, ng0, ng1, gate_grad,
    xv, cv, wg, wu, wd, ga, pg, pu, st_mix, st_ng, st_dw, in_sem, mix_sem, ng_sem, dw_sem,
):
    seq = rows // 2
    loads = []

    def load(src, dst):
        copy = pltpu.make_async_copy(src, dst, in_sem.at[len(loads)])
        copy.start()
        loads.append(copy)

    for part, w in ((0, wg), (1, wu), (2, wd)):
        for k in range(2):
            r = pl.ds(k * hidden, hidden)
            load(w_own.at[k, part], w.at[r, pl.ds(0, own_width)])
            load(w_oth.at[k, part], w.at[r, pl.ds(own_width, width - own_width)])
        if part == 0:
            load(x0, xv.at[pl.ds(0, seq)])
            load(x1, xv.at[pl.ds(seq, seq)])
        if part == 1:
            load(c0, cv.at[pl.ds(0, seq)])
            load(c1, cv.at[pl.ds(seq, seq)])
    for copy in loads:
        copy.wait()

    tiles = rows // COLS

    def out_copies(t, slot):
        copies = []
        for stage, outs, sem in ((st_mix, (mix0, mix1), mix_sem), (st_ng, (ng0, ng1), ng_sem)):
            for part in range(2):
                copies.append((stage.at[slot, pl.ds(part * 128, 128)], outs, sem.at[slot, part], part))
        return copies

    def start_out(t, slot):
        for src, outs, sem, part in out_copies(t, slot):
            first = t * COLS + part * 128

            @pl.when(first < seq)
            def _():
                pltpu.make_async_copy(src, outs[0].at[pl.ds(pl.multiple_of(first, 128), 128)], sem).start()

            @pl.when(first >= seq)
            def _():
                pltpu.make_async_copy(
                    src, outs[1].at[pl.ds(pl.multiple_of(first - seq, 128), 128)], sem
                ).start()

    def wait_out(slot):
        for src, outs, sem, part in out_copies(0, slot):
            pltpu.make_async_copy(src, outs[0].at[pl.ds(0, 128)], sem).wait()

    def token_tile(t, carry):
        slot = lax.rem(t, 2)
        here = pl.ds(pl.multiple_of(t * COLS, COLS), COLS)
        g = dot_nt(wg[...], xv[here, :])
        u = dot_nt(wu[...], xv[here, :])
        h = dot_nt(wd[...], cv[here, :])
        sig = jax.nn.sigmoid(g)
        act = g * sig * u
        product = act * h
        scale_rows = []
        for k in range(2):
            part = product[k * hidden : (k + 1) * hidden]
            gate_grad[pl.ds(k, 1), here] = jnp.sum(part, axis=0, keepdims=True)
            scale_rows.append(jnp.broadcast_to(gate[pl.ds(k, 1), here], (hidden, COLS)))
        scale = jnp.concatenate(scale_rows, axis=0)
        back = scale * h
        ga_t = (scale * act).astype(BF16)
        pg_t = (back * u * sig * (1.0 + g * (1.0 - sig))).astype(BF16)
        pu_t = (back * g * sig).astype(BF16)
        ga[:, here] = ga_t
        pg[:, here] = pg_t
        pu[:, here] = pu_t

        @pl.when(t >= 2)
        def _():
            wait_out(slot)

        st_mix[slot] = dot_nn(ga_t.T, wd[...]).astype(BF16)
        st_ng[slot] = (dot_nn(pg_t.T, wg[...]) + dot_nn(pu_t.T, wu[...])).astype(BF16)
        start_out(t, slot)
        return carry

    lax.fori_loop(0, tiles, token_tile, 0)

    def wait_dw(slot):
        for part in range(3):
            for k in range(2):
                pltpu.make_async_copy(
                    st_dw.at[slot, part, pl.ds(k * hidden, hidden)],
                    dw_own.at[k, part, :, pl.ds(0, COLS)],
                    dw_sem.at[slot, part, k],
                ).wait()

    def weight_tile(n, slot, src_col, dst, dst_col, first):
        cols = pl.ds(pl.multiple_of(src_col, COLS), COLS)

        @pl.when(jnp.logical_not(first))
        def _():
            wait_dw(slot)

        xs = xv[:, cols]
        st_dw[slot, 0] = dot_nn(pg[...], xs).astype(BF16)
        st_dw[slot, 1] = dot_nn(pu[...], xs).astype(BF16)
        st_dw[slot, 2] = dot_nn(ga[...], cv[:, cols]).astype(BF16)
        for part in range(3):
            for k in range(2):
                pltpu.make_async_copy(
                    st_dw.at[slot, part, pl.ds(k * hidden, hidden)],
                    dst.at[k, part, :, pl.ds(pl.multiple_of(dst_col, COLS), COLS)],
                    dw_sem.at[slot, part, k],
                ).start()

    oth_tiles = (width - own_width) // COLS
    own_tiles = own_width // COLS

    def oth_tile(n, carry):
        weight_tile(n, lax.rem(n, 2), own_width + n * COLS, dw_oth, n * COLS, n < 2)
        return carry

    def own_tile(n, carry):
        weight_tile(n, lax.rem(n + oth_tiles, 2), n * COLS, dw_own, n * COLS, n + oth_tiles < 2)
        return carry

    lax.fori_loop(0, oth_tiles, oth_tile, 0)
    lax.fori_loop(0, own_tiles, own_tile, 0)
    for slot in range(2):
        wait_out(slot)
        wait_dw(slot)


def experts_call(x0, x1, c0, c1, gate, w_own, w_oth):
    seq, width = x0.shape
    rows = 2 * seq
    hidden, own_width = w_own.shape[2], w_own.shape[3]
    any_spec = pl.BlockSpec(memory_space=pl.ANY)
    vmem_spec = pl.BlockSpec(memory_space=pltpu.VMEM)
    out_rows = jax.ShapeDtypeStruct((seq, width), BF16)
    macs = 9 * rows * width * 2 * hidden
    return pl.pallas_call(
        functools.partial(experts_kernel, rows, width, own_width, hidden),
        out_shape=[
            jax.ShapeDtypeStruct(w_own.shape, BF16),
            jax.ShapeDtypeStruct(w_oth.shape, BF16),
            out_rows, out_rows, out_rows, out_rows,
            jax.ShapeDtypeStruct((8, rows), F32),
        ],
        in_specs=[any_spec] * 4 + [vmem_spec] + [any_spec] * 2,
        out_specs=[any_spec] * 6 + [vmem_spec],
        scratch_shapes=[
            pltpu.VMEM((rows, width), BF16),
            pltpu.VMEM((rows, width), BF16),
            pltpu.VMEM((2 * hidden, width), BF16),
            pltpu.VMEM((2 * hidden, width), BF16),
            pltpu.VMEM((2 * hidden, width), BF16),
            pltpu.VMEM((2 * hidden, rows), BF16),
            pltpu.VMEM((2 * hidden, rows), BF16),
            pltpu.VMEM((2 * hidden, rows), BF16),
            pltpu.VMEM((2, COLS, width), BF16),
            pltpu.VMEM((2, COLS, width), BF16),
            pltpu.VMEM((2, 3, 2 * hidden, COLS), BF16),
            pltpu.SemaphoreType.DMA((16,)),
            pltpu.SemaphoreType.DMA((2, 2)),
            pltpu.SemaphoreType.DMA((2, 2)),
            pltpu.SemaphoreType.DMA((2, 3, 2)),
        ],
        cost_estimate=pl.CostEstimate(
            flops=2 * macs, bytes_accessed=8 * rows * width + 16 * hidden * width, transcendentals=rows * hidden
        ),
        compiler_params=pltpu.CompilerParams(vmem_limit_bytes=56 * 2**20),
        name="experts",
    )(x0, x1, c0, c1, gate, w_own, w_oth)


def place_kernel(count, table, *refs):
    sources, out = refs[:count], refs[count]
    which = table[0, pl.program_id(0)]
    for k in range(count):

        @pl.when(which == k)
        def _():
            out[...] = sources[k][...].astype(out.dtype)


def place_call(sources, table, slots, parts, dtype):
    first, length = parts
    hidden, width = sources[0].shape[2:]

    def source_map(k):
        return lambda e, tab: (tab[1 + k, e], first // length, 0, 0)

    return pl.pallas_call(
        functools.partial(place_kernel, len(sources)),
        out_shape=jax.ShapeDtypeStruct((slots, length, hidden, width), dtype),
        grid_spec=pltpu.PrefetchScalarGridSpec(
            num_scalar_prefetch=1,
            grid=(slots,),
            in_specs=[
                pl.BlockSpec((1, length, hidden, width), source_map(k)) for k in range(len(sources))
            ],
            out_specs=pl.BlockSpec((1, length, hidden, width), lambda e, tab: (e, 0, 0, 0)),
        ),
        compiler_params=pltpu.CompilerParams(vmem_limit_bytes=40 * 2**20),
        name="place",
    )(table, *sources)


def routed_table(c, x):
    e = jnp.arange(EXPERTS, dtype=jnp.int32)
    firsts = [4 * c + 2 * x, 4 * c + 2 * (1 - x), 4 * (1 - c) + 2 * x, 4 * (1 - c) + 2 * (1 - x)]
    which = sum(jnp.where(e // 2 * 2 == first, k, 0) for k, first in enumerate(firsts))
    return jnp.stack([which] + [(e > first).astype(jnp.int32) for first in firsts]).astype(jnp.int32)


def shared_table(c, x):
    q = jnp.arange(4, dtype=jnp.int32)
    which = jnp.where(q // 2 == c, 0, 1)

    def blocks(half):
        return jnp.clip(q - 2 * half, 0, 1) ^ x

    return jnp.stack([which, blocks(c), blocks(1 - c)]).astype(jnp.int32)


def shards(
    block_input,
    cotangent,
    piece_starts,
    expert_ids,
    norm_gains,
    qkv_weight,
    qkv_bias,
    out_weight,
    router_weight,
    shared_gate,
    expert_gate_up,
    expert_down,
    shared_gate_up,
    shared_down,
):
    f = lax.axis_index("fsdp")
    owners = lax.axis_size("fsdp")
    r = lax.axis_index("rep")
    c, x = r % 2, r // 2
    shard = norm_gains.shape[1]
    width = owners * shard
    local_width = qkv_weight.shape[2]
    local_heads = local_width // HEAD_DIM
    half_width = local_width // 2
    hidden = expert_gate_up.shape[3]
    scale = HEAD_DIM ** (-0.5)

    def turn(rows):
        return jnp.roll(rows, -f * shard, axis=1)

    def turn_back(rows):
        return jnp.roll(rows, f * shard, axis=1)

    small = jnp.concatenate(
        [norm_gains.reshape(-1), router_weight.T.reshape(-1), shared_gate, qkv_bias.reshape(-1)]
    )
    small_all = jnp.concatenate([small[None], others_of(small[None], f, 0)], axis=0)
    gains = jnp.swapaxes(small_all[:, : 2 * shard].reshape(owners, 2, shard), 0, 1).reshape(2, width)
    gains = gains.astype(F32)
    router = jnp.swapaxes(
        small_all[:, 2 * shard : 11 * shard].reshape(owners, 9, shard), 0, 1
    ).reshape(9, width)
    bias = jnp.roll(small_all[:, 11 * shard :], f, axis=0).reshape(owners, 3, local_heads, -1)
    bias = jnp.moveaxis(bias, 0, 2).reshape(3, 1, local_width).astype(F32)
    ids_pair = jnp.concatenate([expert_ids, swap_core(expert_ids)], axis=0)

    def fetch_halves(weight, hidden_axis, shard_axis):
        mine = lax.dynamic_slice_in_dim(weight, c * half_width, half_width, hidden_axis)
        got = others_of(mine, f, shard_axis)
        peer = swap_core(got)
        both = jnp.where(
            c == 0,
            jnp.concatenate([got, peer], axis=hidden_axis),
            jnp.concatenate([peer, got], axis=hidden_axis),
        )
        return jnp.concatenate([weight, both], axis=shard_axis), got

    qkv_all, qkv_got = fetch_halves(qkv_weight, 2, 1)
    out_all, out_got = fetch_halves(after(out_weight, qkv_got), 0, 1)

    gate_up_t = jnp.transpose(expert_gate_up, (0, 2, 3, 1))
    shared_up_t = jnp.transpose(shared_gate_up, (1, 2, 0))

    def routed_chunk(first):
        return jnp.concatenate(
            [
                lax.dynamic_slice_in_dim(gate_up_t, first, 2, 0),
                lax.dynamic_slice_in_dim(expert_down, first, 2, 0)[:, None],
            ],
            axis=1,
        )

    def shared_chunk(q):
        return jnp.concatenate(
            [
                lax.dynamic_slice_in_dim(shared_up_t, q * hidden, hidden, 1),
                lax.dynamic_slice_in_dim(shared_down, q * hidden, hidden, 0)[None],
            ],
            axis=0,
        )[None]

    first_a, first_b = 4 * c + 2 * x, 4 * c + 2 * (1 - x)
    own_a, own_b = routed_chunk(first_a), routed_chunk(first_b)
    own_s0, own_s1 = shared_chunk(2 * c + x), shared_chunk(2 * c + 1 - x)
    oth_a = others_of(after(own_a, out_got), f, 3)
    oth_b = swap_x(oth_a)
    oth_s0 = others_of(after(own_s0, oth_a), f, 3)
    oth_s1 = swap_x(oth_s0)
    own_s = jnp.concatenate([own_s0, own_s1], axis=0)
    oth_s = jnp.concatenate([oth_s0, oth_s1], axis=0)

    cos_table, sin_table = rope_tables(LENGTH, HEAD_DIM)
    inputs_f = turn(block_input).astype(F32)
    cot_bf = turn(cotangent)
    cot_local = cot_bf.astype(F32)
    inverse_one = lax.rsqrt(jnp.mean(inputs_f * inputs_f, axis=-1, keepdims=True) + EPSILON)
    normed = gather_rows((inputs_f * inverse_one * gains[0]).astype(BF16))
    cot_rows = gather_rows(after(cot_bf, normed))
    cot_peer = swap_core(cot_rows)
    project = jnp.einsum("ld,cde->cle", normed, qkv_all, preferred_element_type=F32) + bias
    query_rows = rotate(
        project[0].reshape(LENGTH, local_heads, HEAD_DIM), cos_table, sin_table
    ).astype(BF16)
    key_rows = rotate(
        project[1].reshape(LENGTH, local_heads, HEAD_DIM), cos_table, sin_table
    ).astype(BF16)
    value_rows = project[2].reshape(LENGTH, local_heads, HEAD_DIM).astype(BF16)
    visible = visible_mask(piece_starts[0], LENGTH, PIECE)

    def attend_scores():
        raw = jnp.einsum("qhd,khd->hqk", query_rows, key_rows, preferred_element_type=F32) * scale
        return jnp.where(visible[None], raw, -1e30)

    scores = attend_scores()
    top_score = jnp.max(scores, axis=-1, keepdims=True)
    weights_exp = jnp.exp(scores - top_score)
    row_total = jnp.sum(weights_exp, axis=-1, keepdims=True)
    probs = weights_exp / row_total
    attended = (
        jnp.einsum("hqk,khd->qhd", probs.astype(BF16), value_rows, preferred_element_type=F32)
        .reshape(LENGTH, local_width)
        .astype(BF16)
    )
    heads_part = jnp.dot(attended, out_all, preferred_element_type=F32).astype(BF16)
    hidden_rows = inputs_f + scatter_rows(heads_part)
    inverse_two = lax.rsqrt(jnp.mean(hidden_rows * hidden_rows, axis=-1, keepdims=True) + EPSILON)
    mixed = gather_rows((hidden_rows * inverse_two * gains[1]).astype(BF16))
    mixed_peer = swap_core(mixed)
    mixed_pair = jnp.concatenate([mixed, mixed_peer], axis=0)

    logits = lax.dot_general(router, mixed_pair, (((1,), (1,)), ((), ())), preferred_element_type=F32)
    router_probs = jax.nn.softmax(logits[:EXPERTS], axis=0)
    shared_scale = jax.nn.sigmoid(logits[EXPERTS:])
    names = jnp.arange(EXPERTS, dtype=jnp.int32)[:, None, None]
    chosen = jnp.any(ids_pair.T[None] == names, axis=1)
    gates = jnp.where(chosen, router_probs, 0.0)

    def gate_rows(first):
        return jnp.pad(lax.dynamic_slice_in_dim(gates, first, 2, 0), ((0, 6), (0, 0)))

    data = (mixed, mixed_peer, cot_rows, cot_peer)
    dw_own_a, dw_oth_a, *rows_a, grad_a = experts_call(*data, gate_rows(first_a), own_a, oth_a)
    shared_rows = jnp.broadcast_to(shared_scale, (8, shared_scale.shape[1]))
    dw_own_s, dw_oth_s, *rows_s, grad_s = experts_call(*data, shared_rows, own_s, oth_s)
    dw_own_b, dw_oth_b, *rows_b, grad_b = experts_call(*data, gate_rows(first_b), own_b, oth_b)

    prob_grad = jnp.zeros_like(router_probs)
    prob_grad = lax.dynamic_update_slice_in_dim(prob_grad, grad_a[:2], first_a, 0)
    prob_grad = lax.dynamic_update_slice_in_dim(prob_grad, grad_b[:2], first_b, 0)
    prob_grad = jnp.where(chosen, prob_grad, 0.0)
    logit_grad = router_probs * (prob_grad - jnp.sum(router_probs * prob_grad, axis=0, keepdims=True))
    scale_logit_grad = (grad_s[0:1] + grad_s[1:2]) * shared_scale * (1.0 - shared_scale)
    small_grad = jnp.concatenate([logit_grad, scale_logit_grad], axis=0)
    high = small_grad.astype(BF16)
    low = (small_grad - high.astype(F32)).astype(BF16)
    small_pair = jnp.concatenate([high, low], axis=0)
    router_both = jnp.dot(small_pair, mixed_pair, preferred_element_type=F32)
    router_grad = router_both[:9] + router_both[9:]
    router_twice = jnp.concatenate([router, router], axis=0)

    def extra(part):
        return lax.dot_general(
            small_pair[:, part * LENGTH : (part + 1) * LENGTH],
            router_twice,
            (((0,), (0,)), ((), ())),
            preferred_element_type=F32,
        )

    def total(index):
        return (
            rows_a[index].astype(F32) + rows_s[index].astype(F32) + rows_b[index].astype(F32)
        )

    normed_for_peer = (total(3) + extra(1)).astype(BF16)
    normed_grad = total(2) + extra(0) + swap_core(normed_for_peer).astype(F32)
    normed_two_grad = scatter_rows(normed_grad.astype(BF16))
    scaled_two = normed_two_grad * gains[1]
    hidden_grad = cot_local + inverse_two * (
        scaled_two
        - hidden_rows
        * inverse_two
        * inverse_two
        * jnp.mean(scaled_two * hidden_rows, axis=-1, keepdims=True)
    )
    gain_two_grad = jnp.sum(normed_two_grad * hidden_rows * inverse_two, axis=0)
    branch_grad = gather_rows(hidden_grad.astype(BF16))

    mixer_for_peer = after(total(1).astype(BF16), branch_grad)
    mixer = (total(0) + swap_core(mixer_for_peer).astype(F32)).astype(BF16)
    result = turn_back((hidden_rows + scatter_rows(mixer)).astype(BF16))

    out_grad = jnp.einsum("lf,ld->fd", attended, branch_grad, preferred_element_type=F32).astype(BF16)
    attended_grad = jnp.einsum("ld,fd->lf", branch_grad, out_all, preferred_element_type=F32)
    attended_grad = attended_grad.astype(BF16).reshape(LENGTH, local_heads, HEAD_DIM)
    probs = jnp.exp(attend_scores() - top_score) / row_total
    value_grad = jnp.einsum("hqk,qhd->khd", probs.astype(BF16), attended_grad, preferred_element_type=F32)
    pgrad_rows = jnp.einsum("qhd,khd->hqk", attended_grad, value_rows, preferred_element_type=F32)
    score_grad = (
        probs * (pgrad_rows - jnp.sum(probs * pgrad_rows, axis=-1, keepdims=True))
    ).astype(BF16)
    query_grad = jnp.einsum("hqk,khd->qhd", score_grad, key_rows, preferred_element_type=F32) * scale
    key_grad = jnp.einsum("hqk,qhd->khd", score_grad, query_rows, preferred_element_type=F32) * scale
    project_grad = jnp.stack(
        [
            rotate(query_grad, cos_table, -sin_table).reshape(LENGTH, local_width),
            rotate(key_grad, cos_table, -sin_table).reshape(LENGTH, local_width),
            value_grad.reshape(LENGTH, local_width),
        ]
    ).astype(BF16)
    bias_grad = jnp.sum(project_grad, axis=1, dtype=F32)
    normed_one_grad = jnp.einsum("cle,cde->ld", project_grad, qkv_all, preferred_element_type=F32)
    input_row_grad = scatter_rows(normed_one_grad.astype(BF16))
    qkv_grad = jnp.einsum("ld,cle->cde", normed, project_grad, preferred_element_type=F32).astype(BF16)
    scaled_one = input_row_grad * gains[0]
    input_grad = hidden_grad + inverse_one * (
        scaled_one
        - inputs_f
        * inverse_one
        * inverse_one
        * jnp.mean(scaled_one * inputs_f, axis=-1, keepdims=True)
    )
    gain_one_grad = jnp.sum(input_row_grad * inputs_f * inverse_one, axis=0)

    def shard_sum(own, other):
        return reduce_fsdp(own, other, f, 3).astype(BF16)

    sum_a = shard_sum(dw_own_a, dw_oth_a)
    sum_s = shard_sum(dw_own_s, dw_oth_s)
    sum_b = shard_sum(dw_own_b, dw_oth_b)
    from_a, from_s, from_b = swap_x(sum_a), swap_x(sum_s), swap_x(sum_b)

    def add(one, two):
        return (one.astype(F32) + two.astype(F32)).astype(BF16)

    total_b = add(sum_b, from_a)
    total_s = add(sum_s, from_s[::-1])
    total_a = add(sum_a, from_b)
    peer_s, peer_b, peer_a = swap_core(total_s), swap_core(total_b), swap_core(total_a)
    table = routed_table(c, x)
    routed = [total_a, total_b, peer_a, peer_b]
    gate_up_out = jnp.transpose(place_call(routed, table, EXPERTS, (0, 2), F32), (0, 3, 1, 2))
    down_out = place_call(routed, table, EXPERTS, (2, 1), F32).reshape(EXPERTS, hidden, shard)
    table_s = shared_table(c, x)
    shared_up_out = place_call([total_s, peer_s], table_s, 4, (0, 2), BF16)
    shared_up_out = (
        jnp.transpose(shared_up_out, (3, 1, 0, 2)).reshape(shard, 2, 4 * hidden).astype(F32)
    )
    shared_down_out = place_call([total_s, peer_s], table_s, 4, (2, 1), F32).reshape(4 * hidden, shard)

    def dense_sum(grad, hidden_axis, shard_axis):
        keep = lax.dynamic_slice_in_dim(grad, c * half_width, half_width, hidden_axis)
        send = lax.dynamic_slice_in_dim(grad, (1 - c) * half_width, half_width, hidden_axis)
        both = add(keep, swap_core(send))
        own = lax.slice_in_dim(both, 0, shard, axis=shard_axis)
        other = lax.slice_in_dim(both, shard, width, axis=shard_axis)
        part = reduce_fsdp(own, other, f, shard_axis).astype(BF16)
        part = add(part, swap_x(part))
        peer = swap_core(part)
        return jnp.where(
            c == 0,
            jnp.concatenate([part, peer], axis=hidden_axis),
            jnp.concatenate([peer, part], axis=hidden_axis),
        ).astype(F32)

    out_out = dense_sum(out_grad, 0, 1)
    qkv_out = dense_sum(qkv_grad, 2, 1)

    early = jnp.concatenate([router_grad, gain_two_grad[None]], axis=0)
    early = sum_small(early[:, :shard], early[:, shard:], f)
    late = sum_small(gain_one_grad[None, :shard], gain_one_grad[None, shard:], f)
    gains_out = jnp.concatenate([late, early[9:10]], axis=0)
    bias_sum = sum_rep(lax.psum(bias_grad, "fsdp") if owners != 2 else bias_grad + swap_y(bias_grad))
    bias_out = lax.dynamic_slice_in_dim(
        bias_sum.reshape(3, local_heads, HEAD_DIM), f * (HEAD_DIM // owners), HEAD_DIM // owners, 2
    )
    return (
        result,
        turn_back(input_grad),
        gains_out,
        qkv_out,
        bias_out,
        out_out,
        early[:EXPERTS].T,
        early[EXPERTS],
        gate_up_out,
        down_out,
        shared_up_out,
        shared_down_out,
    )


def solution(mesh):
    in_specs = (
        P(("rep", "fsdp", "tensor"), None),
        P(("rep", "fsdp", "tensor"), None),
        P(("rep", "fsdp"), None),
        P(("rep", "fsdp"), None),
        P(None, "fsdp"),
        P(None, "fsdp", "tensor"),
        P(None, "tensor", "fsdp"),
        P("tensor", "fsdp"),
        P("fsdp", None),
        P("fsdp"),
        P(None, "fsdp", None, "tensor"),
        P(None, "tensor", "fsdp"),
        P("fsdp", None, "tensor"),
        P("tensor", "fsdp"),
    )
    out_specs = (
        P(("rep", "fsdp", "tensor"), None),
        P(("rep", "fsdp", "tensor"), None),
        P(None, "fsdp"),
        P(None, "fsdp", "tensor"),
        P(None, "tensor", "fsdp"),
        P("tensor", "fsdp"),
        P("fsdp", None),
        P("fsdp"),
        P(None, "fsdp", None, "tensor"),
        P(None, "tensor", "fsdp"),
        P("fsdp", None, "tensor"),
        P("tensor", "fsdp"),
    )
    return jax.shard_map(shards, mesh=mesh, in_specs=in_specs, out_specs=out_specs, check_vma=False)
```

```python
import functools

import jax
import jax.numpy as jnp
from jax import lax
from jax.experimental import pallas as pl
from jax.experimental.pallas import tpu as pltpu
from jax.sharding import PartitionSpec as P

HEAD_DIM = 128
EXPERTS = 8
LENGTH = 640
PIECE = 256
EPSILON = 1e-06
BF16 = jnp.bfloat16
F32 = jnp.float32
COLS = 256
MESH = pl.DeviceIdType.MESH


def rope_tables(length, head_dim):
    half_dim = head_dim // 2
    frequency = 1000000.0 ** (-jnp.arange(half_dim, dtype=F32) * (2.0 / head_dim))
    angles = jnp.arange(length, dtype=F32)[:, None] * frequency[None, :]
    return (jnp.cos(angles), jnp.sin(angles))


def rotate(head_rows, cos_table, sin_table):
    half_dim = head_rows.shape[-1] // 2
    leading = head_rows[..., :half_dim]
    trailing = head_rows[..., half_dim:]
    cos_rows = cos_table[:, None, :]
    sin_rows = sin_table[:, None, :]
    return jnp.concatenate(
        [leading * cos_rows - trailing * sin_rows, trailing * cos_rows + leading * sin_rows],
        axis=-1,
    )


def visible_mask(starts_row, length, piece_len):
    position = jnp.arange(length, dtype=jnp.int32)
    inside = (position[None, :] >= starts_row[:, None]) & (
        position[None, :] < starts_row[:, None] + piece_len
    )
    label_ids = jnp.arange(1, starts_row.shape[0] + 1, dtype=jnp.int32)[:, None]
    labels = jnp.sum(jnp.where(inside, label_ids, 0), axis=0)
    causal = position[None, :] <= position[:, None]
    same_piece = (labels[:, None] == labels[None, :]) & (labels[:, None] > 0)
    return causal | same_piece


def after(value, *others):
    return lax.optimization_barrier((value,) + others)[0]


def swap_y(a):
    return lax.ppermute(a, "fsdp", [(0, 1), (1, 0)])


def swap_x(a):
    n = lax.axis_size("rep")
    return lax.ppermute(a, "rep", [(i, i ^ 2) for i in range(n)])


def swap_core(a):
    n = lax.axis_size("rep")
    return lax.ppermute(a, "rep", [(i, i ^ 1) for i in range(n)])


CHUNK = 32


def device(axis, index):
    return {axis: index}


def rows_kernel(n, rows, with_core_in, with_scatter, with_gather, with_core_out, middle, extra_count, extra_out, *refs):
    refs = list(refs)
    take = refs.pop
    part = take(0)
    part_peer = take(0) if with_core_in else None
    extras = [take(0) for _ in range(extra_count)]
    outs = [take(0) for _ in range(extra_out)]
    full = take(0) if with_gather else None
    full_peer = take(0) if with_core_out else None
    chunks = rows // CHUNK
    z = lax.axis_index("tensor")
    r = lax.axis_index("rep")
    core = r + 1 - 2 * lax.rem(r, 2)
    has_left, has_right = z > 0, z < n - 1
    pairs = with_core_in or with_core_out
    if with_core_in:
        core_buf, core_in_send, core_in_recv = take(0), take(0), take(0)
    if with_scatter:
        in_bufs, out_bufs = (take(0), take(0)), (take(0), take(0))
        sc_send, sc_recv = take(0), take(0)
    if with_gather:
        ga_send, ga_recv = take(0), take(0)
    if with_core_out:
        core_out_send, core_out_recv = take(0), take(0)

    barrier = pltpu.get_barrier_semaphore()

    @pl.when(has_left)
    def _():
        pl.semaphore_signal(barrier, inc=1, device_id=device("tensor", z - 1), device_id_type=MESH)

    @pl.when(has_right)
    def _():
        pl.semaphore_signal(barrier, inc=1, device_id=device("tensor", z + 1), device_id_type=MESH)

    if pairs:
        pl.semaphore_signal(barrier, inc=1, device_id=device("rep", core), device_id_type=MESH)
    greeted = jnp.where(has_left, 1, 0) + jnp.where(has_right, 1, 0) + (1 if pairs else 0)
    pl.semaphore_wait(barrier, greeted)

    def chunk_at(block, i):
        return pl.ds(pl.multiple_of(block * rows + i * CHUNK, CHUNK), CHUNK)

    def chunk_in(i):
        return pl.ds(pl.multiple_of(i * CHUNK, CHUNK), CHUNK)

    def remote(src, dst, send, recv, axis, index):
        return pltpu.make_async_remote_copy(
            src_ref=src, dst_ref=dst, send_sem=send, recv_sem=recv,
            device_id=device(axis, index), device_id_type=MESH,
        )

    def core_in_copy(block, i):
        here = chunk_at(block, i)
        return remote(
            part_peer.at[here], core_buf.at[here], core_in_send.at[block, i], core_in_recv.at[block, i], "rep", core
        )

    def scatter_copy(way, m, i):
        here = chunk_in(i)
        return remote(
            out_bufs[way].at[m, here], in_bufs[way].at[m, here], sc_send.at[way, m, i], sc_recv.at[way, m, i],
            "tensor", z + 1 - 2 * way,
        )

    def gather_copy(way, k, i):
        here = chunk_at(z - k + 2 * k * way, i)
        return remote(
            full.at[here], full.at[here], ga_send.at[way, k, i], ga_recv.at[way, k, i], "tensor", z + 1 - 2 * way
        )

    def core_out_copy(block, i):
        here = chunk_at(block, i)
        return remote(
            full.at[here], full_peer.at[here], core_out_send.at[block, i], core_out_recv.at[block, i], "rep", core
        )

    def all_chunks(body):
        def step(i, carry):
            body(i)
            return carry

        lax.fori_loop(0, chunks, step, 0)

    if with_core_in:

        @all_chunks
        def _(i):
            for block in range(n):
                core_in_copy(block, i).start()

    def term(block, i):
        here = chunk_at(block, i)
        value = part[here, :].astype(F32)
        if with_core_in:
            core_in_copy(block, i).wait_recv()
            value = value + core_buf[here, :].astype(F32)
        return value

    def inside(i):
        return (i >= 0) & (i < chunks)

    def scatter_step(way, i, has_source, does_send):
        for m in range(n - 1):
            block = n - 1 - m if way == 0 else m
            here = chunk_in(i)

            @pl.when(inside(i) & does_send(block))
            def _():
                value = term(block, i)

                @pl.when(has_source)
                def _():
                    scatter_copy(way, m, i).wait_recv()
                    out_bufs[way][m, here, :] = (value + in_bufs[way][m, here, :].astype(F32)).astype(BF16)

                @pl.when(jnp.logical_not(has_source))
                def _():
                    out_bufs[way][m, here, :] = value.astype(BF16)

                scatter_copy(way, m, i).start()

    def own_step(i):
        @pl.when(inside(i))
        def _():
            here = chunk_in(i)
            if with_scatter:
                total[...] = term(z, i)

                @pl.when(has_left)
                def _():
                    m = n - 1 - z
                    scatter_copy(0, m, i).wait_recv()
                    total[...] += in_bufs[0][m, here, :].astype(F32)

                @pl.when(has_right)
                def _():
                    scatter_copy(1, z, i).wait_recv()
                    total[...] += in_bufs[1][z, here, :].astype(F32)

                sent = middle(total[...], here, extras, outs)
            else:
                sent = part[here, :]
            if with_gather:
                full[chunk_at(z, i), :] = sent

                @pl.when(has_right)
                def _():
                    gather_copy(0, 0, i).start()

                @pl.when(has_left)
                def _():
                    gather_copy(1, 0, i).start()

                if with_core_out:
                    core_out_copy(z, i).start()

    def gather_step(k, i):
        for way in range(2):
            comes = z - k >= 0 if way == 0 else z + k <= n - 1
            goes = has_right if way == 0 else has_left

            @pl.when(inside(i) & comes)
            def _():
                landed = full.at[chunk_at(z - k + 2 * k * way, i)]
                remote(
                    landed, landed, ga_send.at[way, k - 1, i], ga_recv.at[way, k - 1, i], "tensor", z + 1 - 2 * way
                ).wait_recv()
                if k < n - 1:

                    @pl.when(goes)
                    def _():
                        gather_copy(way, k, i).start()

                if with_core_out:
                    core_out_copy(z - k + 2 * k * way, i).start()

    lead = n - 1 if with_scatter else 0
    if with_scatter:
        total = take(0)

    def tick(t, carry):
        if with_scatter:
            scatter_step(0, t - z, has_left, lambda block: block > z)
            scatter_step(1, t - (n - 1 - z), has_right, lambda block: block < z)
        own_step(t - lead)
        if with_gather:
            for k in range(1, n):
                gather_step(k, t - lead - k)
        return carry

    lax.fori_loop(0, chunks + lead + (n - 1 if with_gather else 0), tick, 0)

    @all_chunks
    def _(i):
        if with_core_in:
            for block in range(n):
                core_in_copy(block, i).wait_send()
        for way in range(2):
            goes = has_right if way == 0 else has_left
            if with_scatter:
                for m in range(n - 1):
                    block = n - 1 - m if way == 0 else m

                    @pl.when(goes & ((block > z) if way == 0 else (block < z)))
                    def _():
                        scatter_copy(way, m, i).wait_send()

            if with_gather:
                for k in range(n - 1):
                    has = z - k >= 0 if way == 0 else z + k <= n - 1

                    @pl.when(goes & has)
                    def _():
                        gather_copy(way, k, i).wait_send()

        if with_core_out:
            for block in range(n):
                core_out_copy(block, i).wait_send()
                core_out_copy(block, i).wait_recv()


def rows_call(
    collective_id, part, part_peer=None, extras=(), scatter=True, gather=True, core_out=False, middle=None, out_types=()
):
    n = lax.axis_size("tensor")
    width = part.shape[1]
    rows = part.shape[0] // n if scatter else part.shape[0]
    chunks = rows // CHUNK
    vmem_spec = pl.BlockSpec(memory_space=pltpu.VMEM)
    full = jax.ShapeDtypeStruct((n * rows, width), BF16)
    out_shape = list(out_types) + ([full] if gather else []) + ([full] if core_out else [])
    scratch = []
    if part_peer is not None:
        scratch += [pltpu.VMEM((n * rows, width), BF16)] + [pltpu.SemaphoreType.DMA((n, chunks))] * 2
    if scatter:
        scratch += [pltpu.VMEM((n - 1, rows, width), BF16)] * 4
        scratch += [pltpu.SemaphoreType.DMA((2, n - 1, chunks))] * 2
    if gather:
        scratch += [pltpu.SemaphoreType.DMA((2, n - 1, chunks))] * 2
    if core_out:
        scratch += [pltpu.SemaphoreType.DMA((n, chunks))] * 2
    if scatter:
        scratch += [pltpu.VMEM((CHUNK, width), F32)]
    operands = [part] + ([part_peer] if part_peer is not None else []) + list(extras)
    return pl.pallas_call(
        functools.partial(
            rows_kernel, n, rows, part_peer is not None, scatter, gather, core_out, middle, len(extras), len(out_types)
        ),
        out_shape=out_shape,
        in_specs=[vmem_spec] * len(operands),
        out_specs=[vmem_spec] * len(out_shape),
        scratch_shapes=scratch,
        compiler_params=pltpu.CompilerParams(
            collective_id=collective_id, has_side_effects=True, vmem_limit_bytes=48 * 2**20
        ),
        name="rows",
    )(*operands)


def norm_middle(total, here, extras, outs):
    inputs, gain = extras
    hidden = inputs[here, :].astype(F32) + total
    outs[0][here, :] = hidden
    inverse = lax.rsqrt(jnp.mean(hidden * hidden, axis=-1, keepdims=True) + EPSILON)
    return (hidden * inverse * gain[...]).astype(BF16)


def norm_back_middle(total, here, extras, outs):
    hidden_ref, cot, gain = extras
    hidden = hidden_ref[here, :]
    inverse = lax.rsqrt(jnp.mean(hidden * hidden, axis=-1, keepdims=True) + EPSILON)
    scaled = total * gain[...]
    grad = cot[here, :].astype(F32) + inverse * (
        scaled - hidden * inverse * inverse * jnp.mean(scaled * hidden, axis=-1, keepdims=True)
    )
    outs[0][here, :] = total
    outs[1][here, :] = grad
    return grad.astype(BF16)


def plain_middle(total, here, extras, outs):
    outs[0][here, :] = total


def others_of(own, f, axis):
    if lax.axis_size("fsdp") == 2:
        return swap_y(own)
    whole = lax.all_gather(own, "fsdp", axis=axis, tiled=True)
    size = own.shape[axis]
    turned = jnp.roll(whole, -f * size, axis=axis)
    return lax.slice_in_dim(turned, size, whole.shape[axis], axis=axis)


def reduce_fsdp(own, other, f, axis):
    if lax.axis_size("fsdp") == 2:
        return own.astype(F32) + swap_y(other).astype(F32)
    whole = jnp.roll(jnp.concatenate([own, other], axis=axis), f * own.shape[axis], axis=axis)
    return lax.psum_scatter(whole, "fsdp", scatter_dimension=axis, tiled=True).astype(F32)


def sum_small(values, f, shard):
    total = sum_rep_first(sum_tensor(values))
    if lax.axis_size("fsdp") == 2:
        total = total[:, :shard] + swap_y(total[:, shard:])
    else:
        whole = jnp.roll(total, f * shard, axis=1)
        total = lax.psum_scatter(whole, "fsdp", scatter_dimension=1, tiled=True)
    return total + swap_x(total)


def sum_rep_first(total):
    return total + swap_core(total)


def sum_rep(total):
    total = total + swap_core(total)
    return total + swap_x(total)


def sum_tensor(total):
    n = lax.axis_size("tensor")
    step = 1
    while step < n:
        total = total + lax.ppermute(total, "tensor", [(i, i ^ step) for i in range(n)])
        step *= 2
    return total


def dot_nt(a, b):
    return lax.dot_general(a, b, (((1,), (1,)), ((), ())), preferred_element_type=F32)


def dot_nn(a, b):
    return lax.dot_general(a, b, (((1,), (0,)), ((), ())), preferred_element_type=F32)


def experts_kernel(
    rows, width, own_width, hidden,
    x0, x1, c0, c1, gate, w_own0, w_own1, w_oth0, w_oth1,
    dw_own, dw_oth, mix0, mix1, ng0, ng1, gate_grad,
    xv, cv, wg, wu, wd, ga, pg, pu, st_mix, st_ng, st_dw, in_sem, mix_sem, ng_sem, dw_sem,
):
    seq = rows // 2
    loads = []

    def load(src, dst):
        copy = pltpu.make_async_copy(src, dst, in_sem.at[len(loads)])
        copy.start()
        loads.append(copy)

    for part, w in ((0, wg), (1, wu), (2, wd)):
        for k in range(2):
            r = pl.ds(k * hidden, hidden)
            load((w_own0, w_own1)[k].at[part], w.at[r, pl.ds(0, own_width)])
            load((w_oth0, w_oth1)[k].at[part], w.at[r, pl.ds(own_width, width - own_width)])
        if part == 0:
            load(x0, xv.at[pl.ds(0, seq)])
            load(x1, xv.at[pl.ds(seq, seq)])
        if part == 1:
            load(c0, cv.at[pl.ds(0, seq)])
            load(c1, cv.at[pl.ds(seq, seq)])
    for copy in loads:
        copy.wait()

    tiles = rows // COLS

    def out_copies(t, slot):
        copies = []
        for stage, outs, sem in ((st_mix, (mix0, mix1), mix_sem), (st_ng, (ng0, ng1), ng_sem)):
            for part in range(2):
                copies.append((stage.at[slot, pl.ds(part * 128, 128)], outs, sem.at[slot, part], part))
        return copies

    def start_out(t, slot):
        for src, outs, sem, part in out_copies(t, slot):
            first = t * COLS + part * 128

            @pl.when(first < seq)
            def _():
                pltpu.make_async_copy(src, outs[0].at[pl.ds(pl.multiple_of(first, 128), 128)], sem).start()

            @pl.when(first >= seq)
            def _():
                pltpu.make_async_copy(
                    src, outs[1].at[pl.ds(pl.multiple_of(first - seq, 128), 128)], sem
                ).start()

    def wait_out(slot):
        for src, outs, sem, part in out_copies(0, slot):
            pltpu.make_async_copy(src, outs[0].at[pl.ds(0, 128)], sem).wait()

    def token_tile(t, carry):
        slot = lax.rem(t, 2)
        here = pl.ds(pl.multiple_of(t * COLS, COLS), COLS)
        g = dot_nt(wg[...], xv[here, :])
        u = dot_nt(wu[...], xv[here, :])
        h = dot_nt(wd[...], cv[here, :])
        sig = jax.nn.sigmoid(g)
        act = g * sig * u
        product = act * h
        scale_rows = []
        for k in range(2):
            part = product[k * hidden : (k + 1) * hidden]
            gate_grad[pl.ds(k, 1), here] = jnp.sum(part, axis=0, keepdims=True)
            scale_rows.append(jnp.broadcast_to(gate[pl.ds(k, 1), here], (hidden, COLS)))
        scale = jnp.concatenate(scale_rows, axis=0)
        back = scale * h
        ga_t = (scale * act).astype(BF16)
        pg_t = (back * u * sig * (1.0 + g * (1.0 - sig))).astype(BF16)
        pu_t = (back * g * sig).astype(BF16)
        ga[:, here] = ga_t
        pg[:, here] = pg_t
        pu[:, here] = pu_t

        @pl.when(t >= 2)
        def _():
            wait_out(slot)

        st_mix[slot] = dot_nn(ga_t.T, wd[...]).astype(BF16)
        st_ng[slot] = (dot_nn(pg_t.T, wg[...]) + dot_nn(pu_t.T, wu[...])).astype(BF16)
        start_out(t, slot)
        return carry

    lax.fori_loop(0, tiles, token_tile, 0)

    def wait_dw(slot):
        for part in range(3):
            for k in range(2):
                pltpu.make_async_copy(
                    st_dw.at[slot, part, pl.ds(k * hidden, hidden)],
                    dw_own.at[k, part, :, pl.ds(0, COLS)],
                    dw_sem.at[slot, part, k],
                ).wait()

    def weight_tile(n, slot, src_col, dst, dst_col, first):
        cols = pl.ds(pl.multiple_of(src_col, COLS), COLS)

        @pl.when(jnp.logical_not(first))
        def _():
            wait_dw(slot)

        xs = xv[:, cols]
        st_dw[slot, 0] = dot_nn(pg[...], xs).astype(BF16)
        st_dw[slot, 1] = dot_nn(pu[...], xs).astype(BF16)
        st_dw[slot, 2] = dot_nn(ga[...], cv[:, cols]).astype(BF16)
        for part in range(3):
            for k in range(2):
                pltpu.make_async_copy(
                    st_dw.at[slot, part, pl.ds(k * hidden, hidden)],
                    dst.at[k, part, :, pl.ds(pl.multiple_of(dst_col, COLS), COLS)],
                    dw_sem.at[slot, part, k],
                ).start()

    oth_tiles = (width - own_width) // COLS
    own_tiles = own_width // COLS

    def oth_tile(n, carry):
        weight_tile(n, lax.rem(n, 2), own_width + n * COLS, dw_oth, n * COLS, n < 2)
        return carry

    def own_tile(n, carry):
        weight_tile(n, lax.rem(n + oth_tiles, 2), n * COLS, dw_own, n * COLS, n + oth_tiles < 2)
        return carry

    lax.fori_loop(0, oth_tiles, oth_tile, 0)
    lax.fori_loop(0, own_tiles, own_tile, 0)
    for slot in range(2):
        wait_out(slot)
        wait_dw(slot)


def experts_call(x0, x1, c0, c1, gate, w_own, w_oth):
    seq, width = x0.shape
    rows = 2 * seq
    hidden, own_width = w_own[0].shape[1:]
    any_spec = pl.BlockSpec(memory_space=pl.ANY)
    vmem_spec = pl.BlockSpec(memory_space=pltpu.VMEM)
    out_rows = jax.ShapeDtypeStruct((seq, width), BF16)
    macs = 9 * rows * width * 2 * hidden
    return pl.pallas_call(
        functools.partial(experts_kernel, rows, width, own_width, hidden),
        out_shape=[
            jax.ShapeDtypeStruct((2, 3, hidden, own_width), BF16),
            jax.ShapeDtypeStruct((2, 3, hidden, width - own_width), BF16),
            out_rows, out_rows, out_rows, out_rows,
            jax.ShapeDtypeStruct((8, rows), F32),
        ],
        in_specs=[any_spec] * 4 + [vmem_spec] + [any_spec] * 4,
        out_specs=[any_spec] * 6 + [vmem_spec],
        scratch_shapes=[
            pltpu.VMEM((rows, width), BF16),
            pltpu.VMEM((rows, width), BF16),
            pltpu.VMEM((2 * hidden, width), BF16),
            pltpu.VMEM((2 * hidden, width), BF16),
            pltpu.VMEM((2 * hidden, width), BF16),
            pltpu.VMEM((2 * hidden, rows), BF16),
            pltpu.VMEM((2 * hidden, rows), BF16),
            pltpu.VMEM((2 * hidden, rows), BF16),
            pltpu.VMEM((2, COLS, width), BF16),
            pltpu.VMEM((2, COLS, width), BF16),
            pltpu.VMEM((2, 3, 2 * hidden, COLS), BF16),
            pltpu.SemaphoreType.DMA((16,)),
            pltpu.SemaphoreType.DMA((2, 2)),
            pltpu.SemaphoreType.DMA((2, 2)),
            pltpu.SemaphoreType.DMA((2, 3, 2)),
        ],
        cost_estimate=pl.CostEstimate(
            flops=2 * macs, bytes_accessed=8 * rows * width + 16 * hidden * width, transcendentals=rows * hidden
        ),
        compiler_params=pltpu.CompilerParams(vmem_limit_bytes=56 * 2**20),
        name="experts",
    )(x0, x1, c0, c1, gate, *w_own, *w_oth)


def place_kernel(count, table, *refs):
    sources, out = refs[:count], refs[count]
    which = table[0, pl.program_id(0)]
    for k in range(count):

        @pl.when(which == k)
        def _():
            out[...] = sources[k][...].astype(out.dtype)


def place_call(sources, table, slots, parts, dtype):
    first, length = parts
    hidden, width = sources[0].shape[2:]

    def source_map(k):
        return lambda e, tab: (tab[1 + k, e], first // length, 0, 0)

    return pl.pallas_call(
        functools.partial(place_kernel, len(sources)),
        out_shape=jax.ShapeDtypeStruct((slots, length, hidden, width), dtype),
        grid_spec=pltpu.PrefetchScalarGridSpec(
            num_scalar_prefetch=1,
            grid=(slots,),
            in_specs=[
                pl.BlockSpec((1, length, hidden, width), source_map(k)) for k in range(len(sources))
            ],
            out_specs=pl.BlockSpec((1, length, hidden, width), lambda e, tab: (e, 0, 0, 0)),
        ),
        compiler_params=pltpu.CompilerParams(vmem_limit_bytes=40 * 2**20),
        name="place",
    )(table, *sources)


def routed_table(c, x):
    e = jnp.arange(EXPERTS, dtype=jnp.int32)
    firsts = [4 * c + 2 * x, 4 * c + 2 * (1 - x), 4 * (1 - c) + 2 * x, 4 * (1 - c) + 2 * (1 - x)]
    which = sum(jnp.where(e // 2 * 2 == first, k, 0) for k, first in enumerate(firsts))
    return jnp.stack([which] + [(e > first).astype(jnp.int32) for first in firsts]).astype(jnp.int32)


def shared_table(c, x):
    q = jnp.arange(4, dtype=jnp.int32)
    which = jnp.where(q // 2 == c, 0, 1)

    def blocks(half):
        return jnp.clip(q - 2 * half, 0, 1) ^ x

    return jnp.stack([which, blocks(c), blocks(1 - c)]).astype(jnp.int32)


def shards(
    block_input,
    cotangent,
    piece_starts,
    expert_ids,
    norm_gains,
    qkv_weight,
    qkv_bias,
    out_weight,
    router_weight,
    shared_gate,
    expert_gate_up,
    expert_down,
    shared_gate_up,
    shared_down,
):
    f = lax.axis_index("fsdp")
    owners = lax.axis_size("fsdp")
    r = lax.axis_index("rep")
    c, x = r % 2, r // 2
    shard = norm_gains.shape[1]
    width = owners * shard
    local_width = qkv_weight.shape[2]
    local_heads = local_width // HEAD_DIM
    half_width = local_width // 2
    hidden = expert_gate_up.shape[3]
    scale = HEAD_DIM ** (-0.5)

    def turn(rows):
        return jnp.roll(rows, -f * shard, axis=1)

    def turn_back(rows):
        return jnp.roll(rows, f * shard, axis=1)

    small = jnp.concatenate(
        [norm_gains.reshape(-1), router_weight.T.reshape(-1), shared_gate, qkv_bias.reshape(-1)]
    )
    small_all = jnp.concatenate([small[None], others_of(small[None], f, 0)], axis=0)
    gains = jnp.swapaxes(small_all[:, : 2 * shard].reshape(owners, 2, shard), 0, 1).reshape(2, width)
    gains = gains.astype(F32)
    router = jnp.swapaxes(
        small_all[:, 2 * shard : 11 * shard].reshape(owners, 9, shard), 0, 1
    ).reshape(9, width)
    bias = jnp.roll(small_all[:, 11 * shard :], f, axis=0).reshape(owners, 3, local_heads, -1)
    bias = jnp.moveaxis(bias, 0, 2).reshape(3, 1, local_width).astype(F32)
    ids_pair = jnp.concatenate([expert_ids, swap_core(expert_ids)], axis=0)

    def fetch_halves(weight, hidden_axis, shard_axis):
        mine = lax.dynamic_slice_in_dim(weight, c * half_width, half_width, hidden_axis)
        got = others_of(mine, f, shard_axis)
        peer = swap_core(got)
        both = jnp.where(
            c == 0,
            jnp.concatenate([got, peer], axis=hidden_axis),
            jnp.concatenate([peer, got], axis=hidden_axis),
        )
        return jnp.concatenate([weight, both], axis=shard_axis), got

    qkv_all, qkv_got = fetch_halves(qkv_weight, 2, 1)
    out_all, out_got = fetch_halves(after(out_weight, qkv_got), 0, 1)

    gate_up_t = jnp.transpose(expert_gate_up, (0, 2, 3, 1))
    shared_up_t = jnp.transpose(shared_gate_up, (1, 2, 0))

    def routed_chunk(first):
        return jnp.concatenate(
            [
                lax.dynamic_slice_in_dim(gate_up_t, first, 2, 0),
                lax.dynamic_slice_in_dim(expert_down, first, 2, 0)[:, None],
            ],
            axis=1,
        )

    def shared_chunk(q):
        return jnp.concatenate(
            [
                lax.dynamic_slice_in_dim(shared_up_t, q * hidden, hidden, 1),
                lax.dynamic_slice_in_dim(shared_down, q * hidden, hidden, 0)[None],
            ],
            axis=0,
        )[None]

    first_a, first_b = 4 * c + 2 * x, 4 * c + 2 * (1 - x)
    own_a, own_b = routed_chunk(first_a), routed_chunk(first_b)
    own_s = jnp.concatenate([shared_chunk(2 * c + x), shared_chunk(2 * c + 1 - x)], axis=0)

    cos_table, sin_table = rope_tables(LENGTH, HEAD_DIM)
    inputs = turn(block_input)
    inputs_f = inputs.astype(F32)
    cot = turn(cotangent)
    inverse_one = lax.rsqrt(jnp.mean(inputs_f * inputs_f, axis=-1, keepdims=True) + EPSILON)
    (normed,) = rows_call(0, (inputs_f * inverse_one * gains[0]).astype(BF16), scatter=False)
    cot_rows = lax.all_gather(after(cot, normed), "tensor", axis=0, tiled=True)
    cot_peer = swap_core(cot_rows)
    oth_a = others_of(after(own_a, normed, qkv_got), f, 3)
    project = jnp.einsum("ld,cde->cle", normed, qkv_all, preferred_element_type=F32) + bias
    query_rows = rotate(
        project[0].reshape(LENGTH, local_heads, HEAD_DIM), cos_table, sin_table
    ).astype(BF16)
    key_rows = rotate(
        project[1].reshape(LENGTH, local_heads, HEAD_DIM), cos_table, sin_table
    ).astype(BF16)
    value_rows = project[2].reshape(LENGTH, local_heads, HEAD_DIM).astype(BF16)
    visible = visible_mask(piece_starts[0], LENGTH, PIECE)
    oth_s = others_of(after(own_s, query_rows, out_got), f, 3)
    oth_b = swap_x(oth_a)

    def attend_scores():
        raw = jnp.einsum("qhd,khd->hqk", query_rows, key_rows, preferred_element_type=F32) * scale
        return jnp.where(visible[None], raw, -1e30)

    scores = attend_scores()
    top_score = jnp.max(scores, axis=-1, keepdims=True)
    weights_exp = jnp.exp(scores - top_score)
    row_total = jnp.sum(weights_exp, axis=-1, keepdims=True)
    probs = weights_exp / row_total
    attended = (
        jnp.einsum("hqk,khd->qhd", probs.astype(BF16), value_rows, preferred_element_type=F32)
        .reshape(LENGTH, local_width)
        .astype(BF16)
    )
    heads_part = jnp.dot(attended, out_all, preferred_element_type=F32).astype(BF16)
    block_f32 = jax.ShapeDtypeStruct(inputs.shape, F32)
    hidden_rows, mixed, mixed_peer = rows_call(
        1, heads_part, extras=(inputs, gains[1:2]), core_out=True, middle=norm_middle, out_types=[block_f32]
    )
    mixed_pair = jnp.concatenate([mixed, mixed_peer], axis=0)

    logits = lax.dot_general(router, mixed_pair, (((1,), (1,)), ((), ())), preferred_element_type=F32)
    router_probs = jax.nn.softmax(logits[:EXPERTS], axis=0)
    shared_scale = jax.nn.sigmoid(logits[EXPERTS:])
    names = jnp.arange(EXPERTS, dtype=jnp.int32)[:, None, None]
    chosen = jnp.any(ids_pair.T[None] == names, axis=1)
    gates = jnp.where(chosen, router_probs, 0.0)

    def gate_rows(first):
        return jnp.pad(lax.dynamic_slice_in_dim(gates, first, 2, 0), ((0, 6), (0, 0)))

    data = (mixed, mixed_peer, cot_rows, cot_peer)
    dw_own_a, dw_oth_a, *rows_a, grad_a = experts_call(*data, gate_rows(first_a), (own_a[0], own_a[1]), (oth_a[0], oth_a[1]))
    shared_rows = jnp.broadcast_to(shared_scale, (8, shared_scale.shape[1]))
    dw_own_s, dw_oth_s, *rows_s, grad_s = experts_call(*data, shared_rows, (own_s[0], own_s[1]), (oth_s[0], oth_s[1]))
    dw_own_b, dw_oth_b, *rows_b, grad_b = experts_call(*data, gate_rows(first_b), (own_b[0], own_b[1]), (oth_b[0], oth_b[1]))

    prob_grad = jnp.zeros_like(router_probs)
    prob_grad = lax.dynamic_update_slice_in_dim(prob_grad, grad_a[:2], first_a, 0)
    prob_grad = lax.dynamic_update_slice_in_dim(prob_grad, grad_b[:2], first_b, 0)
    prob_grad = jnp.where(chosen, prob_grad, 0.0)
    logit_grad = router_probs * (prob_grad - jnp.sum(router_probs * prob_grad, axis=0, keepdims=True))
    scale_logit_grad = (grad_s[0:1] + grad_s[1:2]) * shared_scale * (1.0 - shared_scale)
    small_grad = jnp.concatenate([logit_grad, scale_logit_grad], axis=0)
    high = small_grad.astype(BF16)
    low = (small_grad - high.astype(F32)).astype(BF16)
    small_pair = jnp.concatenate([high, low], axis=0)
    router_both = jnp.dot(small_pair, mixed_pair, preferred_element_type=F32)
    router_grad = router_both[:9] + router_both[9:]
    router_twice = jnp.concatenate([router, router], axis=0)

    def extra(part):
        return lax.dot_general(
            small_pair[:, part * LENGTH : (part + 1) * LENGTH],
            router_twice,
            (((0,), (0,)), ((), ())),
            preferred_element_type=F32,
        )

    def total(index):
        return (
            rows_a[index].astype(F32) + rows_s[index].astype(F32) + rows_b[index].astype(F32)
        )

    normed_two_grad, hidden_grad, branch_grad = rows_call(
        2,
        (total(2) + extra(0)).astype(BF16),
        part_peer=(total(3) + extra(1)).astype(BF16),
        extras=(hidden_rows, cot, gains[1:2]),
        middle=norm_back_middle,
        out_types=[block_f32, block_f32],
    )
    inverse_two = lax.rsqrt(jnp.mean(hidden_rows * hidden_rows, axis=-1, keepdims=True) + EPSILON)
    gain_two_grad = jnp.sum(normed_two_grad * hidden_rows * inverse_two, axis=0)

    mixer_for_peer = after(total(1).astype(BF16), branch_grad)
    mixer = (total(0) + swap_core(mixer_for_peer).astype(F32)).astype(BF16)
    mixer_local = lax.psum_scatter(mixer, "tensor", scatter_dimension=0, tiled=True).astype(F32)
    result = turn_back((hidden_rows + mixer_local).astype(BF16))

    out_grad = jnp.einsum("lf,ld->fd", attended, branch_grad, preferred_element_type=F32).astype(BF16)
    attended_grad = jnp.einsum("ld,fd->lf", branch_grad, out_all, preferred_element_type=F32)
    attended_grad = attended_grad.astype(BF16).reshape(LENGTH, local_heads, HEAD_DIM)
    probs = jnp.exp(attend_scores() - top_score) / row_total
    value_grad = jnp.einsum("hqk,qhd->khd", probs.astype(BF16), attended_grad, preferred_element_type=F32)
    pgrad_rows = jnp.einsum("qhd,khd->hqk", attended_grad, value_rows, preferred_element_type=F32)
    score_grad = (
        probs * (pgrad_rows - jnp.sum(probs * pgrad_rows, axis=-1, keepdims=True))
    ).astype(BF16)
    query_grad = jnp.einsum("hqk,khd->qhd", score_grad, key_rows, preferred_element_type=F32) * scale
    key_grad = jnp.einsum("hqk,qhd->khd", score_grad, query_rows, preferred_element_type=F32) * scale
    project_grad = jnp.stack(
        [
            rotate(query_grad, cos_table, -sin_table).reshape(LENGTH, local_width),
            rotate(key_grad, cos_table, -sin_table).reshape(LENGTH, local_width),
            value_grad.reshape(LENGTH, local_width),
        ]
    ).astype(BF16)
    bias_grad = jnp.sum(project_grad, axis=1, dtype=F32)
    normed_one_grad = jnp.einsum("cle,cde->ld", project_grad, qkv_all, preferred_element_type=F32)
    (input_row_grad,) = rows_call(
        3, normed_one_grad.astype(BF16), gather=False, middle=plain_middle, out_types=[block_f32]
    )
    qkv_grad = jnp.einsum("ld,cle->cde", normed, project_grad, preferred_element_type=F32).astype(BF16)
    scaled_one = input_row_grad * gains[0]
    input_grad = hidden_grad + inverse_one * (
        scaled_one
        - inputs_f
        * inverse_one
        * inverse_one
        * jnp.mean(scaled_one * inputs_f, axis=-1, keepdims=True)
    )
    gain_one_grad = jnp.sum(input_row_grad * inputs_f * inverse_one, axis=0)

    def shard_sum(own, other):
        return reduce_fsdp(own, other, f, 3).astype(BF16)

    sum_a = shard_sum(dw_own_a, dw_oth_a)
    sum_s = shard_sum(dw_own_s, dw_oth_s)
    sum_b = shard_sum(dw_own_b, dw_oth_b)
    from_a, from_s, from_b = swap_x(sum_a), swap_x(sum_s), swap_x(sum_b)

    def add(one, two):
        return (one.astype(F32) + two.astype(F32)).astype(BF16)

    total_b = add(sum_b, from_a)
    total_s = add(sum_s, from_s[::-1])
    total_a = add(sum_a, from_b)
    peer_s, peer_b, peer_a = swap_core(total_s), swap_core(total_b), swap_core(total_a)
    table = routed_table(c, x)
    routed = [total_a, total_b, peer_a, peer_b]
    gate_up_out = jnp.transpose(place_call(routed, table, EXPERTS, (0, 2), F32), (0, 3, 1, 2))
    down_out = place_call(routed, table, EXPERTS, (2, 1), F32).reshape(EXPERTS, hidden, shard)
    table_s = shared_table(c, x)
    shared_up_out = place_call([total_s, peer_s], table_s, 4, (0, 2), BF16)
    shared_up_out = (
        jnp.transpose(shared_up_out, (3, 1, 0, 2)).reshape(shard, 2, 4 * hidden).astype(F32)
    )
    shared_down_out = place_call([total_s, peer_s], table_s, 4, (2, 1), F32).reshape(4 * hidden, shard)

    def dense_sum(grad, hidden_axis, shard_axis):
        keep = lax.dynamic_slice_in_dim(grad, c * half_width, half_width, hidden_axis)
        send = lax.dynamic_slice_in_dim(grad, (1 - c) * half_width, half_width, hidden_axis)
        both = add(keep, swap_core(send))
        own = lax.slice_in_dim(both, 0, shard, axis=shard_axis)
        other = lax.slice_in_dim(both, shard, width, axis=shard_axis)
        part = reduce_fsdp(own, other, f, shard_axis).astype(BF16)
        part = add(part, swap_x(part))
        peer = swap_core(part)
        return jnp.where(
            c == 0,
            jnp.concatenate([part, peer], axis=hidden_axis),
            jnp.concatenate([peer, part], axis=hidden_axis),
        ).astype(F32)

    out_out = dense_sum(out_grad, 0, 1)
    qkv_out = dense_sum(qkv_grad, 2, 1)

    small_sums = jnp.concatenate([router_grad, gain_one_grad[None], gain_two_grad[None]], axis=0)
    small_sums = sum_small(small_sums, f, shard)
    bias_sum = sum_rep(lax.psum(bias_grad, "fsdp") if owners != 2 else bias_grad + swap_y(bias_grad))
    bias_out = lax.dynamic_slice_in_dim(
        bias_sum.reshape(3, local_heads, HEAD_DIM), f * (HEAD_DIM // owners), HEAD_DIM // owners, 2
    )
    return (
        result,
        turn_back(input_grad),
        small_sums[9:],
        qkv_out,
        bias_out,
        out_out,
        small_sums[:EXPERTS].T,
        small_sums[EXPERTS],
        gate_up_out,
        down_out,
        shared_up_out,
        shared_down_out,
    )


def solution(mesh):
    in_specs = (
        P(("rep", "fsdp", "tensor"), None),
        P(("rep", "fsdp", "tensor"), None),
        P(("rep", "fsdp"), None),
        P(("rep", "fsdp"), None),
        P(None, "fsdp"),
        P(None, "fsdp", "tensor"),
        P(None, "tensor", "fsdp"),
        P("tensor", "fsdp"),
        P("fsdp", None),
        P("fsdp"),
        P(None, "fsdp", None, "tensor"),
        P(None, "tensor", "fsdp"),
        P("fsdp", None, "tensor"),
        P("tensor", "fsdp"),
    )
    out_specs = (
        P(("rep", "fsdp", "tensor"), None),
        P(("rep", "fsdp", "tensor"), None),
        P(None, "fsdp"),
        P(None, "fsdp", "tensor"),
        P(None, "tensor", "fsdp"),
        P("tensor", "fsdp"),
        P("fsdp", None),
        P("fsdp"),
        P(None, "fsdp", None, "tensor"),
        P(None, "tensor", "fsdp"),
        P("fsdp", None, "tensor"),
        P("tensor", "fsdp"),
    )
    return jax.shard_map(shards, mesh=mesh, in_specs=in_specs, out_specs=out_specs, check_vma=False)
```

```python
import functools

import jax
import jax.numpy as jnp
from jax import lax
from jax.experimental import pallas as pl
from jax.experimental.pallas import tpu as pltpu
from jax.sharding import PartitionSpec as P

HEAD_DIM = 128
EXPERTS = 8
LENGTH = 640
PIECE = 256
EPSILON = 1e-06
BF16 = jnp.bfloat16
F32 = jnp.float32
COLS = 256
MESH = pl.DeviceIdType.MESH
CHEAP = pl.CostEstimate(flops=1, bytes_accessed=1, transcendentals=0)


def rope_tables(length, head_dim):
    half_dim = head_dim // 2
    frequency = 1000000.0 ** (-jnp.arange(half_dim, dtype=F32) * (2.0 / head_dim))
    angles = jnp.arange(length, dtype=F32)[:, None] * frequency[None, :]
    return (jnp.cos(angles), jnp.sin(angles))


def after(value, *others):
    return lax.optimization_barrier((value,) + others)[0]


def swap_y(a):
    return lax.ppermute(a, "fsdp", [(0, 1), (1, 0)])


def swap_x(a):
    n = lax.axis_size("rep")
    return lax.ppermute(a, "rep", [(i, i ^ 2) for i in range(n)])


def swap_core(a):
    n = lax.axis_size("rep")
    return lax.ppermute(a, "rep", [(i, i ^ 1) for i in range(n)])


CHUNK = 16


def device(axis, index):
    return {axis: index}


def rows_kernel(
    n, rows, part_count, with_core_in, with_thin, with_scatter, with_gather, with_core_out, middle, extra_count, extra_out, bulk_count, *refs
):
    refs = list(refs)
    take = refs.pop
    parts = [take(0) for _ in range(part_count)]
    peer_parts = [take(0) for _ in range(part_count)] if with_core_in else None
    thin, thin_peer, thin_matrix = (take(0), take(0), take(0)) if with_thin else (None, None, None)
    extras = [take(0) for _ in range(extra_count)]
    bulk_src = [take(0) for _ in range(bulk_count)]
    outs = [take(0) for _ in range(extra_out)]
    full = take(0) if with_gather else None
    full_peer = take(0) if with_core_out else None
    bulk_dst = [take(0) for _ in range(bulk_count)]
    chunks = rows // CHUNK
    z = lax.axis_index("tensor")
    r = lax.axis_index("rep")
    core = r + 1 - 2 * lax.rem(r, 2)
    has_left, has_right = z > 0, z < n - 1
    pairs = with_core_in or with_core_out
    if bulk_count:
        bulk_send, bulk_recv = take(0), take(0)
    if with_core_in:
        core_src, core_buf, core_in_send, core_in_recv = take(0), take(0), take(0), take(0)
    if with_scatter:
        in_bufs, out_bufs = (take(0), take(0)), (take(0), take(0))
        sc_send, sc_recv = take(0), take(0)
    if with_gather:
        ga_send, ga_recv = take(0), take(0)
    if with_core_out:
        core_out_send, core_out_recv = take(0), take(0)

    barrier = pltpu.get_barrier_semaphore()

    @pl.when(has_left)
    def _():
        pl.semaphore_signal(barrier, inc=1, device_id=device("tensor", z - 1), device_id_type=MESH)

    @pl.when(has_right)
    def _():
        pl.semaphore_signal(barrier, inc=1, device_id=device("tensor", z + 1), device_id_type=MESH)

    if pairs:
        pl.semaphore_signal(barrier, inc=1, device_id=device("rep", core), device_id_type=MESH)
    across = r + 2 - 4 * (r // 2)
    if bulk_count:
        pl.semaphore_signal(barrier, inc=1, device_id=device("rep", across), device_id_type=MESH)
    greeted = jnp.where(has_left, 1, 0) + jnp.where(has_right, 1, 0) + int(pairs) + int(bulk_count > 0)
    pl.semaphore_wait(barrier, greeted)

    def chunk_at(block, i):
        return pl.ds(pl.multiple_of(block * rows + i * CHUNK, CHUNK), CHUNK)

    def chunk_in(i):
        return pl.ds(pl.multiple_of(i * CHUNK, CHUNK), CHUNK)

    def remote(src, dst, send, recv, axis, index):
        return pltpu.make_async_remote_copy(
            src_ref=src, dst_ref=dst, send_sem=send, recv_sem=recv,
            device_id=device(axis, index), device_id_type=MESH,
        )

    def bulk_copy(k):
        return remote(bulk_src[k], bulk_dst[k], bulk_send.at[k], bulk_recv.at[k], "rep", across)

    for k in range(bulk_count):
        bulk_copy(k).start()

    def core_in_copy(block, i):
        here = chunk_at(block, i)
        return remote(
            core_src.at[here], core_buf.at[here], core_in_send.at[block, i], core_in_recv.at[block, i], "rep", core
        )

    def scatter_copy(way, m, i):
        here = chunk_in(i)
        return remote(
            out_bufs[way].at[m, here], in_bufs[way].at[m, here], sc_send.at[way, m, i], sc_recv.at[way, m, i],
            "tensor", z + 1 - 2 * way,
        )

    def gather_copy(way, k, i):
        here = chunk_at(z - k + 2 * k * way, i)
        return remote(
            full.at[here], full.at[here], ga_send.at[way, k, i], ga_recv.at[way, k, i], "tensor", z + 1 - 2 * way
        )

    def core_out_copy(block, i):
        here = chunk_at(block, i)
        return remote(
            full.at[here], full_peer.at[here], core_out_send.at[block, i], core_out_recv.at[block, i], "rep", core
        )

    def all_chunks(body):
        def step(i, carry):
            body(i)
            return carry

        lax.fori_loop(0, chunks, step, 0)

    def sum_terms(arrays, small, here):
        value = arrays[0][here, :].astype(F32)
        for more in arrays[1:]:
            value = value + more[here, :].astype(F32)
        if with_thin:
            value = value + dot_nn(small[here, :], thin_matrix[...])
        return value

    def core_in_step(i):
        @pl.when(i < chunks)
        def _():
            for block in range(n):
                here = chunk_at(block, i)
                core_src[here, :] = sum_terms(peer_parts, thin_peer, here).astype(BF16)
                core_in_copy(block, i).start()

    ahead = 2
    if with_core_in:
        for i in range(ahead):
            core_in_step(i)

    def term(block, i):
        here = chunk_at(block, i)
        value = sum_terms(parts, thin, here)
        if with_core_in:
            core_in_copy(block, i).wait_recv()
            value = value + core_buf[here, :].astype(F32)
        return value

    def inside(i):
        return (i >= 0) & (i < chunks)

    def scatter_step(way, i, has_source, does_send):
        for m in range(n - 1):
            scatter_message(way, m, i - m, has_source, does_send(n - 1 - m if way == 0 else m))

    def scatter_message(way, m, i, has_source, does_send):
        block = n - 1 - m if way == 0 else m
        here = chunk_in(i)

        @pl.when(inside(i) & does_send)
        def _():
            value = term(block, i)

            @pl.when(has_source)
            def _():
                scatter_copy(way, m, i).wait_recv()
                out_bufs[way][m, here, :] = (value + in_bufs[way][m, here, :].astype(F32)).astype(BF16)

            @pl.when(jnp.logical_not(has_source))
            def _():
                out_bufs[way][m, here, :] = value.astype(BF16)

            scatter_copy(way, m, i).start()

    def own_step(i):
        @pl.when(inside(i))
        def _():
            here = chunk_in(i)
            if with_scatter:
                total[...] = term(z, i)

                @pl.when(has_left)
                def _():
                    m = n - 1 - z
                    scatter_copy(0, m, i).wait_recv()
                    total[...] += in_bufs[0][m, here, :].astype(F32)

                @pl.when(has_right)
                def _():
                    scatter_copy(1, z, i).wait_recv()
                    total[...] += in_bufs[1][z, here, :].astype(F32)

                sent = middle(total[...], here, extras, outs)
            else:
                sent = parts[0][here, :]
            if with_gather:
                full[chunk_at(z, i), :] = sent

                @pl.when(has_right)
                def _():
                    gather_copy(0, 0, i).start()

                @pl.when(has_left)
                def _():
                    gather_copy(1, 0, i).start()

                if with_core_out:
                    core_out_copy(z, i).start()

    def gather_step(k, i):
        for way in range(2):
            comes = z - k >= 0 if way == 0 else z + k <= n - 1
            goes = has_right if way == 0 else has_left

            @pl.when(inside(i) & comes)
            def _():
                landed = full.at[chunk_at(z - k + 2 * k * way, i)]
                remote(
                    landed, landed, ga_send.at[way, k - 1, i], ga_recv.at[way, k - 1, i], "tensor", z + 1 - 2 * way
                ).wait_recv()
                if k < n - 1:

                    @pl.when(goes)
                    def _():
                        gather_copy(way, k, i).start()

                if with_core_out:
                    core_out_copy(z - k + 2 * k * way, i).start()

    lead = n - 1 if with_scatter else 0
    if with_scatter:
        total = take(0)

    def tick(t, carry):
        if with_core_in:
            core_in_step(t + ahead)
        if with_scatter:
            scatter_step(0, t - z, has_left, lambda block: block > z)
            scatter_step(1, t - (n - 1 - z), has_right, lambda block: block < z)
        own_step(t - lead)
        if with_gather:
            for k in range(1, n):
                gather_step(k, t - lead - k)
        return carry

    lax.fori_loop(0, chunks + lead + (n - 1 if with_gather else 0), tick, 0)

    @all_chunks
    def _(i):
        if with_core_in:
            for block in range(n):
                core_in_copy(block, i).wait_send()
        for way in range(2):
            goes = has_right if way == 0 else has_left
            if with_scatter:
                for m in range(n - 1):
                    block = n - 1 - m if way == 0 else m

                    @pl.when(goes & ((block > z) if way == 0 else (block < z)))
                    def _():
                        scatter_copy(way, m, i).wait_send()

            if with_gather:
                for k in range(n - 1):
                    has = z - k >= 0 if way == 0 else z + k <= n - 1

                    @pl.when(goes & has)
                    def _():
                        gather_copy(way, k, i).wait_send()

        if with_core_out:
            for block in range(n):
                core_out_copy(block, i).wait_send()
                core_out_copy(block, i).wait_recv()

    for k in range(bulk_count):
        bulk_copy(k).wait()


def rows_call(
    collective_id, parts, peer_parts=(), thin=(), extras=(), bulk=(), scatter=True, gather=True, core_out=False, middle=None,
    out_types=(),
):
    n = lax.axis_size("tensor")
    width = parts[0].shape[1]
    rows = parts[0].shape[0] // n if scatter else parts[0].shape[0]
    chunks = rows // CHUNK
    vmem_spec = pl.BlockSpec(memory_space=pltpu.VMEM)
    full = jax.ShapeDtypeStruct((n * rows, width), BF16)
    out_shape = list(out_types) + ([full] if gather else []) + ([full] if core_out else [])
    vmem_outs = len(out_shape)
    out_shape += [jax.ShapeDtypeStruct(a.shape, a.dtype) for a in bulk]
    any_spec = pl.BlockSpec(memory_space=pl.ANY)
    scratch = [pltpu.SemaphoreType.DMA((len(bulk),))] * 2 if bulk else []
    if peer_parts:
        scratch += [pltpu.VMEM((n * rows, width), BF16)] * 2 + [pltpu.SemaphoreType.DMA((n, chunks))] * 2
    if scatter:
        scratch += [pltpu.VMEM((n - 1, rows, width), BF16)] * 4
        scratch += [pltpu.SemaphoreType.DMA((2, n - 1, chunks))] * 2
    if gather:
        scratch += [pltpu.SemaphoreType.DMA((2, n - 1, chunks))] * 2
    if core_out:
        scratch += [pltpu.SemaphoreType.DMA((n, chunks))] * 2
    if scatter:
        scratch += [pltpu.VMEM((CHUNK, width), F32)]
    operands = [*parts, *peer_parts, *thin, *extras]
    vmem_ins = len(operands)
    operands += list(bulk)
    return pl.pallas_call(
        functools.partial(
            rows_kernel, n, rows, len(parts), bool(peer_parts), bool(thin), scatter, gather, core_out, middle, len(extras), len(out_types), len(bulk)
        ),
        out_shape=out_shape,
        in_specs=[vmem_spec] * vmem_ins + [any_spec] * len(bulk),
        out_specs=[vmem_spec] * vmem_outs + [any_spec] * len(bulk),
        scratch_shapes=scratch,
        compiler_params=pltpu.CompilerParams(
            collective_id=collective_id, has_side_effects=True, vmem_limit_bytes=56 * 2**20
        ),
        cost_estimate=CHEAP,
        name="rows",
    )(*operands)


def norm_middle(total, here, extras, outs):
    inputs, gain = extras
    hidden = inputs[here, :].astype(F32) + total
    outs[0][here, :] = hidden
    inverse = lax.rsqrt(jnp.mean(hidden * hidden, axis=-1, keepdims=True) + EPSILON)
    return (hidden * inverse * gain[...]).astype(BF16)


def norm_back_middle(total, here, extras, outs):
    hidden_ref, cot, gain = extras
    hidden = hidden_ref[here, :]
    inverse = lax.rsqrt(jnp.mean(hidden * hidden, axis=-1, keepdims=True) + EPSILON)
    scaled = total * gain[...]
    grad = cot[here, :].astype(F32) + inverse * (
        scaled - hidden * inverse * inverse * jnp.mean(scaled * hidden, axis=-1, keepdims=True)
    )
    outs[0][here, :] = total
    outs[1][here, :] = grad
    return grad.astype(BF16)


def plain_middle(total, here, extras, outs):
    outs[0][here, :] = total


def others_of(own, f, axis):
    if lax.axis_size("fsdp") == 2:
        return swap_y(own)
    whole = lax.all_gather(own, "fsdp", axis=axis, tiled=True)
    size = own.shape[axis]
    turned = jnp.roll(whole, -f * size, axis=axis)
    return lax.slice_in_dim(turned, size, whole.shape[axis], axis=axis)


def reduce_fsdp(own, other, f, axis, add):
    if lax.axis_size("fsdp") == 2:
        return add(own, swap_y(other))
    whole = jnp.roll(jnp.concatenate([own, other], axis=axis), f * own.shape[axis], axis=axis)
    return lax.psum_scatter(whole, "fsdp", scatter_dimension=axis, tiled=True)


def sum_small(values, per_tensor, f, shard):
    total = sum_rep_first(jnp.concatenate([sum_tensor(values), per_tensor], axis=0))
    if lax.axis_size("fsdp") == 2:
        total = total[:, :shard] + swap_y(total[:, shard:])
    else:
        whole = jnp.roll(total, f * shard, axis=1)
        total = lax.psum_scatter(whole, "fsdp", scatter_dimension=1, tiled=True)
    return total


def sum_rep_first(total):
    return total + swap_core(total)


def sum_tensor(total):
    n = lax.axis_size("tensor")
    step = 1
    while step < n:
        total = total + lax.ppermute(total, "tensor", [(i, i ^ step) for i in range(n)])
        step *= 2
    return total


def dot_nt(a, b):
    return lax.dot_general(a, b, (((1,), (1,)), ((), ())), preferred_element_type=F32)


def dot_nn(a, b):
    return lax.dot_general(a, b, (((1,), (0,)), ((), ())), preferred_element_type=F32)


def mask_rows(starts, length):
    key = lax.broadcasted_iota(jnp.int32, (length, length), 0)
    query = lax.broadcasted_iota(jnp.int32, (length, length), 1)
    visible = key <= query
    for piece in range(2):
        first = starts[0, piece]
        visible |= (jnp.minimum(key, query) >= first) & (jnp.maximum(key, query) < first + PIECE)
    return jnp.where(visible, 0.0, -1e30).astype(F32)


def attend_kernel(
    heads, own_width, starts, rows, w_own, w_oth, bias, cos, sin, out_own, out_oth,
    q_out, k_out, v_out, attended, stats, part, mask,
):
    length = rows.shape[0]
    scale = HEAD_DIM ** (-0.5)
    for c, out in ((0, q_out), (1, k_out), (2, v_out)):
        project = dot_nn(rows[:, :own_width], w_own[c]) + dot_nn(rows[:, own_width:], w_oth[c]) + bias[c : c + 1, :]
        for h in range(heads):
            here = slice(h * HEAD_DIM, (h + 1) * HEAD_DIM)
            values = project[:, here]
            if c < 2:
                values = values * cos[...] + pltpu.roll(values, HEAD_DIM // 2, 1) * sin[...]
            out[:, here] = values.astype(BF16)
    mask[...] = mask_rows(starts, length)

    def one_head(h, carry):
        here = pl.ds(pl.multiple_of(h * HEAD_DIM, HEAD_DIM), HEAD_DIM)
        scores = dot_nt(k_out[:, here], q_out[:, here]) * scale + mask[...]
        top = jnp.max(scores, axis=0, keepdims=True)
        weights = jnp.exp(scores - top)
        inverse = 1.0 / jnp.sum(weights, axis=0, keepdims=True)
        probs = (weights * inverse).astype(BF16)
        attended[:, here] = dot_nn(v_out[:, here].T, probs).T.astype(BF16)
        stats[pl.ds(h, 1), :] = top
        stats[pl.ds(heads + h, 1), :] = inverse
        return carry

    lax.fori_loop(0, heads, one_head, 0)
    part[:, :own_width] = dot_nn(attended[...], out_own[...]).astype(BF16)
    part[:, own_width:] = dot_nn(attended[...], out_oth[...]).astype(BF16)


def attend_back_kernel(
    heads, own_width, starts, grad, w_own, w_oth, cos, sin, out_own, out_oth, q, k, v, stats,
    project_grad, bias_grad, rows_grad, mask, attended_grad,
):
    length = grad.shape[0]
    scale = HEAD_DIM ** (-0.5)
    attended_grad[...] = (
        dot_nt(grad[:, :own_width], out_own[...]) + dot_nt(grad[:, own_width:], out_oth[...])
    ).astype(BF16)
    mask[...] = mask_rows(starts, length)

    def turn_back(values):
        return values * cos[...] - pltpu.roll(values, HEAD_DIM // 2, 1) * sin[...]

    def one_head(h, carry):
        here = pl.ds(pl.multiple_of(h * HEAD_DIM, HEAD_DIM), HEAD_DIM)
        queries, keys, grads = q[:, here], k[:, here], attended_grad[:, here]
        scores = dot_nt(keys, queries) * scale + mask[...]
        probs = jnp.exp(scores - stats[pl.ds(h, 1), :]) * stats[pl.ds(heads + h, 1), :]
        value_grad = dot_nn(probs.astype(BF16), grads)
        probs_grad = dot_nt(v[:, here], grads)
        mean = jnp.sum(probs * probs_grad, axis=0, keepdims=True)
        score_grad = (probs * (probs_grad - mean)).astype(BF16)
        key_grad = dot_nn(score_grad, queries) * scale
        query_grad = dot_nn(score_grad.T, keys) * scale
        project_grad[0, :, here] = turn_back(query_grad).astype(BF16)
        project_grad[1, :, here] = turn_back(key_grad).astype(BF16)
        project_grad[2, :, here] = value_grad.astype(BF16)
        return carry

    lax.fori_loop(0, heads, one_head, 0)
    total_own = total_oth = None
    for c in range(3):
        grads = project_grad[c]
        bias_grad[c : c + 1, :] = jnp.sum(grads.astype(F32), axis=0, keepdims=True)
        own, oth = dot_nt(grads, w_own[c]), dot_nt(grads, w_oth[c])
        total_own = own if c == 0 else total_own + own
        total_oth = oth if c == 0 else total_oth + oth
    rows_grad[:, :own_width] = total_own.astype(BF16)
    rows_grad[:, own_width:] = total_oth.astype(BF16)


def attention_call(kernel, name, operands, out_shape, heads, own_width, length, more_scratch=()):
    vmem_spec = pl.BlockSpec(memory_space=pltpu.VMEM)
    return pl.pallas_call(
        functools.partial(kernel, heads, own_width),
        out_shape=out_shape,
        in_specs=[pl.BlockSpec(memory_space=pltpu.SMEM)] + [vmem_spec] * (len(operands) - 1),
        out_specs=[vmem_spec] * len(out_shape),
        scratch_shapes=[pltpu.VMEM((length, length), F32), *more_scratch],
        cost_estimate=CHEAP,
        compiler_params=pltpu.CompilerParams(vmem_limit_bytes=56 * 2**20),
        name=name,
    )(*operands)


def experts_kernel(rows, width, own_width, hidden, direct, *refs):
    if direct:
        first, x0, x1, c0, c1, gate, gate_up, down, w_oth, *refs = refs
    else:
        x0, x1, c0, c1, gate, w_own, w_oth, *refs = refs
    dw_own, dw_oth, mix0, mix1, ng0, ng1, gate_grad, *refs = refs
    xv, cv, wgu, wd, ga, pre, ga_t, pre_t, st_mix, st_ng, st_dw, w_sem, x_sem, c_sem, out_sem, dw_sem = refs
    seq = rows // 2
    both = 2 * hidden
    oth_width = width - own_width

    def w_copies(part):
        copies = []
        for k in range(2):
            if direct:
                own = gate_up.at[first[0] + k, part] if part < 2 else down.at[first[0] + k]
            else:
                own = w_own.at[k, part]
            to = wd.at[pl.ds(k * hidden, hidden)] if part == 2 else wgu.at[pl.ds(part * both + k * hidden, hidden)]
            copies.append(pltpu.make_async_copy(own, to.at[:, pl.ds(0, own_width)], w_sem.at[part, k, 0]))
            copies.append(
                pltpu.make_async_copy(w_oth.at[k, part], to.at[:, pl.ds(own_width, oth_width)], w_sem.at[part, k, 1])
            )
        return copies

    def row_copies(sources, to, sem):
        return [
            pltpu.make_async_copy(sources[s], to.at[pl.ds(s * seq, seq)], sem.at[s]) for s in range(2)
        ]

    x_copies, c_copies = row_copies((x0, x1), xv, x_sem), row_copies((c0, c1), cv, c_sem)
    order = [x_copies[0], *w_copies(0), *w_copies(1), c_copies[0], *w_copies(2), x_copies[1], c_copies[1]]
    for copy in order:
        copy.start()
    for copy in order[:-2]:
        copy.wait()

    def token_tile(t, carry):
        @pl.when(t == seq // COLS)
        def _():
            x_copies[1].wait()
            c_copies[1].wait()

        here = pl.ds(pl.multiple_of(t * COLS, COLS), COLS)
        gu = dot_nt(wgu[...], xv[here, :])
        h = dot_nt(wd[...], cv[here, :])
        g, u = gu[:both], gu[both:]
        sig = jax.nn.sigmoid(g)
        act = g * sig * u
        product = act * h
        scale_rows = []
        for k in range(2):
            part = product[k * hidden : (k + 1) * hidden]
            gate_grad[pl.ds(k, 1), here] = jnp.sum(part, axis=0, keepdims=True)
            scale_rows.append(jnp.broadcast_to(gate[pl.ds(k, 1), here], (hidden, COLS)))
        scale = jnp.concatenate(scale_rows, axis=0)
        back = scale * h
        ga_here = (scale * act).astype(BF16)
        pg_here = (back * u * sig * (1.0 + g * (1.0 - sig))).astype(BF16)
        pu_here = (back * g * sig).astype(BF16)
        ga[:, here] = ga_here
        pre[:both, here] = pg_here
        pre[both:, here] = pu_here
        ga_t[here, :] = ga_here.T
        pre_t[here, :both] = pg_here.T
        pre_t[here, both:] = pu_here.T
        return carry

    lax.fori_loop(0, rows // COLS, token_tile, 0)

    def row_outs(slot, cols):
        return [
            pltpu.make_async_copy(stage.at[slot, pl.ds(s * seq, seq)], outs[s].at[:, cols], out_sem.at[slot, i, s])
            for i, (stage, outs) in enumerate(((st_mix, (mix0, mix1)), (st_ng, (ng0, ng1))))
            for s in range(2)
        ]

    def weight_outs(slot, dst, cols):
        return [
            pltpu.make_async_copy(
                st_dw.at[slot, pl.ds((part * 2 + k) * hidden, hidden)], dst.at[k, part, :, cols], dw_sem.at[slot, part, k]
            )
            for part in range(3)
            for k in range(2)
        ]

    def wait_slot(slot):
        for copy in row_outs(slot, pl.ds(0, COLS)) + weight_outs(slot, dw_own, pl.ds(0, COLS)):
            copy.wait()

    def column_tile(n, slot, src_col, dst, dst_col):
        cols = pl.ds(pl.multiple_of(src_col, COLS), COLS)

        @pl.when(n >= 2)
        def _():
            wait_slot(slot)

        st_dw[slot, : 2 * both] = dot_nn(pre[...], xv[:, cols]).astype(BF16)
        st_dw[slot, 2 * both :] = dot_nn(ga[...], cv[:, cols]).astype(BF16)
        for copy in weight_outs(slot, dst, pl.ds(pl.multiple_of(dst_col, COLS), COLS)):
            copy.start()
        st_ng[slot] = dot_nn(pre_t[...], wgu[:, cols]).astype(BF16)
        st_mix[slot] = dot_nn(ga_t[...], wd[:, cols]).astype(BF16)
        for copy in row_outs(slot, cols):
            copy.start()

    oth_tiles, own_tiles = oth_width // COLS, own_width // COLS

    def oth_tile(n, carry):
        column_tile(n, lax.rem(n, 2), own_width + n * COLS, dw_oth, n * COLS)
        return carry

    def own_tile(n, carry):
        column_tile(n + oth_tiles, lax.rem(n + oth_tiles, 2), n * COLS, dw_own, n * COLS)
        return carry

    lax.fori_loop(0, oth_tiles, oth_tile, 0)
    lax.fori_loop(0, own_tiles, own_tile, 0)
    for slot in range(2):
        wait_slot(slot)


def experts_call(x0, x1, c0, c1, gate, w_own, w_oth):
    direct = isinstance(w_own, tuple)
    seq, width = x0.shape
    rows = 2 * seq
    hidden, own_width = (w_own[1] if direct else w_own).shape[2:]
    smem_spec = pl.BlockSpec(memory_space=pltpu.SMEM)
    own_operands = w_own[1:] if direct else (w_own,)
    any_spec = pl.BlockSpec(memory_space=pl.ANY)
    vmem_spec = pl.BlockSpec(memory_space=pltpu.VMEM)
    out_rows = jax.ShapeDtypeStruct((seq, width), BF16)
    return pl.pallas_call(
        functools.partial(experts_kernel, rows, width, own_width, hidden, direct),
        out_shape=[
            jax.ShapeDtypeStruct((2, 3, hidden, own_width), BF16),
            jax.ShapeDtypeStruct((2, 3, hidden, width - own_width), BF16),
            out_rows, out_rows, out_rows, out_rows,
            jax.ShapeDtypeStruct((8, rows), F32),
        ],
        in_specs=[smem_spec] * direct + [any_spec] * 4 + [vmem_spec] + [any_spec] * (len(own_operands) + 1),
        out_specs=[any_spec] * 6 + [vmem_spec],
        scratch_shapes=[
            pltpu.VMEM((rows, width), BF16),
            pltpu.VMEM((rows, width), BF16),
            pltpu.VMEM((4 * hidden, width), BF16),
            pltpu.VMEM((2 * hidden, width), BF16),
            pltpu.VMEM((2 * hidden, rows), BF16),
            pltpu.VMEM((4 * hidden, rows), BF16),
            pltpu.VMEM((rows, 2 * hidden), BF16),
            pltpu.VMEM((rows, 4 * hidden), BF16),
            pltpu.VMEM((2, rows, COLS), BF16),
            pltpu.VMEM((2, rows, COLS), BF16),
            pltpu.VMEM((2, 6 * hidden, COLS), BF16),
            pltpu.SemaphoreType.DMA((3, 2, 2)),
            pltpu.SemaphoreType.DMA((2,)),
            pltpu.SemaphoreType.DMA((2,)),
            pltpu.SemaphoreType.DMA((2, 2, 2)),
            pltpu.SemaphoreType.DMA((2, 3, 2)),
        ],
        cost_estimate=CHEAP,
        compiler_params=pltpu.CompilerParams(vmem_limit_bytes=58 * 2**20),
        name="experts",
    )(*([w_own[0]] if direct else []), x0, x1, c0, c1, gate, *own_operands, w_oth)


def sum_kernel(*refs):
    total = refs[0][...].astype(F32)
    for ref in refs[1:-1]:
        total = total + ref[...].astype(F32)
    refs[-1][...] = total.astype(BF16)


def sum_call(arrays, steps, flip=-1):
    rows, columns = arrays[0].shape
    block = (rows // steps, columns)

    def spec(k):
        if k == flip:
            return pl.BlockSpec(block, lambda i: (lax.rem(i + steps // 2, steps), 0))
        return pl.BlockSpec(block, lambda i: (i, 0))

    return pl.pallas_call(
        sum_kernel,
        out_shape=jax.ShapeDtypeStruct((rows, columns), BF16),
        grid=(steps,),
        in_specs=[spec(k) for k in range(len(arrays))],
        out_specs=spec(-2),
        cost_estimate=CHEAP,
        compiler_params=pltpu.CompilerParams(vmem_limit_bytes=40 * 2**20),
        name="sums",
    )(*arrays)


def add_experts(one, two, flip=False):
    flat = [a.reshape(-1, a.shape[-1]) for a in (one, two)]
    return sum_call(flat, 4, 1 if flip else -1).reshape(one.shape)


def dense_kernel(half, own_width, core, rows, project_grad, attended, branch_grad, *outs):
    qkv_own, qkv_oth, qkv_send, out_own, out_oth, out_send, rows_t = outs
    rows_t[...] = rows[...].T
    for keep in (False, True):
        cols = pl.ds(pl.multiple_of((core[0] if keep else 1 - core[0]) * half, half), half)
        for c in range(3):
            grad = dot_nn(rows_t[...], project_grad[c, :, cols]).astype(BF16)
            if keep:
                qkv_own[c] = grad[:own_width]
                qkv_oth[c] = grad[own_width:]
            else:
                qkv_send[c] = grad
        grad = dot_nn(attended[:, cols].T, branch_grad[...]).astype(BF16)
        if keep:
            out_own[...] = grad[:, :own_width]
            out_oth[...] = grad[:, own_width:]
        else:
            out_send[...] = grad


def dense_call(core, rows, project_grad, attended, branch_grad, own_width):
    length, width = rows.shape
    half = attended.shape[1] // 2
    vmem_spec = pl.BlockSpec(memory_space=pltpu.VMEM)
    shapes = [(3, own_width, half), (3, width - own_width, half), (3, width, half)]
    shapes += [(half, own_width), (half, width - own_width), (half, width)]
    return pl.pallas_call(
        functools.partial(dense_kernel, half, own_width),
        out_shape=[jax.ShapeDtypeStruct(shape, BF16) for shape in shapes],
        in_specs=[pl.BlockSpec(memory_space=pltpu.SMEM)] + [vmem_spec] * 4,
        out_specs=[vmem_spec] * 6,
        scratch_shapes=[pltpu.VMEM((width, length), BF16)],
        cost_estimate=CHEAP,
        compiler_params=pltpu.CompilerParams(vmem_limit_bytes=48 * 2**20),
        name="dense_grads",
    )(core, rows, project_grad, attended, branch_grad)


def place_kernel(table, mine, peer, *refs):
    out = refs[-1]
    which = table[1, pl.program_id(0)]

    @pl.when(which == 0)
    def _():
        out[...] = mine[...].astype(F32)

    @pl.when(which == 1)
    def _():
        out[...] = peer[...].astype(F32)


def place_call(mine, peer, c, first, parts, base=None):
    at, length = parts
    hidden, width = mine.shape[2:]
    half = EXPERTS // 2
    step = jnp.arange(4, dtype=jnp.int32)
    which = (step // 2 != c).astype(jnp.int32)

    def blocks(own_half):
        return jnp.clip(step - 2 * own_half, 0, 1)

    table = jnp.stack([step // 2 * half + first + step % 2, which, blocks(c), blocks(1 - c)]).astype(jnp.int32)

    def source(row):
        return pl.BlockSpec((1, length, hidden, width), lambda e, tab: (tab[row, e], at // length, 0, 0))

    return pl.pallas_call(
        place_kernel,
        out_shape=jax.ShapeDtypeStruct((EXPERTS, length, hidden, width), F32),
        grid_spec=pltpu.PrefetchScalarGridSpec(
            num_scalar_prefetch=1,
            grid=(4,),
            in_specs=[source(2), source(3)] + [pl.BlockSpec(memory_space=pl.ANY)] * (base is not None),
            out_specs=pl.BlockSpec((1, length, hidden, width), lambda e, tab: (tab[0, e], 0, 0, 0)),
        ),
        input_output_aliases={} if base is None else {3: 0},
        cost_estimate=CHEAP,
        compiler_params=pltpu.CompilerParams(vmem_limit_bytes=40 * 2**20),
        name="place",
    )(table, mine, peer, *([] if base is None else [base]))


def shared_kernel(table, mine, peer, up, down):
    def quarter(q, part):
        block = table[q]
        return jnp.where(table[4 + q] == 0, mine[block, part].astype(F32), peer[block, part].astype(F32))

    for part in range(2):
        up[:, part, :] = jnp.concatenate([quarter(q, part) for q in range(4)], axis=0).T
    down[...] = jnp.concatenate([quarter(q, 2) for q in range(4)], axis=0)


def shared_call(mine, peer, c, x):
    hidden, width = mine.shape[2:]
    q = jnp.arange(4, dtype=jnp.int32)
    table = jnp.concatenate([(q % 2) ^ x, (q // 2 != c).astype(jnp.int32)]).astype(jnp.int32)
    source = pl.BlockSpec((2, 3, hidden, 128), lambda n, tab: (0, 0, 0, n))
    return pl.pallas_call(
        shared_kernel,
        out_shape=[
            jax.ShapeDtypeStruct((width, 2, 4 * hidden), F32),
            jax.ShapeDtypeStruct((4 * hidden, width), F32),
        ],
        grid_spec=pltpu.PrefetchScalarGridSpec(
            num_scalar_prefetch=1,
            grid=(width // 128,),
            in_specs=[source, source],
            out_specs=[
                pl.BlockSpec((128, 2, 4 * hidden), lambda n, tab: (n, 0, 0)),
                pl.BlockSpec((4 * hidden, 128), lambda n, tab: (0, n)),
            ],
        ),
        cost_estimate=CHEAP,
        compiler_params=pltpu.CompilerParams(vmem_limit_bytes=40 * 2**20),
        name="shared",
    )(table, mine, peer)


def shards(
    block_input,
    cotangent,
    piece_starts,
    expert_ids,
    norm_gains,
    qkv_weight,
    qkv_bias,
    out_weight,
    router_weight,
    shared_gate,
    expert_gate_up,
    expert_down,
    shared_gate_up,
    shared_down,
):
    f = lax.axis_index("fsdp")
    owners = lax.axis_size("fsdp")
    r = lax.axis_index("rep")
    c, x = r % 2, r // 2
    shard = norm_gains.shape[1]
    width = owners * shard
    local_width = qkv_weight.shape[2]
    local_heads = local_width // HEAD_DIM
    half_width = local_width // 2
    hidden = expert_gate_up.shape[3]
    scale = HEAD_DIM ** (-0.5)

    def turn(rows):
        return jnp.roll(rows, -f * shard, axis=1)

    def turn_back(rows):
        return jnp.roll(rows, f * shard, axis=1)

    small = jnp.concatenate(
        [norm_gains.reshape(-1), router_weight.T.reshape(-1), shared_gate, qkv_bias.reshape(-1)]
    )
    small_all = jnp.concatenate([small[None], others_of(small[None], f, 0)], axis=0)
    gains = jnp.swapaxes(small_all[:, : 2 * shard].reshape(owners, 2, shard), 0, 1).reshape(2, width)
    gains = gains.astype(F32)
    router = jnp.swapaxes(
        small_all[:, 2 * shard : 11 * shard].reshape(owners, 9, shard), 0, 1
    ).reshape(9, width)
    bias = jnp.roll(small_all[:, 11 * shard :], f, axis=0).reshape(owners, 3, local_heads, -1)
    bias = jnp.moveaxis(bias, 0, 2).reshape(3, local_width).astype(F32)
    cos_table, sin_table = rope_tables(LENGTH, HEAD_DIM)
    inputs = turn(block_input)
    inputs_f = inputs.astype(F32)
    cot = turn(cotangent)
    inverse_one = lax.rsqrt(jnp.mean(inputs_f * inputs_f, axis=-1, keepdims=True) + EPSILON)
    normed_local = (inputs_f * inverse_one * gains[0]).astype(BF16)
    normed = lax.all_gather(normed_local, "tensor", axis=0, tiled=True)
    gate_up_t = jnp.transpose(after(expert_gate_up, normed_local), (0, 2, 3, 1))

    quarter = local_width // 4

    def fetch_quarters(weight, hidden_axis, shard_axis):
        mine = lax.dynamic_slice_in_dim(weight, r * quarter, quarter, hidden_axis)
        got = others_of(mine, f, shard_axis)
        pair = jnp.stack([got, swap_x(got)])
        peers = swap_core(pair)
        pair = jnp.where(x == 0, pair, pair[::-1])
        peers = jnp.where(x == 0, peers, peers[::-1])
        order = jnp.where(c == 0, jnp.stack([pair, peers], 1), jnp.stack([peers, pair], 1))
        return jnp.concatenate([order[i, j] for i in range(2) for j in range(2)], axis=hidden_axis), got

    qkv_oth, qkv_got = fetch_quarters(qkv_weight, 2, 1)
    out_oth, out_got = fetch_quarters(out_weight, 0, 1)


    def routed_chunk(first, gate_up_t):
        return jnp.concatenate(
            [
                lax.dynamic_slice_in_dim(gate_up_t, first, 2, 0),
                lax.dynamic_slice_in_dim(expert_down, first, 2, 0)[:, None],
            ],
            axis=1,
        )

    def shared_chunk(q, shared_up_t, shared_down):
        return jnp.concatenate(
            [
                lax.dynamic_slice_in_dim(shared_up_t, q * hidden, hidden, 1),
                lax.dynamic_slice_in_dim(shared_down, q * hidden, hidden, 0)[None],
            ],
            axis=0,
        )[None]

    first_a, first_b = 4 * c + 2 * x, 4 * c + 2 * (1 - x)
    shared_gate_up, shared_down, expert_ids = lax.optimization_barrier(
        (shared_gate_up, shared_down, expert_ids, normed_local)
    )[:3]
    ids_pair = jnp.concatenate([expert_ids, swap_core(expert_ids)], axis=0)
    shared_up_t = jnp.stack([shared_gate_up[:, 0].T, shared_gate_up[:, 1].T])
    own_s = jnp.concatenate([shared_chunk(q, shared_up_t, shared_down) for q in (2 * c + x, 2 * c + 1 - x)], axis=0)
    own_a = routed_chunk(first_a, after(gate_up_t, own_s))
    own_b = (jnp.reshape(first_b, (1,)).astype(jnp.int32), gate_up_t, expert_down)

    oth_a = others_of(after(own_a, qkv_got, out_got), f, 3)
    cos_rows = jnp.concatenate([cos_table, cos_table], axis=1)
    sin_rows = jnp.concatenate([-sin_table, sin_table], axis=1)
    normed = after(normed, own_s, ids_pair, cos_rows, sin_rows, bias, qkv_oth, out_oth)
    cot_rows = lax.all_gather(after(cot, normed), "tensor", axis=0, tiled=True)
    oth_s = others_of(after(own_s, normed), f, 3)

    heads_rows = jax.ShapeDtypeStruct((LENGTH, local_width), BF16)
    all_rows = jax.ShapeDtypeStruct((LENGTH, width), BF16)
    query_rows, key_rows, value_rows, attended, stats, heads_part = attention_call(
        attend_kernel,
        "attend",
        [piece_starts, normed, qkv_weight, qkv_oth, bias, cos_rows, sin_rows, out_weight, out_oth],
        [heads_rows] * 4 + [jax.ShapeDtypeStruct((2 * local_heads, LENGTH), F32), all_rows],
        local_heads,
        shard,
        LENGTH,
    )
    block_f32 = jax.ShapeDtypeStruct(inputs.shape, F32)
    hidden_rows, mixed, mixed_peer = rows_call(
        1, [heads_part], extras=(inputs, gains[1:2]), core_out=True, middle=norm_middle, out_types=[block_f32]
    )
    cot_rows = after(cot_rows, mixed)
    cot_peer = swap_core(cot_rows)
    oth_b = swap_x(after(oth_a, mixed))
    mixed_pair = jnp.concatenate([mixed, mixed_peer], axis=0)

    logits = lax.dot_general(router, mixed_pair, (((1,), (1,)), ((), ())), preferred_element_type=F32)
    router_probs = jax.nn.softmax(logits[:EXPERTS], axis=0)
    shared_scale = jax.nn.sigmoid(logits[EXPERTS:])
    names = jnp.arange(EXPERTS, dtype=jnp.int32)[:, None, None]
    chosen = jnp.any(ids_pair.T[None] == names, axis=1)
    gates = jnp.where(chosen, router_probs, 0.0)

    def gate_rows(first):
        return jnp.pad(lax.dynamic_slice_in_dim(gates, first, 2, 0), ((0, 6), (0, 0)))

    data = (mixed, mixed_peer, cot_rows, cot_peer)
    dw_own_a, dw_oth_a, *rows_a, grad_a = experts_call(*data, gate_rows(first_a), own_a, oth_a)
    shared_rows = after(jnp.broadcast_to(shared_scale, (8, shared_scale.shape[1])), grad_a)
    dw_own_s, dw_oth_s, *rows_s, grad_s = experts_call(*data, shared_rows, own_s, oth_s)
    dw_own_b, dw_oth_b, *rows_b, grad_b = experts_call(
        *data, after(gate_rows(first_b), grad_s), own_b, oth_b
    )

    prob_grad = jnp.zeros_like(router_probs)
    prob_grad = lax.dynamic_update_slice_in_dim(prob_grad, grad_a[:2], first_a, 0)
    prob_grad = lax.dynamic_update_slice_in_dim(prob_grad, grad_b[:2], first_b, 0)
    prob_grad = jnp.where(chosen, prob_grad, 0.0)
    logit_grad = router_probs * (prob_grad - jnp.sum(router_probs * prob_grad, axis=0, keepdims=True))
    scale_logit_grad = (grad_s[0:1] + grad_s[1:2]) * shared_scale * (1.0 - shared_scale)
    small_grad = jnp.concatenate([logit_grad, scale_logit_grad], axis=0)
    high = small_grad.astype(BF16)
    low = (small_grad - high.astype(F32)).astype(BF16)
    small_pair = jnp.concatenate([high, low], axis=0)
    router_both = jnp.dot(small_pair, mixed_pair, preferred_element_type=F32)
    router_grad = router_both[:9] + router_both[9:]
    thin = jnp.pad(small_pair, ((0, 128 - small_pair.shape[0]), (0, 0))).T
    thin_matrix = jnp.pad(jnp.concatenate([router, router], axis=0), ((0, 128 - small_pair.shape[0]), (0, 0)))

    def add(one, two):
        return (one.astype(F32) + two.astype(F32)).astype(BF16)

    def shard_sum(own, other):
        return reduce_fsdp(own, other, f, 3, add_experts)

    sum_a = shard_sum(dw_own_a, dw_oth_a)
    from_a = swap_x(sum_a)
    normed_two_grad, hidden_grad, branch_grad = rows_call(
        2,
        [after(rows_a[2], sum_a), rows_s[2], rows_b[2]],
        [rows_a[3], rows_s[3], rows_b[3]],
        [thin[:LENGTH], thin[LENGTH:], thin_matrix],
        extras=(hidden_rows, cot, gains[1:2]),
        middle=norm_back_middle,
        out_types=[block_f32, block_f32],
    )
    inverse_two = lax.rsqrt(jnp.mean(hidden_rows * hidden_rows, axis=-1, keepdims=True) + EPSILON)
    gain_two_grad = jnp.sum(normed_two_grad * hidden_rows * inverse_two, axis=0)

    sum_s = shard_sum(after(dw_own_s, branch_grad), dw_oth_s)
    branch_grad = after(branch_grad, sum_s)
    from_s = swap_x(sum_s)
    project_grad, bias_grad, normed_one_grad = attention_call(
        attend_back_kernel,
        "attend_back",
        [
            piece_starts, branch_grad, qkv_weight, qkv_oth, cos_rows, sin_rows, out_weight, out_oth,
            query_rows, key_rows, value_rows, stats,
        ],
        [
            jax.ShapeDtypeStruct((3, LENGTH, local_width), BF16),
            jax.ShapeDtypeStruct((3, local_width), F32),
            all_rows,
        ],
        local_heads,
        shard,
        LENGTH,
        [pltpu.VMEM((LENGTH, local_width), BF16)],
    )
    (input_row_grad,) = rows_call(
        3, [after(normed_one_grad, from_a)], gather=False, middle=plain_middle, out_types=[block_f32]
    )
    out_grad = jnp.einsum("lf,ld->fd", attended, branch_grad, preferred_element_type=F32).astype(BF16)
    sum_b = shard_sum(after(dw_own_b, input_row_grad), dw_oth_b)
    from_b = swap_x(sum_b)
    total_b = add_experts(sum_b, from_a)
    peer_b = swap_core(total_b)
    input_row_grad, project_grad, attended, branch_grad = lax.optimization_barrier(
        (input_row_grad, project_grad, attended, branch_grad, sum_b)
    )[:4]
    qkv_own, qkv_more, qkv_send, out_own, out_more, out_send = dense_call(
        jnp.reshape(c, (1,)).astype(jnp.int32), normed, project_grad, attended, branch_grad, shard
    )

    qkv_peer, out_peer = swap_core(qkv_send), swap_core(out_send)
    total_s = add_experts(after(sum_s, qkv_send, total_b), from_s, flip=True)
    peer_s = swap_core(total_s)

    def fsdp_part(own, more, peer, shard_axis):
        own, more, peer = lax.optimization_barrier((own, more, peer, total_s))[:3]
        more = add(more, lax.slice_in_dim(peer, shard, width, axis=shard_axis))
        own = add(own, lax.slice_in_dim(peer, 0, shard, axis=shard_axis))
        return reduce_fsdp(own, more, f, shard_axis, add), more

    (qkv_part, qkv_both), (out_part, out_both) = (
        fsdp_part(qkv_own, qkv_more, qkv_peer, 1),
        fsdp_part(out_own, out_more, out_peer, 1),
    )

    input_row_grad = after(input_row_grad, qkv_both, out_both)
    scaled_one = input_row_grad * gains[0]
    input_grad = hidden_grad + inverse_one * (
        scaled_one
        - inputs_f
        * inverse_one
        * inverse_one
        * jnp.mean(scaled_one * inputs_f, axis=-1, keepdims=True)
    )
    gain_one_grad = jnp.sum(input_row_grad * inputs_f * inverse_one, axis=0)

    mixes = [lax.optimization_barrier((row[0], row[1], qkv_send))[:2] for row in (rows_a, rows_s, rows_b)]
    mixer_peer = swap_core(sum_call([mix[1] for mix in mixes], 5))
    mixer = sum_call([mix[0] for mix in mixes] + [mixer_peer], 5)
    mixer_local = lax.psum_scatter(mixer, "tensor", scatter_dimension=0, tiled=True)

    per_shard = HEAD_DIM // owners
    bias_parts = jnp.moveaxis(bias_grad.reshape(3, local_heads, owners, per_shard), 2, 0).reshape(owners, -1)
    bias_parts = jnp.pad(jnp.roll(bias_parts, -f, axis=0), ((0, 0), (0, shard - 3 * local_heads * per_shard)))
    small_sums = jnp.concatenate([router_grad, gain_one_grad[None], gain_two_grad[None]], axis=0)
    small_here = sum_small(small_sums, bias_parts.reshape(1, width), f, shard)
    small_sums = small_here + swap_x(small_here)
    bias_out = small_sums[11, : 3 * local_heads * per_shard].reshape(3, local_heads, per_shard)

    shared_up_out, shared_down_out = shared_call(after(total_s, qkv_part, out_part), peer_s, c, x)
    gate_up_out = place_call(after(total_b, shared_up_out), peer_b, c, 2 * (1 - x), (0, 2))
    down_out = place_call(total_b, peer_b, c, 2 * (1 - x), (2, 1))
    total_a = add_experts(after(sum_a, qkv_part, out_part, gate_up_out, down_out, small_here), from_b)
    peer_a = swap_core(total_a)

    def core_join(part, hidden_axis):
        part = add(part, after(swap_x(part), total_a))
        peer = swap_core(part)
        return jnp.where(
            c == 0,
            jnp.concatenate([part, peer], axis=hidden_axis),
            jnp.concatenate([peer, part], axis=hidden_axis),
        ).astype(F32)

    qkv_out, out_out = core_join(qkv_part, 2), core_join(out_part, 0)
    result = turn_back((hidden_rows + after(mixer_local, qkv_out).astype(F32)).astype(BF16))
    gate_up_out = place_call(total_a, peer_a, c, 2 * x, (0, 2), gate_up_out)
    gate_up_out = jnp.transpose(gate_up_out, (0, 3, 1, 2))
    down_out = place_call(total_a, peer_a, c, 2 * x, (2, 1), down_out).reshape(EXPERTS, hidden, shard)

    return (
        result,
        turn_back(input_grad),
        small_sums[9:11],
        qkv_out,
        bias_out,
        out_out,
        small_sums[:EXPERTS].T,
        small_sums[EXPERTS],
        gate_up_out,
        down_out,
        shared_up_out,
        shared_down_out,
    )


def solution(mesh):
    in_specs = (
        P(("rep", "fsdp", "tensor"), None),
        P(("rep", "fsdp", "tensor"), None),
        P(("rep", "fsdp"), None),
        P(("rep", "fsdp"), None),
        P(None, "fsdp"),
        P(None, "fsdp", "tensor"),
        P(None, "tensor", "fsdp"),
        P("tensor", "fsdp"),
        P("fsdp", None),
        P("fsdp"),
        P(None, "fsdp", None, "tensor"),
        P(None, "tensor", "fsdp"),
        P("fsdp", None, "tensor"),
        P("tensor", "fsdp"),
    )
    out_specs = (
        P(("rep", "fsdp", "tensor"), None),
        P(("rep", "fsdp", "tensor"), None),
        P(None, "fsdp"),
        P(None, "fsdp", "tensor"),
        P(None, "tensor", "fsdp"),
        P("tensor", "fsdp"),
        P("fsdp", None),
        P("fsdp"),
        P(None, "fsdp", None, "tensor"),
        P(None, "tensor", "fsdp"),
        P("fsdp", None, "tensor"),
        P("tensor", "fsdp"),
    )
    return jax.shard_map(shards, mesh=mesh, in_specs=in_specs, out_specs=out_specs, check_vma=False)
```

```python
import functools

import jax
import jax.numpy as jnp
from jax import lax
from jax.experimental import pallas as pl
from jax.experimental.pallas import tpu as pltpu
from jax.sharding import PartitionSpec as P

HEAD_DIM = 128
EXPERTS = 8
LENGTH = 640
PIECE = 256
EPSILON = 1e-06
BF16 = jnp.bfloat16
F32 = jnp.float32
COLS = 256
MESH = pl.DeviceIdType.MESH
CHEAP = pl.CostEstimate(flops=1, bytes_accessed=1, transcendentals=0)


def rope_tables(length, head_dim):
    half_dim = head_dim // 2
    frequency = 1000000.0 ** (-jnp.arange(half_dim, dtype=F32) * (2.0 / head_dim))
    angles = jnp.arange(length, dtype=F32)[:, None] * frequency[None, :]
    return (jnp.cos(angles), jnp.sin(angles))


def after(value, *others):
    return lax.optimization_barrier((value,) + others)[0]


def swap_y(a):
    return lax.ppermute(a, "fsdp", [(0, 1), (1, 0)])


def swap_x(a):
    n = lax.axis_size("rep")
    return lax.ppermute(a, "rep", [(i, i ^ 2) for i in range(n)])


def swap_core(a):
    n = lax.axis_size("rep")
    return lax.ppermute(a, "rep", [(i, i ^ 1) for i in range(n)])


CHUNK = 16


def device(axis, index):
    return {axis: index}


def rows_kernel(
    n, rows, part_count, with_core_in, with_thin, with_scatter, with_gather, with_core_out, middle, extra_count, extra_out, bulk_count, *refs
):
    refs = list(refs)
    take = refs.pop
    parts = [take(0) for _ in range(part_count)]
    peer_parts = [take(0) for _ in range(part_count)] if with_core_in else None
    thin, thin_peer, thin_matrix = (take(0), take(0), take(0)) if with_thin else (None, None, None)
    extras = [take(0) for _ in range(extra_count)]
    bulk_src = [take(0) for _ in range(bulk_count)]
    outs = [take(0) for _ in range(extra_out)]
    full = take(0) if with_gather else None
    full_peer = take(0) if with_core_out else None
    bulk_dst = [take(0) for _ in range(bulk_count)]
    chunks = rows // CHUNK
    z = lax.axis_index("tensor")
    r = lax.axis_index("rep")
    core = r + 1 - 2 * lax.rem(r, 2)
    has_left, has_right = z > 0, z < n - 1
    pairs = with_core_in or with_core_out
    if bulk_count:
        bulk_send, bulk_recv = take(0), take(0)
    if with_core_in:
        core_src, core_buf, core_in_send, core_in_recv = take(0), take(0), take(0), take(0)
    if with_scatter:
        in_bufs, out_bufs = (take(0), take(0)), (take(0), take(0))
        sc_send, sc_recv = take(0), take(0)
    if with_gather:
        ga_send, ga_recv = take(0), take(0)
    if with_core_out:
        core_out_send, core_out_recv = take(0), take(0)

    barrier = pltpu.get_barrier_semaphore()

    @pl.when(has_left)
    def _():
        pl.semaphore_signal(barrier, inc=1, device_id=device("tensor", z - 1), device_id_type=MESH)

    @pl.when(has_right)
    def _():
        pl.semaphore_signal(barrier, inc=1, device_id=device("tensor", z + 1), device_id_type=MESH)

    if pairs:
        pl.semaphore_signal(barrier, inc=1, device_id=device("rep", core), device_id_type=MESH)
    across = r + 2 - 4 * (r // 2)
    if bulk_count:
        pl.semaphore_signal(barrier, inc=1, device_id=device("rep", across), device_id_type=MESH)
    greeted = jnp.where(has_left, 1, 0) + jnp.where(has_right, 1, 0) + int(pairs) + int(bulk_count > 0)
    pl.semaphore_wait(barrier, greeted)

    def chunk_at(block, i):
        return pl.ds(pl.multiple_of(block * rows + i * CHUNK, CHUNK), CHUNK)

    def chunk_in(i):
        return pl.ds(pl.multiple_of(i * CHUNK, CHUNK), CHUNK)

    def remote(src, dst, send, recv, axis, index):
        return pltpu.make_async_remote_copy(
            src_ref=src, dst_ref=dst, send_sem=send, recv_sem=recv,
            device_id=device(axis, index), device_id_type=MESH,
        )

    def bulk_copy(k):
        return remote(bulk_src[k], bulk_dst[k], bulk_send.at[k], bulk_recv.at[k], "rep", across)

    for k in range(bulk_count):
        bulk_copy(k).start()

    def core_in_copy(block, i):
        here = chunk_at(block, i)
        return remote(
            core_src.at[here], core_buf.at[here], core_in_send.at[block, i], core_in_recv.at[block, i], "rep", core
        )

    def scatter_copy(way, m, i):
        here = chunk_in(i)
        return remote(
            out_bufs[way].at[m, here], in_bufs[way].at[m, here], sc_send.at[way, m, i], sc_recv.at[way, m, i],
            "tensor", z + 1 - 2 * way,
        )

    def gather_copy(way, k, i):
        here = chunk_at(z - k + 2 * k * way, i)
        return remote(
            full.at[here], full.at[here], ga_send.at[way, k, i], ga_recv.at[way, k, i], "tensor", z + 1 - 2 * way
        )

    def core_out_copy(block, i):
        here = chunk_at(block, i)
        return remote(
            full.at[here], full_peer.at[here], core_out_send.at[block, i], core_out_recv.at[block, i], "rep", core
        )

    def all_chunks(body):
        def step(i, carry):
            body(i)
            return carry

        lax.fori_loop(0, chunks, step, 0)

    def sum_terms(arrays, small, here):
        value = arrays[0][here, :].astype(F32)
        for more in arrays[1:]:
            value = value + more[here, :].astype(F32)
        if with_thin:
            value = value + dot_nn(small[here, :], thin_matrix[...])
        return value

    def core_in_step(i):
        @pl.when(i < chunks)
        def _():
            for block in range(n):
                here = chunk_at(block, i)
                core_src[here, :] = sum_terms(peer_parts, thin_peer, here).astype(BF16)
                core_in_copy(block, i).start()

    ahead = 2
    if with_core_in:
        for i in range(ahead):
            core_in_step(i)

    def term(block, i):
        here = chunk_at(block, i)
        value = sum_terms(parts, thin, here)
        if with_core_in:
            core_in_copy(block, i).wait_recv()
            value = value + core_buf[here, :].astype(F32)
        return value

    def inside(i):
        return (i >= 0) & (i < chunks)

    def scatter_step(way, i, has_source, does_send):
        for m in range(n - 1):
            scatter_message(way, m, i - m, has_source, does_send(n - 1 - m if way == 0 else m))

    def scatter_message(way, m, i, has_source, does_send):
        block = n - 1 - m if way == 0 else m
        here = chunk_in(i)

        @pl.when(inside(i) & does_send)
        def _():
            value = term(block, i)

            @pl.when(has_source)
            def _():
                scatter_copy(way, m, i).wait_recv()
                out_bufs[way][m, here, :] = (value + in_bufs[way][m, here, :].astype(F32)).astype(BF16)

            @pl.when(jnp.logical_not(has_source))
            def _():
                out_bufs[way][m, here, :] = value.astype(BF16)

            scatter_copy(way, m, i).start()

    def own_step(i):
        @pl.when(inside(i))
        def _():
            here = chunk_in(i)
            if with_scatter:
                total[...] = term(z, i)

                @pl.when(has_left)
                def _():
                    m = n - 1 - z
                    scatter_copy(0, m, i).wait_recv()
                    total[...] += in_bufs[0][m, here, :].astype(F32)

                @pl.when(has_right)
                def _():
                    scatter_copy(1, z, i).wait_recv()
                    total[...] += in_bufs[1][z, here, :].astype(F32)

                sent = middle(total[...], here, extras, outs)
            else:
                sent = parts[0][here, :]
            if with_gather:
                full[chunk_at(z, i), :] = sent

                @pl.when(has_right)
                def _():
                    gather_copy(0, 0, i).start()

                @pl.when(has_left)
                def _():
                    gather_copy(1, 0, i).start()

                if with_core_out:
                    core_out_copy(z, i).start()

    def gather_step(k, i):
        for way in range(2):
            comes = z - k >= 0 if way == 0 else z + k <= n - 1
            goes = has_right if way == 0 else has_left

            @pl.when(inside(i) & comes)
            def _():
                landed = full.at[chunk_at(z - k + 2 * k * way, i)]
                remote(
                    landed, landed, ga_send.at[way, k - 1, i], ga_recv.at[way, k - 1, i], "tensor", z + 1 - 2 * way
                ).wait_recv()
                if k < n - 1:

                    @pl.when(goes)
                    def _():
                        gather_copy(way, k, i).start()

                if with_core_out:
                    core_out_copy(z - k + 2 * k * way, i).start()

    lead = n - 1 if with_scatter else 0
    if with_scatter:
        total = take(0)

    def tick(t, carry):
        if with_core_in:
            core_in_step(t + ahead)
        if with_scatter:
            scatter_step(0, t - z, has_left, lambda block: block > z)
            scatter_step(1, t - (n - 1 - z), has_right, lambda block: block < z)
        own_step(t - lead)
        if with_gather:
            for k in range(1, n):
                gather_step(k, t - lead - k)
        return carry

    lax.fori_loop(0, chunks + lead + (n - 1 if with_gather else 0), tick, 0)

    @all_chunks
    def _(i):
        if with_core_in:
            for block in range(n):
                core_in_copy(block, i).wait_send()
        for way in range(2):
            goes = has_right if way == 0 else has_left
            if with_scatter:
                for m in range(n - 1):
                    block = n - 1 - m if way == 0 else m

                    @pl.when(goes & ((block > z) if way == 0 else (block < z)))
                    def _():
                        scatter_copy(way, m, i).wait_send()

            if with_gather:
                for k in range(n - 1):
                    has = z - k >= 0 if way == 0 else z + k <= n - 1

                    @pl.when(goes & has)
                    def _():
                        gather_copy(way, k, i).wait_send()

        if with_core_out:
            for block in range(n):
                core_out_copy(block, i).wait_send()
                core_out_copy(block, i).wait_recv()

    for k in range(bulk_count):
        bulk_copy(k).wait()


def rows_call(
    collective_id, parts, peer_parts=(), thin=(), extras=(), bulk=(), scatter=True, gather=True, core_out=False, middle=None,
    out_types=(),
):
    n = lax.axis_size("tensor")
    width = parts[0].shape[1]
    rows = parts[0].shape[0] // n if scatter else parts[0].shape[0]
    chunks = rows // CHUNK
    vmem_spec = pl.BlockSpec(memory_space=pltpu.VMEM)
    full = jax.ShapeDtypeStruct((n * rows, width), BF16)
    out_shape = list(out_types) + ([full] if gather else []) + ([full] if core_out else [])
    vmem_outs = len(out_shape)
    out_shape += [jax.ShapeDtypeStruct(a.shape, a.dtype) for a in bulk]
    any_spec = pl.BlockSpec(memory_space=pl.ANY)
    scratch = [pltpu.SemaphoreType.DMA((len(bulk),))] * 2 if bulk else []
    if peer_parts:
        scratch += [pltpu.VMEM((n * rows, width), BF16)] * 2 + [pltpu.SemaphoreType.DMA((n, chunks))] * 2
    if scatter:
        scratch += [pltpu.VMEM((n - 1, rows, width), BF16)] * 4
        scratch += [pltpu.SemaphoreType.DMA((2, n - 1, chunks))] * 2
    if gather:
        scratch += [pltpu.SemaphoreType.DMA((2, n - 1, chunks))] * 2
    if core_out:
        scratch += [pltpu.SemaphoreType.DMA((n, chunks))] * 2
    if scatter:
        scratch += [pltpu.VMEM((CHUNK, width), F32)]
    operands = [*parts, *peer_parts, *thin, *extras]
    vmem_ins = len(operands)
    operands += list(bulk)
    return pl.pallas_call(
        functools.partial(
            rows_kernel, n, rows, len(parts), bool(peer_parts), bool(thin), scatter, gather, core_out, middle, len(extras), len(out_types), len(bulk)
        ),
        out_shape=out_shape,
        in_specs=[vmem_spec] * vmem_ins + [any_spec] * len(bulk),
        out_specs=[vmem_spec] * vmem_outs + [any_spec] * len(bulk),
        scratch_shapes=scratch,
        compiler_params=pltpu.CompilerParams(
            collective_id=collective_id, has_side_effects=True, vmem_limit_bytes=56 * 2**20
        ),
        cost_estimate=CHEAP,
        name="rows",
    )(*operands)


def norm_middle(total, here, extras, outs):
    inputs, gain = extras
    hidden = inputs[here, :].astype(F32) + total
    outs[0][here, :] = hidden
    inverse = lax.rsqrt(jnp.mean(hidden * hidden, axis=-1, keepdims=True) + EPSILON)
    return (hidden * inverse * gain[...]).astype(BF16)


def norm_back_middle(total, here, extras, outs):
    hidden_ref, cot, gain = extras
    hidden = hidden_ref[here, :]
    inverse = lax.rsqrt(jnp.mean(hidden * hidden, axis=-1, keepdims=True) + EPSILON)
    scaled = total * gain[...]
    grad = cot[here, :].astype(F32) + inverse * (
        scaled - hidden * inverse * inverse * jnp.mean(scaled * hidden, axis=-1, keepdims=True)
    )
    outs[0][here, :] = total
    outs[1][here, :] = grad
    return grad.astype(BF16)


def plain_middle(total, here, extras, outs):
    outs[0][here, :] = total


def others_of(own, f, axis):
    if lax.axis_size("fsdp") == 2:
        return swap_y(own)
    whole = lax.all_gather(own, "fsdp", axis=axis, tiled=True)
    size = own.shape[axis]
    turned = jnp.roll(whole, -f * size, axis=axis)
    return lax.slice_in_dim(turned, size, whole.shape[axis], axis=axis)


def reduce_fsdp(own, other, f, axis, add):
    if lax.axis_size("fsdp") == 2:
        return add(own, swap_y(other))
    whole = jnp.roll(jnp.concatenate([own, other], axis=axis), f * own.shape[axis], axis=axis)
    return lax.psum_scatter(whole, "fsdp", scatter_dimension=axis, tiled=True)


def sum_small(values, per_tensor, f, shard):
    total = sum_rep_first(jnp.concatenate([sum_tensor(values), per_tensor], axis=0))
    if lax.axis_size("fsdp") == 2:
        total = total[:, :shard] + swap_y(total[:, shard:])
    else:
        whole = jnp.roll(total, f * shard, axis=1)
        total = lax.psum_scatter(whole, "fsdp", scatter_dimension=1, tiled=True)
    return total


def sum_rep_first(total):
    return total + swap_core(total)


def sum_tensor(total):
    n = lax.axis_size("tensor")
    step = 1
    while step < n:
        total = total + lax.ppermute(total, "tensor", [(i, i ^ step) for i in range(n)])
        step *= 2
    return total


def dot_nt(a, b):
    return lax.dot_general(a, b, (((1,), (1,)), ((), ())), preferred_element_type=F32)


def dot_nn(a, b):
    return lax.dot_general(a, b, (((1,), (0,)), ((), ())), preferred_element_type=F32)


def mask_rows(starts, length):
    key = lax.broadcasted_iota(jnp.int32, (length, length), 0)
    query = lax.broadcasted_iota(jnp.int32, (length, length), 1)
    visible = key <= query
    for piece in range(2):
        first = starts[0, piece]
        visible |= (jnp.minimum(key, query) >= first) & (jnp.maximum(key, query) < first + PIECE)
    return jnp.where(visible, 0.0, -1e30).astype(F32)


def attend_kernel(
    heads, own_width, starts, rows, w_own, w_oth, bias, cos, sin, out_own, out_oth,
    q_out, k_out, v_out, attended, stats, part, mask,
):
    length = rows.shape[0]
    scale = HEAD_DIM ** (-0.5)
    for c, out in ((0, q_out), (1, k_out), (2, v_out)):
        project = dot_nn(rows[:, :own_width], w_own[c]) + dot_nn(rows[:, own_width:], w_oth[c]) + bias[c : c + 1, :]
        for h in range(heads):
            here = slice(h * HEAD_DIM, (h + 1) * HEAD_DIM)
            values = project[:, here]
            if c < 2:
                values = values * cos[...] + pltpu.roll(values, HEAD_DIM // 2, 1) * sin[...]
            out[:, here] = values.astype(BF16)
    mask[...] = mask_rows(starts, length)

    def one_head(h, carry):
        here = pl.ds(pl.multiple_of(h * HEAD_DIM, HEAD_DIM), HEAD_DIM)
        scores = dot_nt(k_out[:, here], q_out[:, here]) * scale + mask[...]
        top = jnp.max(scores, axis=0, keepdims=True)
        weights = jnp.exp(scores - top)
        inverse = 1.0 / jnp.sum(weights, axis=0, keepdims=True)
        probs = (weights * inverse).astype(BF16)
        attended[:, here] = dot_nn(v_out[:, here].T, probs).T.astype(BF16)
        stats[pl.ds(h, 1), :] = top
        stats[pl.ds(heads + h, 1), :] = inverse
        return carry

    lax.fori_loop(0, heads, one_head, 0)
    part[:, :own_width] = dot_nn(attended[...], out_own[...]).astype(BF16)
    part[:, own_width:] = dot_nn(attended[...], out_oth[...]).astype(BF16)


def attend_back_kernel(
    heads, own_width, starts, grad, w_own, w_oth, cos, sin, out_own, out_oth, q, k, v, stats,
    project_grad, bias_grad, rows_grad, mask, attended_grad,
):
    length = grad.shape[0]
    scale = HEAD_DIM ** (-0.5)
    attended_grad[...] = (
        dot_nt(grad[:, :own_width], out_own[...]) + dot_nt(grad[:, own_width:], out_oth[...])
    ).astype(BF16)
    mask[...] = mask_rows(starts, length)

    def turn_back(values):
        return values * cos[...] - pltpu.roll(values, HEAD_DIM // 2, 1) * sin[...]

    def one_head(h, carry):
        here = pl.ds(pl.multiple_of(h * HEAD_DIM, HEAD_DIM), HEAD_DIM)
        queries, keys, grads = q[:, here], k[:, here], attended_grad[:, here]
        scores = dot_nt(keys, queries) * scale + mask[...]
        probs = jnp.exp(scores - stats[pl.ds(h, 1), :]) * stats[pl.ds(heads + h, 1), :]
        value_grad = dot_nn(probs.astype(BF16), grads)
        probs_grad = dot_nt(v[:, here], grads)
        mean = jnp.sum(probs * probs_grad, axis=0, keepdims=True)
        score_grad = (probs * (probs_grad - mean)).astype(BF16)
        key_grad = dot_nn(score_grad, queries) * scale
        query_grad = dot_nn(score_grad.T, keys) * scale
        project_grad[0, :, here] = turn_back(query_grad).astype(BF16)
        project_grad[1, :, here] = turn_back(key_grad).astype(BF16)
        project_grad[2, :, here] = value_grad.astype(BF16)
        return carry

    lax.fori_loop(0, heads, one_head, 0)
    total_own = total_oth = None
    for c in range(3):
        grads = project_grad[c]
        bias_grad[c : c + 1, :] = jnp.sum(grads.astype(F32), axis=0, keepdims=True)
        own, oth = dot_nt(grads, w_own[c]), dot_nt(grads, w_oth[c])
        total_own = own if c == 0 else total_own + own
        total_oth = oth if c == 0 else total_oth + oth
    rows_grad[:, :own_width] = total_own.astype(BF16)
    rows_grad[:, own_width:] = total_oth.astype(BF16)


def attention_call(kernel, name, operands, out_shape, heads, own_width, length, more_scratch=()):
    vmem_spec = pl.BlockSpec(memory_space=pltpu.VMEM)
    return pl.pallas_call(
        functools.partial(kernel, heads, own_width),
        out_shape=out_shape,
        in_specs=[pl.BlockSpec(memory_space=pltpu.SMEM)] + [vmem_spec] * (len(operands) - 1),
        out_specs=[vmem_spec] * len(out_shape),
        scratch_shapes=[pltpu.VMEM((length, length), F32), *more_scratch],
        cost_estimate=CHEAP,
        compiler_params=pltpu.CompilerParams(vmem_limit_bytes=56 * 2**20),
        name=name,
    )(*operands)


def experts_kernel(rows, width, own_width, hidden, direct, *refs):
    if direct:
        first, x0, x1, c0, c10, c11, gate, gate_up, down, w_oth, *refs = refs
    else:
        x0, x1, c0, c10, c11, gate, w_own, w_oth, *refs = refs
    dw_own, dw_oth, mix0, mix1, ng0, ng1, gate_grad, *refs = refs
    xv, cv, wgu, wd, ga, pre, ga_t, pre_t, st_mix, st_ng, st_dw, w_sem, x_sem, c_sem, out_sem, dw_sem = refs
    seq = rows // 2
    both = 2 * hidden
    oth_width = width - own_width

    def w_copies(part):
        copies = []
        for k in range(2):
            if direct:
                own = gate_up.at[first[0] + k, part] if part < 2 else down.at[first[0] + k]
            else:
                own = w_own.at[k, part]
            to = wd.at[pl.ds(k * hidden, hidden)] if part == 2 else wgu.at[pl.ds(part * both + k * hidden, hidden)]
            copies.append(pltpu.make_async_copy(own, to.at[:, pl.ds(0, own_width)], w_sem.at[part, k, 0]))
            copies.append(
                pltpu.make_async_copy(w_oth.at[k, part], to.at[:, pl.ds(own_width, oth_width)], w_sem.at[part, k, 1])
            )
        return copies

    def row_copies(sources, to, sem):
        return [
            pltpu.make_async_copy(sources[s], to.at[pl.ds(s * seq, seq)], sem.at[s]) for s in range(2)
        ]

    x_copies = row_copies((x0, x1), xv, x_sem)
    c_copies = [pltpu.make_async_copy(c0, cv.at[pl.ds(0, seq)], c_sem.at[0])]
    for i, part in enumerate((c10, c11)):
        here = pl.ds(seq + i * part.shape[0], part.shape[0])
        c_copies.append(pltpu.make_async_copy(part, cv.at[here], c_sem.at[1 + i]))
    order = [x_copies[0], *w_copies(0), *w_copies(1), c_copies[0], *w_copies(2)]
    later = [x_copies[1], *c_copies[1:]]
    for copy in order + later:
        copy.start()
    for copy in order:
        copy.wait()

    def token_tile(t, carry):
        @pl.when(t == seq // COLS)
        def _():
            for copy in later:
                copy.wait()

        here = pl.ds(pl.multiple_of(t * COLS, COLS), COLS)
        gu = dot_nt(wgu[...], xv[here, :])
        h = dot_nt(wd[...], cv[here, :])
        g, u = gu[:both], gu[both:]
        sig = jax.nn.sigmoid(g)
        act = g * sig * u
        product = act * h
        scale_rows = []
        for k in range(2):
            part = product[k * hidden : (k + 1) * hidden]
            gate_grad[pl.ds(k, 1), here] = jnp.sum(part, axis=0, keepdims=True)
            scale_rows.append(jnp.broadcast_to(gate[pl.ds(k, 1), here], (hidden, COLS)))
        scale = jnp.concatenate(scale_rows, axis=0)
        back = scale * h
        ga_here = (scale * act).astype(BF16)
        pg_here = (back * u * sig * (1.0 + g * (1.0 - sig))).astype(BF16)
        pu_here = (back * g * sig).astype(BF16)
        ga[:, here] = ga_here
        pre[:both, here] = pg_here
        pre[both:, here] = pu_here
        ga_t[here, :] = ga_here.T
        pre_t[here, :both] = pg_here.T
        pre_t[here, both:] = pu_here.T
        return carry

    lax.fori_loop(0, rows // COLS, token_tile, 0)

    def row_outs(slot, cols):
        return [
            pltpu.make_async_copy(stage.at[slot, pl.ds(s * seq, seq)], outs[s].at[:, cols], out_sem.at[slot, i, s])
            for i, (stage, outs) in enumerate(((st_mix, (mix0, mix1)), (st_ng, (ng0, ng1))))
            for s in range(2)
        ]

    def weight_outs(slot, dst, cols):
        return [
            pltpu.make_async_copy(
                st_dw.at[slot, pl.ds((part * 2 + k) * hidden, hidden)], dst.at[k, part, :, cols], dw_sem.at[slot, part, k]
            )
            for part in range(3)
            for k in range(2)
        ]

    def wait_slot(slot):
        for copy in row_outs(slot, pl.ds(0, COLS)) + weight_outs(slot, dw_own, pl.ds(0, COLS)):
            copy.wait()

    def column_tile(n, slot, src_col, dst, dst_col):
        cols = pl.ds(pl.multiple_of(src_col, COLS), COLS)

        @pl.when(n >= 2)
        def _():
            wait_slot(slot)

        st_dw[slot, : 2 * both] = dot_nn(pre[...], xv[:, cols]).astype(BF16)
        st_dw[slot, 2 * both :] = dot_nn(ga[...], cv[:, cols]).astype(BF16)
        for copy in weight_outs(slot, dst, pl.ds(pl.multiple_of(dst_col, COLS), COLS)):
            copy.start()
        st_ng[slot] = dot_nn(pre_t[...], wgu[:, cols]).astype(BF16)
        st_mix[slot] = dot_nn(ga_t[...], wd[:, cols]).astype(BF16)
        for copy in row_outs(slot, cols):
            copy.start()

    oth_tiles, own_tiles = oth_width // COLS, own_width // COLS

    def oth_tile(n, carry):
        column_tile(n, lax.rem(n, 2), own_width + n * COLS, dw_oth, n * COLS)
        return carry

    def own_tile(n, carry):
        column_tile(n + oth_tiles, lax.rem(n + oth_tiles, 2), n * COLS, dw_own, n * COLS)
        return carry

    lax.fori_loop(0, oth_tiles, oth_tile, 0)
    lax.fori_loop(0, own_tiles, own_tile, 0)
    for slot in range(2):
        wait_slot(slot)


def experts_call(x0, x1, c0, c1, gate, w_own, w_oth):
    direct = isinstance(w_own, tuple)
    seq, width = x0.shape
    rows = 2 * seq
    hidden, own_width = (w_own[1] if direct else w_own).shape[2:]
    smem_spec = pl.BlockSpec(memory_space=pltpu.SMEM)
    own_operands = w_own[1:] if direct else (w_own,)
    any_spec = pl.BlockSpec(memory_space=pl.ANY)
    vmem_spec = pl.BlockSpec(memory_space=pltpu.VMEM)
    out_rows = jax.ShapeDtypeStruct((seq, width), BF16)
    return pl.pallas_call(
        functools.partial(experts_kernel, rows, width, own_width, hidden, direct),
        out_shape=[
            jax.ShapeDtypeStruct((2, 3, hidden, own_width), BF16),
            jax.ShapeDtypeStruct((2, 3, hidden, width - own_width), BF16),
            out_rows, out_rows, out_rows, out_rows,
            jax.ShapeDtypeStruct((8, rows), F32),
        ],
        in_specs=[smem_spec] * direct + [any_spec] * 5 + [vmem_spec] + [any_spec] * (len(own_operands) + 1),
        out_specs=[any_spec] * 6 + [vmem_spec],
        scratch_shapes=[
            pltpu.VMEM((rows, width), BF16),
            pltpu.VMEM((rows, width), BF16),
            pltpu.VMEM((4 * hidden, width), BF16),
            pltpu.VMEM((2 * hidden, width), BF16),
            pltpu.VMEM((2 * hidden, rows), BF16),
            pltpu.VMEM((4 * hidden, rows), BF16),
            pltpu.VMEM((rows, 2 * hidden), BF16),
            pltpu.VMEM((rows, 4 * hidden), BF16),
            pltpu.VMEM((2, rows, COLS), BF16),
            pltpu.VMEM((2, rows, COLS), BF16),
            pltpu.VMEM((2, 6 * hidden, COLS), BF16),
            pltpu.SemaphoreType.DMA((3, 2, 2)),
            pltpu.SemaphoreType.DMA((2,)),
            pltpu.SemaphoreType.DMA((3,)),
            pltpu.SemaphoreType.DMA((2, 2, 2)),
            pltpu.SemaphoreType.DMA((2, 3, 2)),
        ],
        cost_estimate=CHEAP,
        compiler_params=pltpu.CompilerParams(vmem_limit_bytes=58 * 2**20),
        name="experts",
    )(*([w_own[0]] if direct else []), x0, x1, c0, *c1, gate, *own_operands, w_oth)


def sum_kernel(*refs):
    total = refs[0][...].astype(F32)
    for ref in refs[1:-1]:
        total = total + ref[...].astype(F32)
    refs[-1][...] = total.astype(BF16)


def sum_call(arrays, steps, flip=-1):
    rows, columns = arrays[0].shape
    block = (rows // steps, columns)

    def spec(k):
        if k == flip:
            return pl.BlockSpec(block, lambda i: (lax.rem(i + steps // 2, steps), 0))
        return pl.BlockSpec(block, lambda i: (i, 0))

    return pl.pallas_call(
        sum_kernel,
        out_shape=jax.ShapeDtypeStruct((rows, columns), BF16),
        grid=(steps,),
        in_specs=[spec(k) for k in range(len(arrays))],
        out_specs=spec(-2),
        cost_estimate=CHEAP,
        compiler_params=pltpu.CompilerParams(vmem_limit_bytes=40 * 2**20),
        name="sums",
    )(*arrays)


def add_experts(one, two, flip=False):
    flat = [a.reshape(-1, a.shape[-1]) for a in (one, two)]
    return sum_call(flat, 4, 1 if flip else -1).reshape(one.shape)


def dense_kernel(half, own_width, core, rows, project_grad, attended, branch_grad, *outs):
    qkv_own, qkv_oth, qkv_send, out_own, out_oth, out_send, rows_t = outs
    rows_t[...] = rows[...].T
    for keep in (False, True):
        cols = pl.ds(pl.multiple_of((core[0] if keep else 1 - core[0]) * half, half), half)
        for c in range(3):
            grad = dot_nn(rows_t[...], project_grad[c, :, cols]).astype(BF16)
            if keep:
                qkv_own[c] = grad[:own_width]
                qkv_oth[c] = grad[own_width:]
            else:
                qkv_send[c] = grad
        grad = dot_nn(attended[:, cols].T, branch_grad[...]).astype(BF16)
        if keep:
            out_own[...] = grad[:, :own_width]
            out_oth[...] = grad[:, own_width:]
        else:
            out_send[...] = grad


def dense_call(core, rows, project_grad, attended, branch_grad, own_width):
    length, width = rows.shape
    half = attended.shape[1] // 2
    vmem_spec = pl.BlockSpec(memory_space=pltpu.VMEM)
    shapes = [(3, own_width, half), (3, width - own_width, half), (3, width, half)]
    shapes += [(half, own_width), (half, width - own_width), (half, width)]
    return pl.pallas_call(
        functools.partial(dense_kernel, half, own_width),
        out_shape=[jax.ShapeDtypeStruct(shape, BF16) for shape in shapes],
        in_specs=[pl.BlockSpec(memory_space=pltpu.SMEM)] + [vmem_spec] * 4,
        out_specs=[vmem_spec] * 6,
        scratch_shapes=[pltpu.VMEM((width, length), BF16)],
        cost_estimate=CHEAP,
        compiler_params=pltpu.CompilerParams(vmem_limit_bytes=48 * 2**20),
        name="dense_grads",
    )(core, rows, project_grad, attended, branch_grad)


def place_kernel(table, source, *refs):
    refs[-1][...] = source[...].astype(F32)


def place_call(source, first, parts, base=None):
    at, length = parts
    count, _, hidden, width = source.shape
    return pl.pallas_call(
        place_kernel,
        out_shape=jax.ShapeDtypeStruct((EXPERTS, length, hidden, width), F32),
        grid_spec=pltpu.PrefetchScalarGridSpec(
            num_scalar_prefetch=1,
            grid=(count, length),
            in_specs=[pl.BlockSpec((1, 1, hidden, width), lambda e, part, tab: (e, at + part, 0, 0))]
            + [pl.BlockSpec(memory_space=pl.ANY)] * (base is not None),
            out_specs=pl.BlockSpec((1, 1, hidden, width), lambda e, part, tab: (tab[0] + e, part, 0, 0)),
        ),
        input_output_aliases={} if base is None else {2: 0},
        cost_estimate=CHEAP,
        compiler_params=pltpu.CompilerParams(vmem_limit_bytes=40 * 2**20),
        name="place",
    )(jnp.reshape(first, (1,)).astype(jnp.int32), source, *([] if base is None else [base]))


def shared_kernel(table, mine, peer, up, down):
    def quarter(q, part):
        block = table[q]
        return jnp.where(table[4 + q] == 0, mine[block, part].astype(F32), peer[block, part].astype(F32))

    for part in range(2):
        up[:, part, :] = jnp.concatenate([quarter(q, part) for q in range(4)], axis=0).T
    down[...] = jnp.concatenate([quarter(q, 2) for q in range(4)], axis=0)


def shared_call(mine, peer, c, x):
    hidden, width = mine.shape[2:]
    q = jnp.arange(4, dtype=jnp.int32)
    table = jnp.concatenate([(q % 2) ^ x, (q // 2 != c).astype(jnp.int32)]).astype(jnp.int32)
    source = pl.BlockSpec((2, 3, hidden, 128), lambda n, tab: (0, 0, 0, n))
    return pl.pallas_call(
        shared_kernel,
        out_shape=[
            jax.ShapeDtypeStruct((width, 2, 4 * hidden), F32),
            jax.ShapeDtypeStruct((4 * hidden, width), F32),
        ],
        grid_spec=pltpu.PrefetchScalarGridSpec(
            num_scalar_prefetch=1,
            grid=(width // 128,),
            in_specs=[source, source],
            out_specs=[
                pl.BlockSpec((128, 2, 4 * hidden), lambda n, tab: (n, 0, 0)),
                pl.BlockSpec((4 * hidden, 128), lambda n, tab: (0, n)),
            ],
        ),
        cost_estimate=CHEAP,
        compiler_params=pltpu.CompilerParams(vmem_limit_bytes=40 * 2**20),
        name="shared",
    )(table, mine, peer)


def shards(
    block_input,
    cotangent,
    piece_starts,
    expert_ids,
    norm_gains,
    qkv_weight,
    qkv_bias,
    out_weight,
    router_weight,
    shared_gate,
    expert_gate_up,
    expert_down,
    shared_gate_up,
    shared_down,
):
    f = lax.axis_index("fsdp")
    owners = lax.axis_size("fsdp")
    r = lax.axis_index("rep")
    c, x = r % 2, r // 2
    shard = norm_gains.shape[1]
    width = owners * shard
    local_width = qkv_weight.shape[2]
    local_heads = local_width // HEAD_DIM
    half_width = local_width // 2
    hidden = expert_gate_up.shape[3]
    scale = HEAD_DIM ** (-0.5)

    def turn(rows):
        return jnp.roll(rows, -f * shard, axis=1)

    def turn_back(rows):
        return jnp.roll(rows, f * shard, axis=1)

    gains = jnp.concatenate([norm_gains, others_of(norm_gains, f, 1)], axis=1).astype(F32)
    cos_table, sin_table = rope_tables(LENGTH, HEAD_DIM)
    inputs = turn(block_input)
    inputs_f = inputs.astype(F32)
    cot = turn(cotangent)
    inverse_one = lax.rsqrt(jnp.mean(inputs_f * inputs_f, axis=-1, keepdims=True) + EPSILON)
    normed_local = (inputs_f * inverse_one * gains[0]).astype(BF16)
    normed = lax.all_gather(normed_local, "tensor", axis=0, tiled=True)
    gate_up_t = jnp.transpose(after(expert_gate_up, normed_local), (0, 2, 3, 1))
    small = jnp.concatenate([after(router_weight, normed_local).T.reshape(-1), shared_gate, qkv_bias.reshape(-1)])
    small_all = jnp.concatenate([small[None], others_of(small[None], f, 0)], axis=0)
    router = jnp.swapaxes(small_all[:, : 9 * shard].reshape(owners, 9, shard), 0, 1).reshape(9, width)
    bias = jnp.roll(small_all[:, 9 * shard :], f, axis=0).reshape(owners, 3, local_heads, -1)
    bias = jnp.moveaxis(bias, 0, 2).reshape(3, local_width).astype(F32)

    quarter = local_width // 4

    def fetch_quarters(weight, hidden_axis, shard_axis):
        mine = lax.dynamic_slice_in_dim(weight, r * quarter, quarter, hidden_axis)
        got = others_of(mine, f, shard_axis)
        pair = jnp.stack([got, swap_x(got)])
        peers = swap_core(pair)
        pair = jnp.where(x == 0, pair, pair[::-1])
        peers = jnp.where(x == 0, peers, peers[::-1])
        order = jnp.where(c == 0, jnp.stack([pair, peers], 1), jnp.stack([peers, pair], 1))
        return jnp.concatenate([order[i, j] for i in range(2) for j in range(2)], axis=hidden_axis), got

    qkv_oth, qkv_got = fetch_quarters(qkv_weight, 2, 1)
    out_oth, out_got = fetch_quarters(out_weight, 0, 1)


    def routed_chunk(first, gate_up_t):
        return jnp.concatenate(
            [
                lax.dynamic_slice_in_dim(gate_up_t, first, 2, 0),
                lax.dynamic_slice_in_dim(expert_down, first, 2, 0)[:, None],
            ],
            axis=1,
        )

    def shared_chunk(q, shared_up_t, shared_down):
        return jnp.concatenate(
            [
                lax.dynamic_slice_in_dim(shared_up_t, q * hidden, hidden, 1),
                lax.dynamic_slice_in_dim(shared_down, q * hidden, hidden, 0)[None],
            ],
            axis=0,
        )[None]

    first_a, first_b = 4 * c + 2 * x, 4 * c + 2 * (1 - x)
    shared_gate_up, shared_down, expert_ids = lax.optimization_barrier(
        (shared_gate_up, shared_down, expert_ids, normed_local)
    )[:3]
    ids_pair = jnp.concatenate([expert_ids, swap_core(expert_ids)], axis=0)
    shared_up_t = jnp.stack([shared_gate_up[:, 0].T, shared_gate_up[:, 1].T])
    own_s = jnp.concatenate([shared_chunk(q, shared_up_t, shared_down) for q in (2 * c + x, 2 * c + 1 - x)], axis=0)
    own_a = routed_chunk(first_a, after(gate_up_t, own_s))
    own_b = (jnp.reshape(first_b, (1,)).astype(jnp.int32), gate_up_t, expert_down)

    oth_a = others_of(after(own_a, qkv_got, out_got), f, 3)
    cos_rows = jnp.concatenate([cos_table, cos_table], axis=1)
    sin_rows = jnp.concatenate([-sin_table, sin_table], axis=1)
    normed = after(normed, own_s, ids_pair, cos_rows, sin_rows, bias, qkv_oth, out_oth)
    cot_rows = lax.all_gather(after(cot, normed), "tensor", axis=0, tiled=True)
    oth_s = others_of(after(own_s, normed), f, 3)

    heads_rows = jax.ShapeDtypeStruct((LENGTH, local_width), BF16)
    all_rows = jax.ShapeDtypeStruct((LENGTH, width), BF16)
    query_rows, key_rows, value_rows, attended, stats, heads_part = attention_call(
        attend_kernel,
        "attend",
        [piece_starts, normed, qkv_weight, qkv_oth, bias, cos_rows, sin_rows, out_weight, out_oth],
        [heads_rows] * 4 + [jax.ShapeDtypeStruct((2 * local_heads, LENGTH), F32), all_rows],
        local_heads,
        shard,
        LENGTH,
    )
    block_f32 = jax.ShapeDtypeStruct(inputs.shape, F32)
    hidden_rows, mixed, mixed_peer = rows_call(
        1, [heads_part], extras=(inputs, gains[1:2]), core_out=True, middle=norm_middle, out_types=[block_f32]
    )
    cot_rows = after(cot_rows, mixed)
    cot_peer = [swap_core(piece) for piece in jnp.split(cot_rows, 2)]
    oth_b = swap_x(after(oth_a, mixed))
    mixed_pair = jnp.concatenate([mixed, mixed_peer], axis=0)

    logits = lax.dot_general(router, mixed_pair, (((1,), (1,)), ((), ())), preferred_element_type=F32)
    router_probs = jax.nn.softmax(logits[:EXPERTS], axis=0)
    shared_scale = jax.nn.sigmoid(logits[EXPERTS:])
    names = jnp.arange(EXPERTS, dtype=jnp.int32)[:, None, None]
    chosen = jnp.any(ids_pair.T[None] == names, axis=1)
    gates = jnp.where(chosen, router_probs, 0.0)

    def gate_rows(first):
        return jnp.pad(lax.dynamic_slice_in_dim(gates, first, 2, 0), ((0, 6), (0, 0)))

    data = (mixed, mixed_peer, cot_rows, cot_peer)
    dw_own_a, dw_oth_a, *rows_a, grad_a = experts_call(*data, gate_rows(first_a), own_a, oth_a)
    shared_rows = after(jnp.broadcast_to(shared_scale, (8, shared_scale.shape[1])), grad_a)
    dw_own_s, dw_oth_s, *rows_s, grad_s = experts_call(*data, shared_rows, own_s, oth_s)
    dw_own_b, dw_oth_b, *rows_b, grad_b = experts_call(
        *data, after(gate_rows(first_b), grad_s), own_b, oth_b
    )

    prob_grad = jnp.zeros_like(router_probs)
    prob_grad = lax.dynamic_update_slice_in_dim(prob_grad, grad_a[:2], first_a, 0)
    prob_grad = lax.dynamic_update_slice_in_dim(prob_grad, grad_b[:2], first_b, 0)
    prob_grad = jnp.where(chosen, prob_grad, 0.0)
    logit_grad = router_probs * (prob_grad - jnp.sum(router_probs * prob_grad, axis=0, keepdims=True))
    scale_logit_grad = (grad_s[0:1] + grad_s[1:2]) * shared_scale * (1.0 - shared_scale)
    small_grad = jnp.concatenate([logit_grad, scale_logit_grad], axis=0)
    high = small_grad.astype(BF16)
    low = (small_grad - high.astype(F32)).astype(BF16)
    small_pair = jnp.concatenate([high, low], axis=0)
    router_both = jnp.dot(small_pair, mixed_pair, preferred_element_type=F32)
    router_grad = router_both[:9] + router_both[9:]
    thin = jnp.pad(small_pair, ((0, 128 - small_pair.shape[0]), (0, 0))).T
    thin_matrix = jnp.pad(jnp.concatenate([router, router], axis=0), ((0, 128 - small_pair.shape[0]), (0, 0)))

    def add(one, two):
        return (one.astype(F32) + two.astype(F32)).astype(BF16)

    def shard_sum(own, other):
        return reduce_fsdp(own, other, f, 3, add_experts)

    sum_a = shard_sum(dw_own_a, dw_oth_a)
    from_a = swap_x(sum_a)
    normed_two_grad, hidden_grad, branch_grad = rows_call(
        2,
        [after(rows_a[2], sum_a), rows_s[2], rows_b[2]],
        [rows_a[3], rows_s[3], rows_b[3]],
        [thin[:LENGTH], thin[LENGTH:], thin_matrix],
        extras=(hidden_rows, cot, gains[1:2]),
        middle=norm_back_middle,
        out_types=[block_f32, block_f32],
    )
    inverse_two = lax.rsqrt(jnp.mean(hidden_rows * hidden_rows, axis=-1, keepdims=True) + EPSILON)
    gain_two_grad = jnp.sum(normed_two_grad * hidden_rows * inverse_two, axis=0)

    sum_s = shard_sum(after(dw_own_s, branch_grad), dw_oth_s)
    branch_grad = after(branch_grad, sum_s)
    from_s = swap_x(sum_s)
    project_grad, bias_grad, normed_one_grad = attention_call(
        attend_back_kernel,
        "attend_back",
        [
            piece_starts, branch_grad, qkv_weight, qkv_oth, cos_rows, sin_rows, out_weight, out_oth,
            query_rows, key_rows, value_rows, stats,
        ],
        [
            jax.ShapeDtypeStruct((3, LENGTH, local_width), BF16),
            jax.ShapeDtypeStruct((3, local_width), F32),
            all_rows,
        ],
        local_heads,
        shard,
        LENGTH,
        [pltpu.VMEM((LENGTH, local_width), BF16)],
    )
    (input_row_grad,) = rows_call(
        3, [after(normed_one_grad, from_a)], gather=False, middle=plain_middle, out_types=[block_f32]
    )
    out_grad = jnp.einsum("lf,ld->fd", attended, branch_grad, preferred_element_type=F32).astype(BF16)
    sum_b = shard_sum(after(dw_own_b, input_row_grad), dw_oth_b)
    from_b = swap_x(sum_b)
    total_b = add_experts(sum_b, from_a)
    peer_b = swap_core(total_b)
    input_row_grad, project_grad, attended, branch_grad = lax.optimization_barrier(
        (input_row_grad, project_grad, attended, branch_grad, sum_b)
    )[:4]
    qkv_own, qkv_more, qkv_send, out_own, out_more, out_send = dense_call(
        jnp.reshape(c, (1,)).astype(jnp.int32), normed, project_grad, attended, branch_grad, shard
    )

    qkv_peer, out_peer = swap_core(qkv_send), swap_core(out_send)
    total_s = add_experts(after(sum_s, qkv_send, total_b), from_s, flip=True)
    peer_s = swap_core(total_s)

    def fsdp_part(own, more, peer, shard_axis):
        own, more, peer = lax.optimization_barrier((own, more, peer, total_s))[:3]
        more = add(more, lax.slice_in_dim(peer, shard, width, axis=shard_axis))
        own = add(own, lax.slice_in_dim(peer, 0, shard, axis=shard_axis))
        return reduce_fsdp(own, more, f, shard_axis, add), more

    (qkv_part, qkv_both), (out_part, out_both) = (
        fsdp_part(qkv_own, qkv_more, qkv_peer, 1),
        fsdp_part(out_own, out_more, out_peer, 1),
    )

    input_row_grad = after(input_row_grad, qkv_both, out_both)
    scaled_one = input_row_grad * gains[0]
    input_grad = hidden_grad + inverse_one * (
        scaled_one
        - inputs_f
        * inverse_one
        * inverse_one
        * jnp.mean(scaled_one * inputs_f, axis=-1, keepdims=True)
    )
    gain_one_grad = jnp.sum(input_row_grad * inputs_f * inverse_one, axis=0)

    mixes = [lax.optimization_barrier((row[0], row[1], qkv_send))[:2] for row in (rows_a, rows_s, rows_b)]
    mixer_peer = swap_core(sum_call([mix[1] for mix in mixes], 5))
    mixer = sum_call([mix[0] for mix in mixes] + [mixer_peer], 5)
    mixer_local = lax.psum_scatter(mixer, "tensor", scatter_dimension=0, tiled=True)

    per_shard = HEAD_DIM // owners
    bias_parts = jnp.moveaxis(bias_grad.reshape(3, local_heads, owners, per_shard), 2, 0).reshape(owners, -1)
    bias_parts = jnp.pad(jnp.roll(bias_parts, -f, axis=0), ((0, 0), (0, shard - 3 * local_heads * per_shard)))
    small_sums = jnp.concatenate([router_grad, gain_one_grad[None], gain_two_grad[None]], axis=0)
    small_here = sum_small(small_sums, bias_parts.reshape(1, width), f, shard)
    small_sums = small_here + swap_x(small_here)
    bias_out = small_sums[11, : 3 * local_heads * per_shard].reshape(3, local_heads, per_shard)

    shared_up_out, shared_down_out = shared_call(after(total_s, qkv_part, out_part), peer_s, c, x)
    own_first, peer_first = EXPERTS // 2 * c, EXPERTS // 2 * (1 - c)
    gate_up_out = place_call(after(total_b, shared_up_out), own_first + 2 * (1 - x), (0, 2))
    gate_up_out = place_call(peer_b, peer_first + 2 * (1 - x), (0, 2), gate_up_out)
    down_out = place_call(total_b, own_first + 2 * (1 - x), (2, 1))
    down_out = place_call(peer_b, peer_first + 2 * (1 - x), (2, 1), down_out)
    total_a = add_experts(after(sum_a, qkv_part, out_part, gate_up_out, down_out, small_here), from_b)
    peer_a = swap_core(total_a)

    gate_up_out = place_call(total_a, own_first + 2 * x, (0, 2), gate_up_out)
    down_out = place_call(total_a, own_first + 2 * x, (2, 1), down_out)

    def core_join(part, hidden_axis):
        part = add(part, after(swap_x(part), gate_up_out, down_out))
        peer = swap_core(part)
        return jnp.where(
            c == 0,
            jnp.concatenate([part, peer], axis=hidden_axis),
            jnp.concatenate([peer, part], axis=hidden_axis),
        ).astype(F32)

    qkv_out, out_out = core_join(qkv_part, 2), core_join(out_part, 0)
    result = turn_back((hidden_rows + after(mixer_local, qkv_out).astype(F32)).astype(BF16))
    gate_up_out = place_call(peer_a, peer_first + 2 * x, (0, 2), gate_up_out)
    gate_up_out = jnp.transpose(gate_up_out, (0, 3, 1, 2))
    down_out = place_call(peer_a, peer_first + 2 * x, (2, 1), down_out).reshape(EXPERTS, hidden, shard)

    return (
        result,
        turn_back(input_grad),
        small_sums[9:11],
        qkv_out,
        bias_out,
        out_out,
        small_sums[:EXPERTS].T,
        small_sums[EXPERTS],
        gate_up_out,
        down_out,
        shared_up_out,
        shared_down_out,
    )


def solution(mesh):
    in_specs = (
        P(("rep", "fsdp", "tensor"), None),
        P(("rep", "fsdp", "tensor"), None),
        P(("rep", "fsdp"), None),
        P(("rep", "fsdp"), None),
        P(None, "fsdp"),
        P(None, "fsdp", "tensor"),
        P(None, "tensor", "fsdp"),
        P("tensor", "fsdp"),
        P("fsdp", None),
        P("fsdp"),
        P(None, "fsdp", None, "tensor"),
        P(None, "tensor", "fsdp"),
        P("fsdp", None, "tensor"),
        P("tensor", "fsdp"),
    )
    out_specs = (
        P(("rep", "fsdp", "tensor"), None),
        P(("rep", "fsdp", "tensor"), None),
        P(None, "fsdp"),
        P(None, "fsdp", "tensor"),
        P(None, "tensor", "fsdp"),
        P("tensor", "fsdp"),
        P("fsdp", None),
        P("fsdp"),
        P(None, "fsdp", None, "tensor"),
        P(None, "tensor", "fsdp"),
        P("fsdp", None, "tensor"),
        P("tensor", "fsdp"),
    )
    return jax.shard_map(shards, mesh=mesh, in_specs=in_specs, out_specs=out_specs, check_vma=False)
```

```python
import functools

import jax
import jax.numpy as jnp
from jax import lax
from jax.experimental import pallas as pl
from jax.experimental.pallas import tpu as pltpu
from jax.sharding import PartitionSpec as P

HEAD_DIM = 128
EXPERTS = 8
LENGTH = 640
PIECE = 256
EPSILON = 1e-06
BF16 = jnp.bfloat16
F32 = jnp.float32
COLS = 256
MESH = pl.DeviceIdType.MESH
CHEAP = pl.CostEstimate(flops=1, bytes_accessed=1, transcendentals=0)


def rope_tables(length, head_dim):
    half_dim = head_dim // 2
    frequency = 1000000.0 ** (-jnp.arange(half_dim, dtype=F32) * (2.0 / head_dim))
    angles = jnp.arange(length, dtype=F32)[:, None] * frequency[None, :]
    return (jnp.cos(angles), jnp.sin(angles))


def after(value, *others):
    return lax.optimization_barrier((value,) + others)[0]


def swap_y(a):
    return lax.ppermute(a, "fsdp", [(0, 1), (1, 0)])


def swap_x(a):
    n = lax.axis_size("rep")
    return lax.ppermute(a, "rep", [(i, i ^ 2) for i in range(n)])


def swap_core(a):
    n = lax.axis_size("rep")
    return lax.ppermute(a, "rep", [(i, i ^ 1) for i in range(n)])


CHUNK = 16


def device(axis, index):
    return {axis: index}


def rows_kernel(
    n, rows, part_count, with_core_in, with_thin, with_scatter, with_gather, with_core_out, middle, extra_count, extra_out, bulk_count, *refs
):
    refs = list(refs)
    take = refs.pop
    parts = [take(0) for _ in range(part_count)]
    peer_parts = [take(0) for _ in range(part_count)] if with_core_in else None
    thin, thin_peer, thin_matrix = (take(0), take(0), take(0)) if with_thin else (None, None, None)
    extras = [take(0) for _ in range(extra_count)]
    bulk_src = [take(0) for _ in range(bulk_count)]
    outs = [take(0) for _ in range(extra_out)]
    full = take(0) if with_gather else None
    full_peer = take(0) if with_core_out else None
    bulk_dst = [take(0) for _ in range(bulk_count)]
    chunks = rows // CHUNK
    z = lax.axis_index("tensor")
    r = lax.axis_index("rep")
    core = r + 1 - 2 * lax.rem(r, 2)
    has_left, has_right = z > 0, z < n - 1
    pairs = with_core_in or with_core_out
    if bulk_count:
        bulk_send, bulk_recv = take(0), take(0)
    if with_core_in:
        core_src, core_buf, core_in_send, core_in_recv = take(0), take(0), take(0), take(0)
    if with_scatter:
        in_bufs, out_bufs = (take(0), take(0)), (take(0), take(0))
        sc_send, sc_recv = take(0), take(0)
    if with_gather:
        ga_send, ga_recv = take(0), take(0)
    if with_core_out:
        core_out_send, core_out_recv = take(0), take(0)

    barrier = pltpu.get_barrier_semaphore()

    @pl.when(has_left)
    def _():
        pl.semaphore_signal(barrier, inc=1, device_id=device("tensor", z - 1), device_id_type=MESH)

    @pl.when(has_right)
    def _():
        pl.semaphore_signal(barrier, inc=1, device_id=device("tensor", z + 1), device_id_type=MESH)

    if pairs:
        pl.semaphore_signal(barrier, inc=1, device_id=device("rep", core), device_id_type=MESH)
    across = r + 2 - 4 * (r // 2)
    if bulk_count:
        pl.semaphore_signal(barrier, inc=1, device_id=device("rep", across), device_id_type=MESH)
    greeted = jnp.where(has_left, 1, 0) + jnp.where(has_right, 1, 0) + int(pairs) + int(bulk_count > 0)
    pl.semaphore_wait(barrier, greeted)

    def chunk_at(block, i):
        return pl.ds(pl.multiple_of(block * rows + i * CHUNK, CHUNK), CHUNK)

    def chunk_in(i):
        return pl.ds(pl.multiple_of(i * CHUNK, CHUNK), CHUNK)

    def remote(src, dst, send, recv, axis, index):
        return pltpu.make_async_remote_copy(
            src_ref=src, dst_ref=dst, send_sem=send, recv_sem=recv,
            device_id=device(axis, index), device_id_type=MESH,
        )

    def bulk_copy(k):
        return remote(bulk_src[k], bulk_dst[k], bulk_send.at[k], bulk_recv.at[k], "rep", across)

    for k in range(bulk_count):
        bulk_copy(k).start()

    def core_in_copy(block, i):
        here = chunk_at(block, i)
        return remote(
            core_src.at[here], core_buf.at[here], core_in_send.at[block, i], core_in_recv.at[block, i], "rep", core
        )

    def scatter_copy(way, m, i):
        here = chunk_in(i)
        return remote(
            out_bufs[way].at[m, here], in_bufs[way].at[m, here], sc_send.at[way, m, i], sc_recv.at[way, m, i],
            "tensor", z + 1 - 2 * way,
        )

    def gather_copy(way, k, i):
        here = chunk_at(z - k + 2 * k * way, i)
        return remote(
            full.at[here], full.at[here], ga_send.at[way, k, i], ga_recv.at[way, k, i], "tensor", z + 1 - 2 * way
        )

    def core_out_copy(block, i):
        here = chunk_at(block, i)
        return remote(
            full.at[here], full_peer.at[here], core_out_send.at[block, i], core_out_recv.at[block, i], "rep", core
        )

    def all_chunks(body):
        def step(i, carry):
            body(i)
            return carry

        lax.fori_loop(0, chunks, step, 0)

    def sum_terms(arrays, small, here):
        value = arrays[0][here, :].astype(F32)
        for more in arrays[1:]:
            value = value + more[here, :].astype(F32)
        if with_thin:
            value = value + dot_nn(small[here, :], thin_matrix[...])
        return value

    def core_in_step(i):
        @pl.when(i < chunks)
        def _():
            for block in range(n):
                here = chunk_at(block, i)
                core_src[here, :] = sum_terms(peer_parts, thin_peer, here).astype(BF16)
                core_in_copy(block, i).start()

    ahead = 2
    if with_core_in:
        for i in range(ahead):
            core_in_step(i)

    def term(block, i):
        here = chunk_at(block, i)
        value = sum_terms(parts, thin, here)
        if with_core_in:
            core_in_copy(block, i).wait_recv()
            value = value + core_buf[here, :].astype(F32)
        return value

    def inside(i):
        return (i >= 0) & (i < chunks)

    def scatter_step(way, i, has_source, does_send):
        for m in range(n - 1):
            scatter_message(way, m, i - m, has_source, does_send(n - 1 - m if way == 0 else m))

    def scatter_message(way, m, i, has_source, does_send):
        block = n - 1 - m if way == 0 else m
        here = chunk_in(i)

        @pl.when(inside(i) & does_send)
        def _():
            value = term(block, i)

            @pl.when(has_source)
            def _():
                scatter_copy(way, m, i).wait_recv()
                out_bufs[way][m, here, :] = (value + in_bufs[way][m, here, :].astype(F32)).astype(BF16)

            @pl.when(jnp.logical_not(has_source))
            def _():
                out_bufs[way][m, here, :] = value.astype(BF16)

            scatter_copy(way, m, i).start()

    def own_step(i):
        @pl.when(inside(i))
        def _():
            here = chunk_in(i)
            if with_scatter:
                total[...] = term(z, i)

                @pl.when(has_left)
                def _():
                    m = n - 1 - z
                    scatter_copy(0, m, i).wait_recv()
                    total[...] += in_bufs[0][m, here, :].astype(F32)

                @pl.when(has_right)
                def _():
                    scatter_copy(1, z, i).wait_recv()
                    total[...] += in_bufs[1][z, here, :].astype(F32)

                sent = middle(total[...], here, extras, outs)
            else:
                sent = parts[0][here, :]
            if with_gather:
                full[chunk_at(z, i), :] = sent

                @pl.when(has_right)
                def _():
                    gather_copy(0, 0, i).start()

                @pl.when(has_left)
                def _():
                    gather_copy(1, 0, i).start()

                if with_core_out:
                    core_out_copy(z, i).start()

    def gather_step(k, i):
        for way in range(2):
            comes = z - k >= 0 if way == 0 else z + k <= n - 1
            goes = has_right if way == 0 else has_left

            @pl.when(inside(i) & comes)
            def _():
                landed = full.at[chunk_at(z - k + 2 * k * way, i)]
                remote(
                    landed, landed, ga_send.at[way, k - 1, i], ga_recv.at[way, k - 1, i], "tensor", z + 1 - 2 * way
                ).wait_recv()
                if k < n - 1:

                    @pl.when(goes)
                    def _():
                        gather_copy(way, k, i).start()

                if with_core_out:
                    core_out_copy(z - k + 2 * k * way, i).start()

    lead = n - 1 if with_scatter else 0
    if with_scatter:
        total = take(0)

    def tick(t, carry):
        if with_core_in:
            core_in_step(t + ahead)
        if with_scatter:
            scatter_step(0, t - z, has_left, lambda block: block > z)
            scatter_step(1, t - (n - 1 - z), has_right, lambda block: block < z)
        own_step(t - lead)
        if with_gather:
            for k in range(1, n):
                gather_step(k, t - lead - k)
        return carry

    lax.fori_loop(0, chunks + lead + (n - 1 if with_gather else 0), tick, 0)

    @all_chunks
    def _(i):
        if with_core_in:
            for block in range(n):
                core_in_copy(block, i).wait_send()
        for way in range(2):
            goes = has_right if way == 0 else has_left
            if with_scatter:
                for m in range(n - 1):
                    block = n - 1 - m if way == 0 else m

                    @pl.when(goes & ((block > z) if way == 0 else (block < z)))
                    def _():
                        scatter_copy(way, m, i).wait_send()

            if with_gather:
                for k in range(n - 1):
                    has = z - k >= 0 if way == 0 else z + k <= n - 1

                    @pl.when(goes & has)
                    def _():
                        gather_copy(way, k, i).wait_send()

        if with_core_out:
            for block in range(n):
                core_out_copy(block, i).wait_send()
                core_out_copy(block, i).wait_recv()

    for k in range(bulk_count):
        bulk_copy(k).wait()


def rows_call(
    collective_id, parts, peer_parts=(), thin=(), extras=(), bulk=(), scatter=True, gather=True, core_out=False, middle=None,
    out_types=(),
):
    n = lax.axis_size("tensor")
    width = parts[0].shape[1]
    rows = parts[0].shape[0] // n if scatter else parts[0].shape[0]
    chunks = rows // CHUNK
    vmem_spec = pl.BlockSpec(memory_space=pltpu.VMEM)
    full = jax.ShapeDtypeStruct((n * rows, width), BF16)
    out_shape = list(out_types) + ([full] if gather else []) + ([full] if core_out else [])
    vmem_outs = len(out_shape)
    out_shape += [jax.ShapeDtypeStruct(a.shape, a.dtype) for a in bulk]
    any_spec = pl.BlockSpec(memory_space=pl.ANY)
    scratch = [pltpu.SemaphoreType.DMA((len(bulk),))] * 2 if bulk else []
    if peer_parts:
        scratch += [pltpu.VMEM((n * rows, width), BF16)] * 2 + [pltpu.SemaphoreType.DMA((n, chunks))] * 2
    if scatter:
        scratch += [pltpu.VMEM((n - 1, rows, width), BF16)] * 4
        scratch += [pltpu.SemaphoreType.DMA((2, n - 1, chunks))] * 2
    if gather:
        scratch += [pltpu.SemaphoreType.DMA((2, n - 1, chunks))] * 2
    if core_out:
        scratch += [pltpu.SemaphoreType.DMA((n, chunks))] * 2
    if scatter:
        scratch += [pltpu.VMEM((CHUNK, width), F32)]
    operands = [*parts, *peer_parts, *thin, *extras]
    vmem_ins = len(operands)
    operands += list(bulk)
    return pl.pallas_call(
        functools.partial(
            rows_kernel, n, rows, len(parts), bool(peer_parts), bool(thin), scatter, gather, core_out, middle, len(extras), len(out_types), len(bulk)
        ),
        out_shape=out_shape,
        in_specs=[vmem_spec] * vmem_ins + [any_spec] * len(bulk),
        out_specs=[vmem_spec] * vmem_outs + [any_spec] * len(bulk),
        scratch_shapes=scratch,
        compiler_params=pltpu.CompilerParams(
            collective_id=collective_id, has_side_effects=True, vmem_limit_bytes=56 * 2**20
        ),
        cost_estimate=CHEAP,
        name="rows",
    )(*operands)


def norm_middle(total, here, extras, outs):
    inputs, gain = extras
    hidden = inputs[here, :].astype(F32) + total
    outs[0][here, :] = hidden
    inverse = lax.rsqrt(jnp.mean(hidden * hidden, axis=-1, keepdims=True) + EPSILON)
    return (hidden * inverse * gain[...]).astype(BF16)


def norm_back_middle(total, here, extras, outs):
    hidden_ref, cot, gain = extras
    hidden = hidden_ref[here, :]
    inverse = lax.rsqrt(jnp.mean(hidden * hidden, axis=-1, keepdims=True) + EPSILON)
    scaled = total * gain[...]
    grad = cot[here, :].astype(F32) + inverse * (
        scaled - hidden * inverse * inverse * jnp.mean(scaled * hidden, axis=-1, keepdims=True)
    )
    outs[0][here, :] = total
    outs[1][here, :] = grad
    return grad.astype(BF16)


def plain_middle(total, here, extras, outs):
    outs[0][here, :] = total


def others_of(own, f, axis):
    if lax.axis_size("fsdp") == 2:
        return swap_y(own)
    whole = lax.all_gather(own, "fsdp", axis=axis, tiled=True)
    size = own.shape[axis]
    turned = jnp.roll(whole, -f * size, axis=axis)
    return lax.slice_in_dim(turned, size, whole.shape[axis], axis=axis)


def reduce_fsdp(own, other, f, axis, add):
    if lax.axis_size("fsdp") == 2:
        return add(own, swap_y(other))
    whole = jnp.roll(jnp.concatenate([own, other], axis=axis), f * own.shape[axis], axis=axis)
    return lax.psum_scatter(whole, "fsdp", scatter_dimension=axis, tiled=True)


def sum_small(values, per_tensor, f, shard):
    total = sum_rep_first(jnp.concatenate([sum_tensor(values), per_tensor], axis=0))
    if lax.axis_size("fsdp") == 2:
        total = total[:, :shard] + swap_y(total[:, shard:])
    else:
        whole = jnp.roll(total, f * shard, axis=1)
        total = lax.psum_scatter(whole, "fsdp", scatter_dimension=1, tiled=True)
    return total


def sum_rep_first(total):
    return total + swap_core(total)


def sum_tensor(total):
    n = lax.axis_size("tensor")
    step = 1
    while step < n:
        total = total + lax.ppermute(total, "tensor", [(i, i ^ step) for i in range(n)])
        step *= 2
    return total


def dot_nt(a, b):
    return lax.dot_general(a, b, (((1,), (1,)), ((), ())), preferred_element_type=F32)


def dot_nn(a, b):
    return lax.dot_general(a, b, (((1,), (0,)), ((), ())), preferred_element_type=F32)


def mask_rows(starts, length):
    key = lax.broadcasted_iota(jnp.int32, (length, length), 0)
    query = lax.broadcasted_iota(jnp.int32, (length, length), 1)
    visible = key <= query
    for piece in range(2):
        first = starts[0, piece]
        visible |= (jnp.minimum(key, query) >= first) & (jnp.maximum(key, query) < first + PIECE)
    return jnp.where(visible, 0.0, -1e30).astype(F32)


def attend_kernel(
    heads, own_width, starts, rows, w_own, w_oth, bias, cos, sin, out_own, out_oth,
    q_out, k_out, v_out, attended, stats, part, mask,
):
    length = rows.shape[0]
    scale = HEAD_DIM ** (-0.5)
    for c, out in ((0, q_out), (1, k_out), (2, v_out)):
        project = dot_nn(rows[:, :own_width], w_own[c]) + dot_nn(rows[:, own_width:], w_oth[c]) + bias[c : c + 1, :]
        for h in range(heads):
            here = slice(h * HEAD_DIM, (h + 1) * HEAD_DIM)
            values = project[:, here]
            if c < 2:
                values = values * cos[...] + pltpu.roll(values, HEAD_DIM // 2, 1) * sin[...]
            out[:, here] = values.astype(BF16)
    mask[...] = mask_rows(starts, length)

    def one_head(h, carry):
        here = pl.ds(pl.multiple_of(h * HEAD_DIM, HEAD_DIM), HEAD_DIM)
        scores = dot_nt(k_out[:, here], q_out[:, here]) * scale + mask[...]
        top = jnp.max(scores, axis=0, keepdims=True)
        weights = jnp.exp(scores - top)
        inverse = 1.0 / jnp.sum(weights, axis=0, keepdims=True)
        probs = (weights * inverse).astype(BF16)
        attended[:, here] = dot_nn(v_out[:, here].T, probs).T.astype(BF16)
        stats[pl.ds(h, 1), :] = top
        stats[pl.ds(heads + h, 1), :] = inverse
        return carry

    lax.fori_loop(0, heads, one_head, 0)
    part[:, :own_width] = dot_nn(attended[...], out_own[...]).astype(BF16)
    part[:, own_width:] = dot_nn(attended[...], out_oth[...]).astype(BF16)


def attend_back_kernel(
    heads, own_width, starts, grad, w_own, w_oth, cos, sin, out_own, out_oth, q, k, v, stats,
    project_grad, bias_grad, rows_grad, mask, attended_grad,
):
    length = grad.shape[0]
    scale = HEAD_DIM ** (-0.5)
    attended_grad[...] = (
        dot_nt(grad[:, :own_width], out_own[...]) + dot_nt(grad[:, own_width:], out_oth[...])
    ).astype(BF16)
    mask[...] = mask_rows(starts, length)

    def turn_back(values):
        return values * cos[...] - pltpu.roll(values, HEAD_DIM // 2, 1) * sin[...]

    def one_head(h, carry):
        here = pl.ds(pl.multiple_of(h * HEAD_DIM, HEAD_DIM), HEAD_DIM)
        queries, keys, grads = q[:, here], k[:, here], attended_grad[:, here]
        scores = dot_nt(keys, queries) * scale + mask[...]
        probs = jnp.exp(scores - stats[pl.ds(h, 1), :]) * stats[pl.ds(heads + h, 1), :]
        value_grad = dot_nn(probs.astype(BF16), grads)
        probs_grad = dot_nt(v[:, here], grads)
        mean = jnp.sum(probs * probs_grad, axis=0, keepdims=True)
        score_grad = (probs * (probs_grad - mean)).astype(BF16)
        key_grad = dot_nn(score_grad, queries) * scale
        query_grad = dot_nn(score_grad.T, keys) * scale
        project_grad[0, :, here] = turn_back(query_grad).astype(BF16)
        project_grad[1, :, here] = turn_back(key_grad).astype(BF16)
        project_grad[2, :, here] = value_grad.astype(BF16)
        return carry

    lax.fori_loop(0, heads, one_head, 0)
    total_own = total_oth = None
    for c in range(3):
        grads = project_grad[c]
        bias_grad[c : c + 1, :] = jnp.sum(grads.astype(F32), axis=0, keepdims=True)
        own, oth = dot_nt(grads, w_own[c]), dot_nt(grads, w_oth[c])
        total_own = own if c == 0 else total_own + own
        total_oth = oth if c == 0 else total_oth + oth
    rows_grad[:, :own_width] = total_own.astype(BF16)
    rows_grad[:, own_width:] = total_oth.astype(BF16)


def attention_call(kernel, name, operands, out_shape, heads, own_width, length, more_scratch=()):
    vmem_spec = pl.BlockSpec(memory_space=pltpu.VMEM)
    return pl.pallas_call(
        functools.partial(kernel, heads, own_width),
        out_shape=out_shape,
        in_specs=[pl.BlockSpec(memory_space=pltpu.SMEM)] + [vmem_spec] * (len(operands) - 1),
        out_specs=[vmem_spec] * len(out_shape),
        scratch_shapes=[pltpu.VMEM((length, length), F32), *more_scratch],
        cost_estimate=CHEAP,
        compiler_params=pltpu.CompilerParams(vmem_limit_bytes=56 * 2**20),
        name=name,
    )(*operands)


def experts_kernel(rows, width, own_width, hidden, direct, *refs):
    if direct:
        first, x0, x1, c0, c10, c11, gate, gate_up, down, w_oth, *refs = refs
    else:
        x0, x1, c0, c10, c11, gate, w_own, w_oth, *refs = refs
    dw_own, dw_oth, mix0, mix1, ng0, ng1, gate_grad, *refs = refs
    xv, cv, wgu, wd, ga, pre, ga_t, pre_t, gu_all, st_mix, st_ng, st_dw, w_sem, x_sem, c_sem, out_sem, dw_sem = refs
    seq = rows // 2
    both = 2 * hidden
    oth_width = width - own_width

    def w_copies(part):
        copies = []
        for k in range(2):
            if direct:
                own = gate_up.at[first[0] + k, part] if part < 2 else down.at[first[0] + k]
            else:
                own = w_own.at[k, part]
            to = wd.at[pl.ds(k * hidden, hidden)] if part == 2 else wgu.at[pl.ds(part * both + k * hidden, hidden)]
            copies.append(pltpu.make_async_copy(own, to.at[:, pl.ds(0, own_width)], w_sem.at[part, k, 0]))
            copies.append(
                pltpu.make_async_copy(w_oth.at[k, part], to.at[:, pl.ds(own_width, oth_width)], w_sem.at[part, k, 1])
            )
        return copies

    def row_copies(sources, to, sem):
        return [
            pltpu.make_async_copy(sources[s], to.at[pl.ds(s * seq, seq)], sem.at[s]) for s in range(2)
        ]

    x_copies = row_copies((x0, x1), xv, x_sem)
    c_copies = [pltpu.make_async_copy(c0, cv.at[pl.ds(0, seq)], c_sem.at[0])]
    for i, part in enumerate((c10, c11)):
        here = pl.ds(seq + i * part.shape[0], part.shape[0])
        c_copies.append(pltpu.make_async_copy(part, cv.at[here], c_sem.at[1 + i]))
    for_gate_up = [x_copies[0], *w_copies(0), *w_copies(1)]
    for_down = [*w_copies(2), *c_copies]
    for copy in [*for_gate_up, x_copies[1], *for_down]:
        copy.start()

    def gate_up_tile(t, carry):
        here = pl.ds(pl.multiple_of(t * COLS, COLS), COLS)
        gu_all[:, here] = dot_nt(wgu[...], xv[here, :])
        return carry

    def token_tile(t, carry):
        here = pl.ds(pl.multiple_of(t * COLS, COLS), COLS)
        h = dot_nt(wd[...], cv[here, :])
        gu = gu_all[:, here]
        g, u = gu[:both], gu[both:]
        sig = jax.nn.sigmoid(g)
        act = g * sig * u
        product = act * h
        scale_rows = []
        for k in range(2):
            part = product[k * hidden : (k + 1) * hidden]
            gate_grad[pl.ds(k, 1), here] = jnp.sum(part, axis=0, keepdims=True)
            scale_rows.append(jnp.broadcast_to(gate[pl.ds(k, 1), here], (hidden, COLS)))
        scale = jnp.concatenate(scale_rows, axis=0)
        back = scale * h
        ga_here = (scale * act).astype(BF16)
        pg_here = (back * u * sig * (1.0 + g * (1.0 - sig))).astype(BF16)
        pu_here = (back * g * sig).astype(BF16)
        ga[:, here] = ga_here
        pre[:both, here] = pg_here
        pre[both:, here] = pu_here
        ga_t[here, :] = ga_here.T
        pre_t[here, :both] = pg_here.T
        pre_t[here, both:] = pu_here.T
        return carry

    for copy in for_gate_up:
        copy.wait()
    lax.fori_loop(0, seq // COLS, gate_up_tile, 0)
    x_copies[1].wait()
    lax.fori_loop(seq // COLS, rows // COLS, gate_up_tile, 0)
    for copy in for_down:
        copy.wait()
    lax.fori_loop(0, rows // COLS, token_tile, 0)

    def row_outs(slot, cols):
        return [
            pltpu.make_async_copy(stage.at[slot, pl.ds(s * seq, seq)], outs[s].at[:, cols], out_sem.at[slot, i, s])
            for i, (stage, outs) in enumerate(((st_mix, (mix0, mix1)), (st_ng, (ng0, ng1))))
            for s in range(2)
        ]

    def weight_outs(slot, dst, cols):
        return [
            pltpu.make_async_copy(
                st_dw.at[slot, pl.ds((part * 2 + k) * hidden, hidden)], dst.at[k, part, :, cols], dw_sem.at[slot, part, k]
            )
            for part in range(3)
            for k in range(2)
        ]

    def wait_slot(slot):
        for copy in row_outs(slot, pl.ds(0, COLS)) + weight_outs(slot, dw_own, pl.ds(0, COLS)):
            copy.wait()

    def column_tile(n, slot, src_col, dst, dst_col):
        cols = pl.ds(pl.multiple_of(src_col, COLS), COLS)

        @pl.when(n >= 2)
        def _():
            wait_slot(slot)

        st_dw[slot, : 2 * both] = dot_nn(pre[...], xv[:, cols]).astype(BF16)
        st_dw[slot, 2 * both :] = dot_nn(ga[...], cv[:, cols]).astype(BF16)
        for copy in weight_outs(slot, dst, pl.ds(pl.multiple_of(dst_col, COLS), COLS)):
            copy.start()
        st_ng[slot] = dot_nn(pre_t[...], wgu[:, cols]).astype(BF16)
        st_mix[slot] = dot_nn(ga_t[...], wd[:, cols]).astype(BF16)
        for copy in row_outs(slot, cols):
            copy.start()

    oth_tiles, own_tiles = oth_width // COLS, own_width // COLS

    def oth_tile(n, carry):
        column_tile(n, lax.rem(n, 2), own_width + n * COLS, dw_oth, n * COLS)
        return carry

    def own_tile(n, carry):
        column_tile(n + oth_tiles, lax.rem(n + oth_tiles, 2), n * COLS, dw_own, n * COLS)
        return carry

    lax.fori_loop(0, oth_tiles, oth_tile, 0)
    lax.fori_loop(0, own_tiles, own_tile, 0)
    for slot in range(2):
        wait_slot(slot)


def experts_call(x0, x1, c0, c1, gate, w_own, w_oth):
    direct = isinstance(w_own, tuple)
    seq, width = x0.shape
    rows = 2 * seq
    hidden, own_width = (w_own[1] if direct else w_own).shape[2:]
    smem_spec = pl.BlockSpec(memory_space=pltpu.SMEM)
    own_operands = w_own[1:] if direct else (w_own,)
    any_spec = pl.BlockSpec(memory_space=pl.ANY)
    vmem_spec = pl.BlockSpec(memory_space=pltpu.VMEM)
    out_rows = jax.ShapeDtypeStruct((seq, width), BF16)
    return pl.pallas_call(
        functools.partial(experts_kernel, rows, width, own_width, hidden, direct),
        out_shape=[
            jax.ShapeDtypeStruct((2, 3, hidden, own_width), BF16),
            jax.ShapeDtypeStruct((2, 3, hidden, width - own_width), BF16),
            out_rows, out_rows, out_rows, out_rows,
            jax.ShapeDtypeStruct((8, rows), F32),
        ],
        in_specs=[smem_spec] * direct + [any_spec] * 5 + [vmem_spec] + [any_spec] * (len(own_operands) + 1),
        out_specs=[any_spec] * 6 + [vmem_spec],
        scratch_shapes=[
            pltpu.VMEM((rows, width), BF16),
            pltpu.VMEM((rows, width), BF16),
            pltpu.VMEM((4 * hidden, width), BF16),
            pltpu.VMEM((2 * hidden, width), BF16),
            pltpu.VMEM((2 * hidden, rows), BF16),
            pltpu.VMEM((4 * hidden, rows), BF16),
            pltpu.VMEM((rows, 2 * hidden), BF16),
            pltpu.VMEM((rows, 4 * hidden), BF16),
            pltpu.VMEM((4 * hidden, rows), F32),
            pltpu.VMEM((2, rows, COLS), BF16),
            pltpu.VMEM((2, rows, COLS), BF16),
            pltpu.VMEM((2, 6 * hidden, COLS), BF16),
            pltpu.SemaphoreType.DMA((3, 2, 2)),
            pltpu.SemaphoreType.DMA((2,)),
            pltpu.SemaphoreType.DMA((3,)),
            pltpu.SemaphoreType.DMA((2, 2, 2)),
            pltpu.SemaphoreType.DMA((2, 3, 2)),
        ],
        cost_estimate=CHEAP,
        compiler_params=pltpu.CompilerParams(vmem_limit_bytes=58 * 2**20),
        name="experts",
    )(*([w_own[0]] if direct else []), x0, x1, c0, *c1, gate, *own_operands, w_oth)


def sum_kernel(*refs):
    total = refs[0][...].astype(F32)
    for ref in refs[1:-1]:
        total = total + ref[...].astype(F32)
    refs[-1][...] = total.astype(BF16)


def sum_call(arrays, steps, flip=-1):
    rows, columns = arrays[0].shape
    block = (rows // steps, columns)

    def spec(k):
        if k == flip:
            return pl.BlockSpec(block, lambda i: (lax.rem(i + steps // 2, steps), 0))
        return pl.BlockSpec(block, lambda i: (i, 0))

    return pl.pallas_call(
        sum_kernel,
        out_shape=jax.ShapeDtypeStruct((rows, columns), BF16),
        grid=(steps,),
        in_specs=[spec(k) for k in range(len(arrays))],
        out_specs=spec(-2),
        cost_estimate=CHEAP,
        compiler_params=pltpu.CompilerParams(vmem_limit_bytes=40 * 2**20),
        name="sums",
    )(*arrays)


def add_experts(one, two, flip=False):
    flat = [a.reshape(-1, a.shape[-1]) for a in (one, two)]
    return sum_call(flat, 4, 1 if flip else -1).reshape(one.shape)


def dense_kernel(half, own_width, core, rows, project_grad, attended, branch_grad, *outs):
    qkv_own, qkv_oth, qkv_send, out_own, out_oth, out_send, rows_t = outs
    rows_t[...] = rows[...].T
    for keep in (False, True):
        cols = pl.ds(pl.multiple_of((core[0] if keep else 1 - core[0]) * half, half), half)
        for c in range(3):
            grad = dot_nn(rows_t[...], project_grad[c, :, cols]).astype(BF16)
            if keep:
                qkv_own[c] = grad[:own_width]
                qkv_oth[c] = grad[own_width:]
            else:
                qkv_send[c] = grad
        grad = dot_nn(attended[:, cols].T, branch_grad[...]).astype(BF16)
        if keep:
            out_own[...] = grad[:, :own_width]
            out_oth[...] = grad[:, own_width:]
        else:
            out_send[...] = grad


def dense_call(core, rows, project_grad, attended, branch_grad, own_width):
    length, width = rows.shape
    half = attended.shape[1] // 2
    vmem_spec = pl.BlockSpec(memory_space=pltpu.VMEM)
    shapes = [(3, own_width, half), (3, width - own_width, half), (3, width, half)]
    shapes += [(half, own_width), (half, width - own_width), (half, width)]
    return pl.pallas_call(
        functools.partial(dense_kernel, half, own_width),
        out_shape=[jax.ShapeDtypeStruct(shape, BF16) for shape in shapes],
        in_specs=[pl.BlockSpec(memory_space=pltpu.SMEM)] + [vmem_spec] * 4,
        out_specs=[vmem_spec] * 6,
        scratch_shapes=[pltpu.VMEM((width, length), BF16)],
        cost_estimate=CHEAP,
        compiler_params=pltpu.CompilerParams(vmem_limit_bytes=48 * 2**20),
        name="dense_grads",
    )(core, rows, project_grad, attended, branch_grad)


def place_kernel(table, source, *refs):
    refs[-1][...] = source[...].astype(F32)


def place_call(source, first, parts, base=None):
    at, length = parts
    count, _, hidden, width = source.shape
    return pl.pallas_call(
        place_kernel,
        out_shape=jax.ShapeDtypeStruct((EXPERTS, length, hidden, width), F32),
        grid_spec=pltpu.PrefetchScalarGridSpec(
            num_scalar_prefetch=1,
            grid=(count, length),
            in_specs=[pl.BlockSpec((1, 1, hidden, width), lambda e, part, tab: (e, at + part, 0, 0))]
            + [pl.BlockSpec(memory_space=pl.ANY)] * (base is not None),
            out_specs=pl.BlockSpec((1, 1, hidden, width), lambda e, part, tab: (tab[0] + e, part, 0, 0)),
        ),
        input_output_aliases={} if base is None else {2: 0},
        cost_estimate=CHEAP,
        compiler_params=pltpu.CompilerParams(vmem_limit_bytes=40 * 2**20),
        name="place",
    )(jnp.reshape(first, (1,)).astype(jnp.int32), source, *([] if base is None else [base]))


def shared_kernel(table, mine, peer, up, down):
    def quarter(q, part):
        block = table[q]
        return jnp.where(table[4 + q] == 0, mine[block, part].astype(F32), peer[block, part].astype(F32))

    for part in range(2):
        up[:, part, :] = jnp.concatenate([quarter(q, part) for q in range(4)], axis=0).T
    down[...] = jnp.concatenate([quarter(q, 2) for q in range(4)], axis=0)


def shared_call(mine, peer, c, x):
    hidden, width = mine.shape[2:]
    q = jnp.arange(4, dtype=jnp.int32)
    table = jnp.concatenate([(q % 2) ^ x, (q // 2 != c).astype(jnp.int32)]).astype(jnp.int32)
    source = pl.BlockSpec((2, 3, hidden, 128), lambda n, tab: (0, 0, 0, n))
    return pl.pallas_call(
        shared_kernel,
        out_shape=[
            jax.ShapeDtypeStruct((width, 2, 4 * hidden), F32),
            jax.ShapeDtypeStruct((4 * hidden, width), F32),
        ],
        grid_spec=pltpu.PrefetchScalarGridSpec(
            num_scalar_prefetch=1,
            grid=(width // 128,),
            in_specs=[source, source],
            out_specs=[
                pl.BlockSpec((128, 2, 4 * hidden), lambda n, tab: (n, 0, 0)),
                pl.BlockSpec((4 * hidden, 128), lambda n, tab: (0, n)),
            ],
        ),
        cost_estimate=CHEAP,
        compiler_params=pltpu.CompilerParams(vmem_limit_bytes=40 * 2**20),
        name="shared",
    )(table, mine, peer)


def shards(
    block_input,
    cotangent,
    piece_starts,
    expert_ids,
    norm_gains,
    qkv_weight,
    qkv_bias,
    out_weight,
    router_weight,
    shared_gate,
    expert_gate_up,
    expert_down,
    shared_gate_up,
    shared_down,
):
    f = lax.axis_index("fsdp")
    owners = lax.axis_size("fsdp")
    r = lax.axis_index("rep")
    c, x = r % 2, r // 2
    shard = norm_gains.shape[1]
    width = owners * shard
    local_width = qkv_weight.shape[2]
    local_heads = local_width // HEAD_DIM
    half_width = local_width // 2
    hidden = expert_gate_up.shape[3]
    scale = HEAD_DIM ** (-0.5)

    def turn(rows):
        return jnp.roll(rows, -f * shard, axis=1)

    def turn_back(rows):
        return jnp.roll(rows, f * shard, axis=1)

    gains = jnp.concatenate([norm_gains, others_of(norm_gains, f, 1)], axis=1).astype(F32)
    cos_table, sin_table = rope_tables(LENGTH, HEAD_DIM)
    inputs = turn(block_input)
    inputs_f = inputs.astype(F32)
    cot = turn(cotangent)
    inverse_one = lax.rsqrt(jnp.mean(inputs_f * inputs_f, axis=-1, keepdims=True) + EPSILON)
    normed_local = (inputs_f * inverse_one * gains[0]).astype(BF16)
    normed = lax.all_gather(normed_local, "tensor", axis=0, tiled=True)
    gate_up_t = jnp.transpose(after(expert_gate_up, normed_local), (0, 2, 3, 1))
    small = jnp.concatenate([after(router_weight, normed_local).T.reshape(-1), shared_gate, qkv_bias.reshape(-1)])
    small_all = jnp.concatenate([small[None], others_of(small[None], f, 0)], axis=0)
    router = jnp.swapaxes(small_all[:, : 9 * shard].reshape(owners, 9, shard), 0, 1).reshape(9, width)
    bias = jnp.roll(small_all[:, 9 * shard :], f, axis=0).reshape(owners, 3, local_heads, -1)
    bias = jnp.moveaxis(bias, 0, 2).reshape(3, local_width).astype(F32)

    quarter = local_width // 4

    def fetch_quarters(weight, hidden_axis, shard_axis):
        mine = lax.dynamic_slice_in_dim(weight, r * quarter, quarter, hidden_axis)
        got = others_of(mine, f, shard_axis)
        pair = jnp.stack([got, swap_x(got)])
        peers = swap_core(pair)
        pair = jnp.where(x == 0, pair, pair[::-1])
        peers = jnp.where(x == 0, peers, peers[::-1])
        order = jnp.where(c == 0, jnp.stack([pair, peers], 1), jnp.stack([peers, pair], 1))
        return jnp.concatenate([order[i, j] for i in range(2) for j in range(2)], axis=hidden_axis), got

    qkv_oth, qkv_got = fetch_quarters(qkv_weight, 2, 1)
    out_oth, out_got = fetch_quarters(out_weight, 0, 1)


    def routed_chunk(first, gate_up_t):
        return jnp.concatenate(
            [
                lax.dynamic_slice_in_dim(gate_up_t, first, 2, 0),
                lax.dynamic_slice_in_dim(expert_down, first, 2, 0)[:, None],
            ],
            axis=1,
        )

    def shared_chunk(q, shared_up_t, shared_down):
        return jnp.concatenate(
            [
                lax.dynamic_slice_in_dim(shared_up_t, q * hidden, hidden, 1),
                lax.dynamic_slice_in_dim(shared_down, q * hidden, hidden, 0)[None],
            ],
            axis=0,
        )[None]

    first_a, first_b = 4 * c + 2 * x, 4 * c + 2 * (1 - x)
    shared_gate_up, shared_down, expert_ids = lax.optimization_barrier(
        (shared_gate_up, shared_down, expert_ids, normed_local)
    )[:3]
    ids_pair = jnp.concatenate([expert_ids, swap_core(expert_ids)], axis=0)
    shared_up_t = jnp.stack([shared_gate_up[:, 0].T, shared_gate_up[:, 1].T])
    own_s = jnp.concatenate([shared_chunk(q, shared_up_t, shared_down) for q in (2 * c + x, 2 * c + 1 - x)], axis=0)
    own_a = routed_chunk(first_a, after(gate_up_t, own_s))
    own_b = (jnp.reshape(first_b, (1,)).astype(jnp.int32), gate_up_t, expert_down)

    oth_a = others_of(after(own_a, qkv_got, out_got), f, 3)
    cos_rows = jnp.concatenate([cos_table, cos_table], axis=1)
    sin_rows = jnp.concatenate([-sin_table, sin_table], axis=1)
    normed = after(normed, own_s, ids_pair, cos_rows, sin_rows, bias, qkv_oth, out_oth)
    cot_rows = lax.all_gather(after(cot, normed), "tensor", axis=0, tiled=True)
    oth_s = others_of(after(own_s, normed), f, 3)

    heads_rows = jax.ShapeDtypeStruct((LENGTH, local_width), BF16)
    all_rows = jax.ShapeDtypeStruct((LENGTH, width), BF16)
    query_rows, key_rows, value_rows, attended, stats, heads_part = attention_call(
        attend_kernel,
        "attend",
        [piece_starts, normed, qkv_weight, qkv_oth, bias, cos_rows, sin_rows, out_weight, out_oth],
        [heads_rows] * 4 + [jax.ShapeDtypeStruct((2 * local_heads, LENGTH), F32), all_rows],
        local_heads,
        shard,
        LENGTH,
    )
    block_f32 = jax.ShapeDtypeStruct(inputs.shape, F32)
    hidden_rows, mixed, mixed_peer = rows_call(
        1, [heads_part], extras=(inputs, gains[1:2]), core_out=True, middle=norm_middle, out_types=[block_f32]
    )
    cot_rows = after(cot_rows, mixed)
    cot_peer = [swap_core(piece) for piece in jnp.split(cot_rows, 2)]
    oth_b = swap_x(after(oth_a, mixed))
    mixed_pair = jnp.concatenate([mixed, mixed_peer], axis=0)

    logits = lax.dot_general(router, mixed_pair, (((1,), (1,)), ((), ())), preferred_element_type=F32)
    router_probs = jax.nn.softmax(logits[:EXPERTS], axis=0)
    shared_scale = jax.nn.sigmoid(logits[EXPERTS:])
    names = jnp.arange(EXPERTS, dtype=jnp.int32)[:, None, None]
    chosen = jnp.any(ids_pair.T[None] == names, axis=1)
    gates = jnp.where(chosen, router_probs, 0.0)

    def gate_rows(first):
        return jnp.pad(lax.dynamic_slice_in_dim(gates, first, 2, 0), ((0, 6), (0, 0)))

    data = (mixed, mixed_peer, cot_rows, cot_peer)
    dw_own_a, dw_oth_a, *rows_a, grad_a = experts_call(*data, gate_rows(first_a), own_a, oth_a)
    shared_rows = after(jnp.broadcast_to(shared_scale, (8, shared_scale.shape[1])), grad_a)
    dw_own_s, dw_oth_s, *rows_s, grad_s = experts_call(*data, shared_rows, own_s, oth_s)
    dw_own_b, dw_oth_b, *rows_b, grad_b = experts_call(
        *data, after(gate_rows(first_b), grad_s), own_b, oth_b
    )

    prob_grad = jnp.zeros_like(router_probs)
    prob_grad = lax.dynamic_update_slice_in_dim(prob_grad, grad_a[:2], first_a, 0)
    prob_grad = lax.dynamic_update_slice_in_dim(prob_grad, grad_b[:2], first_b, 0)
    prob_grad = jnp.where(chosen, prob_grad, 0.0)
    logit_grad = router_probs * (prob_grad - jnp.sum(router_probs * prob_grad, axis=0, keepdims=True))
    scale_logit_grad = (grad_s[0:1] + grad_s[1:2]) * shared_scale * (1.0 - shared_scale)
    small_grad = jnp.concatenate([logit_grad, scale_logit_grad], axis=0)
    high = small_grad.astype(BF16)
    low = (small_grad - high.astype(F32)).astype(BF16)
    small_pair = jnp.concatenate([high, low], axis=0)
    router_both = jnp.dot(small_pair, mixed_pair, preferred_element_type=F32)
    router_grad = router_both[:9] + router_both[9:]
    thin = jnp.pad(small_pair, ((0, 128 - small_pair.shape[0]), (0, 0))).T
    thin_matrix = jnp.pad(jnp.concatenate([router, router], axis=0), ((0, 128 - small_pair.shape[0]), (0, 0)))

    def add(one, two):
        return (one.astype(F32) + two.astype(F32)).astype(BF16)

    def shard_sum(own, other):
        return reduce_fsdp(own, other, f, 3, add_experts)

    sum_a = shard_sum(dw_own_a, dw_oth_a)
    from_a = swap_x(sum_a)
    normed_two_grad, hidden_grad, branch_grad = rows_call(
        2,
        [after(rows_a[2], sum_a), rows_s[2], rows_b[2]],
        [rows_a[3], rows_s[3], rows_b[3]],
        [thin[:LENGTH], thin[LENGTH:], thin_matrix],
        extras=(hidden_rows, cot, gains[1:2]),
        middle=norm_back_middle,
        out_types=[block_f32, block_f32],
    )
    inverse_two = lax.rsqrt(jnp.mean(hidden_rows * hidden_rows, axis=-1, keepdims=True) + EPSILON)
    gain_two_grad = jnp.sum(normed_two_grad * hidden_rows * inverse_two, axis=0)

    sum_s = shard_sum(after(dw_own_s, branch_grad), dw_oth_s)
    branch_grad = after(branch_grad, sum_s)
    from_s = swap_x(sum_s)
    project_grad, bias_grad, normed_one_grad = attention_call(
        attend_back_kernel,
        "attend_back",
        [
            piece_starts, branch_grad, qkv_weight, qkv_oth, cos_rows, sin_rows, out_weight, out_oth,
            query_rows, key_rows, value_rows, stats,
        ],
        [
            jax.ShapeDtypeStruct((3, LENGTH, local_width), BF16),
            jax.ShapeDtypeStruct((3, local_width), F32),
            all_rows,
        ],
        local_heads,
        shard,
        LENGTH,
        [pltpu.VMEM((LENGTH, local_width), BF16)],
    )
    (input_row_grad,) = rows_call(
        3, [after(normed_one_grad, from_a)], gather=False, middle=plain_middle, out_types=[block_f32]
    )
    out_grad = jnp.einsum("lf,ld->fd", attended, branch_grad, preferred_element_type=F32).astype(BF16)
    sum_b = shard_sum(after(dw_own_b, input_row_grad), dw_oth_b)
    from_b = swap_x(sum_b)
    total_b = add_experts(sum_b, from_a)
    peer_b = swap_core(total_b)
    input_row_grad, project_grad, attended, branch_grad = lax.optimization_barrier(
        (input_row_grad, project_grad, attended, branch_grad, sum_b)
    )[:4]
    qkv_own, qkv_more, qkv_send, out_own, out_more, out_send = dense_call(
        jnp.reshape(c, (1,)).astype(jnp.int32), normed, project_grad, attended, branch_grad, shard
    )

    qkv_peer, out_peer = swap_core(qkv_send), swap_core(out_send)
    total_s = add_experts(after(sum_s, qkv_send, total_b), from_s, flip=True)
    peer_s = swap_core(total_s)

    def fsdp_part(own, more, peer, shard_axis):
        own, more, peer = lax.optimization_barrier((own, more, peer, total_s))[:3]
        more = add(more, lax.slice_in_dim(peer, shard, width, axis=shard_axis))
        own = add(own, lax.slice_in_dim(peer, 0, shard, axis=shard_axis))
        return reduce_fsdp(own, more, f, shard_axis, add), more

    (qkv_part, qkv_both), (out_part, out_both) = (
        fsdp_part(qkv_own, qkv_more, qkv_peer, 1),
        fsdp_part(out_own, out_more, out_peer, 1),
    )

    input_row_grad = after(input_row_grad, qkv_both, out_both)
    scaled_one = input_row_grad * gains[0]
    input_grad = hidden_grad + inverse_one * (
        scaled_one
        - inputs_f
        * inverse_one
        * inverse_one
        * jnp.mean(scaled_one * inputs_f, axis=-1, keepdims=True)
    )
    gain_one_grad = jnp.sum(input_row_grad * inputs_f * inverse_one, axis=0)

    mixes = [lax.optimization_barrier((row[0], row[1], qkv_send))[:2] for row in (rows_a, rows_s, rows_b)]
    mixer_peer = swap_core(sum_call([mix[1] for mix in mixes], 5))
    mixer = sum_call([mix[0] for mix in mixes] + [mixer_peer], 5)
    mixer_local = lax.psum_scatter(mixer, "tensor", scatter_dimension=0, tiled=True)

    per_shard = HEAD_DIM // owners
    bias_parts = jnp.moveaxis(bias_grad.reshape(3, local_heads, owners, per_shard), 2, 0).reshape(owners, -1)
    bias_parts = jnp.pad(jnp.roll(bias_parts, -f, axis=0), ((0, 0), (0, shard - 3 * local_heads * per_shard)))
    small_sums = jnp.concatenate([router_grad, gain_one_grad[None], gain_two_grad[None]], axis=0)
    small_here = sum_small(small_sums, bias_parts.reshape(1, width), f, shard)
    small_sums = small_here + swap_x(small_here)
    bias_out = small_sums[11, : 3 * local_heads * per_shard].reshape(3, local_heads, per_shard)

    shared_up_out, shared_down_out = shared_call(after(total_s, qkv_part, out_part), peer_s, c, x)
    own_first, peer_first = EXPERTS // 2 * c, EXPERTS // 2 * (1 - c)
    gate_up_out = place_call(after(total_b, shared_up_out), own_first + 2 * (1 - x), (0, 2))
    gate_up_out = place_call(peer_b, peer_first + 2 * (1 - x), (0, 2), gate_up_out)
    down_out = place_call(total_b, own_first + 2 * (1 - x), (2, 1))
    down_out = place_call(peer_b, peer_first + 2 * (1 - x), (2, 1), down_out)
    total_a = add_experts(after(sum_a, qkv_part, out_part, gate_up_out, down_out, small_here), from_b)
    peer_a = swap_core(total_a)

    gate_up_out = place_call(total_a, own_first + 2 * x, (0, 2), gate_up_out)
    down_out = place_call(total_a, own_first + 2 * x, (2, 1), down_out)

    def core_join(part, hidden_axis):
        part = add(part, after(swap_x(part), gate_up_out, down_out))
        peer = swap_core(part)
        return jnp.where(
            c == 0,
            jnp.concatenate([part, peer], axis=hidden_axis),
            jnp.concatenate([peer, part], axis=hidden_axis),
        ).astype(F32)

    qkv_out, out_out = core_join(qkv_part, 2), core_join(out_part, 0)
    result = turn_back((hidden_rows + after(mixer_local, qkv_out).astype(F32)).astype(BF16))
    gate_up_out = place_call(peer_a, peer_first + 2 * x, (0, 2), gate_up_out)
    gate_up_out = jnp.transpose(gate_up_out, (0, 3, 1, 2))
    down_out = place_call(peer_a, peer_first + 2 * x, (2, 1), down_out).reshape(EXPERTS, hidden, shard)

    return (
        result,
        turn_back(input_grad),
        small_sums[9:11],
        qkv_out,
        bias_out,
        out_out,
        small_sums[:EXPERTS].T,
        small_sums[EXPERTS],
        gate_up_out,
        down_out,
        shared_up_out,
        shared_down_out,
    )


def solution(mesh):
    in_specs = (
        P(("rep", "fsdp", "tensor"), None),
        P(("rep", "fsdp", "tensor"), None),
        P(("rep", "fsdp"), None),
        P(("rep", "fsdp"), None),
        P(None, "fsdp"),
        P(None, "fsdp", "tensor"),
        P(None, "tensor", "fsdp"),
        P("tensor", "fsdp"),
        P("fsdp", None),
        P("fsdp"),
        P(None, "fsdp", None, "tensor"),
        P(None, "tensor", "fsdp"),
        P("fsdp", None, "tensor"),
        P("tensor", "fsdp"),
    )
    out_specs = (
        P(("rep", "fsdp", "tensor"), None),
        P(("rep", "fsdp", "tensor"), None),
        P(None, "fsdp"),
        P(None, "fsdp", "tensor"),
        P(None, "tensor", "fsdp"),
        P("tensor", "fsdp"),
        P("fsdp", None),
        P("fsdp"),
        P(None, "fsdp", None, "tensor"),
        P(None, "tensor", "fsdp"),
        P("fsdp", None, "tensor"),
        P("tensor", "fsdp"),
    )
    return jax.shard_map(shards, mesh=mesh, in_specs=in_specs, out_specs=out_specs, check_vma=False)
```
